128 devices in a mesh: dp: 32 (over y, x_hi, z), tp: 4 (over x_lo, core).
Axes of the slice: x: 4 (x_hi: 2, x_lo: 2; x = x_hi * 2 + x_lo), y: 4, z: 4, core: 2. Of those that a mesh axis runs over, the one named last changes fastest.
Arguments:
- tokens: bfloat16 [16384, 2048], P(('dp', 'tp')), may hold values from -6 to 6
- norm_attn: float32 [2048], replicated, may hold values from 0.1 to 1.9
- w_query: bfloat16 [2048, 2048], P(None, 'tp'), may hold values from -0.125 to 0.125
- w_key: bfloat16 [2048, 256], P(None, 'tp'), may hold values from -0.125 to 0.125
- w_value: bfloat16 [2048, 256], P(None, 'tp'), may hold values from -0.125 to 0.125
- w_out: bfloat16 [2048, 2048], P('tp'), may hold values from -0.5 to 0.5
- norm_mlp: float32 [2048], replicated, may hold values from 0.1 to 1.9
- w_gate: bfloat16 [2048, 5632], P(None, 'tp'), may hold values from -0.125 to 0.125
- w_up: bfloat16 [2048, 5632], P(None, 'tp'), may hold values from -0.125 to 0.125
- w_down: bfloat16 [5632, 2048], P('tp'), may hold values from -0.078125 to 0.078125
- segment_ids: int32 [16384], P(('dp', 'tp')), may hold values from 0 to 1, as said below
- cotangent: bfloat16 [16384, 2048], P(('dp', 'tp')), may hold values from -6 to 6
Outputs:
- layer_out: float32 [16384, 2048], P(('dp', 'tp'))
- grad_tokens: float32 [16384, 2048], P(('dp', 'tp'))
- grad_norm_attn: float32 [2048], P(('dp', 'tp'))
- grad_query: float32 [2048, 2048], P('dp', 'tp')
- grad_key: float32 [2048, 256], P('dp', 'tp')
- grad_value: float32 [2048, 256], P('dp', 'tp')
- grad_out: float32 [2048, 2048], P('tp', 'dp')
- grad_norm_mlp: float32 [2048], P(('dp', 'tp'))
- grad_gate: float32 [2048, 5632], P('dp', 'tp')
- grad_up: float32 [2048, 5632], P('dp', 'tp')
- grad_down: float32 [5632, 2048], P('tp', 'dp')
The draws below stay inside these ranges and needn't reach their ends.
Inputs may be any that keep to these rules, and one draw needn't show every extreme that they name: `segment_ids`: within each aligned block of 512 rows the ids never fall and both values occur; one of the two runs is longer than 384 rows.
All inputs are finite; a program needn't handle non-finite values.
Results may differ from the reference program's by a relative error of at most 0.028.
Values may be sent and summed in bfloat16 or wider, within the bound.
A program may use at most 192 MiB of HBM per device.

```python
import math
import jax
import jax.numpy as jnp
from jax import lax

D = 2048
HEADS = 32
KV = 4
HD = 64
FF = 5632
TOK_DEV = 128
GROUP = 512
TOKENS = 16384
N_DP = 32


def draw_segment_ids(key, part):
    key = jax.random.fold_in(key, 7)
    cut_key, order_key = jax.random.split(key)
    cut_points = jax.random.randint(cut_key, (N_DP, 1), 1, TOK_DEV)
    orders = jax.random.randint(order_key, (N_DP, 1), 0, 2)
    row_index = jnp.arange(GROUP, dtype=jnp.int32)[None, :]
    long_first = (row_index >= GROUP - cut_points).astype(jnp.int32)
    short_first = (row_index >= cut_points).astype(jnp.int32)
    return jnp.where(orders == 0, long_first, short_first).reshape(TOKENS)


def block_levels(own_key, dims, cuts, least, top_value):
    factor_of, own = 1.0, jax.random.fold_in(own_key, 6)
    for dim, parts in cuts:
        draws = jnp.exp(jax.random.uniform(jax.random.fold_in(own, dim), (parts,), jnp.float32, least / len(cuts), top_value / len(cuts)))
        factor_of = factor_of * jnp.repeat(draws, dims[dim] // parts).reshape([-1 if axis == dim else 1 for axis in range(len(dims))])
    return factor_of


def centred(own_key, extent, spread, reach, cuts=(), kind=jnp.bfloat16):
    level = block_levels(own_key, extent, cuts, -0.22, 0.18) if cuts else 1.0
    values = jax.random.normal(own_key, extent, jnp.float32) * spread * level
    return jnp.minimum(jnp.maximum(values, -reach), reach).astype(kind)


def setup_inputs(seed: int = 0) -> dict:
    streams_of = jax.random.split(jax.random.key(seed), 13)
    tokens = centred(streams_of[0], (TOKENS, D), 1.0, 6.0, ((0, 128),))
    norm_attn = jnp.clip(1.0 + 0.18 * jax.random.normal(streams_of[1], (D,), jnp.float32), 0.1, 1.9)
    w_query = centred(streams_of[2], (D, HEADS * HD), D ** -0.5, 0.125, ((1, 4),))
    w_key = centred(streams_of[3], (D, KV * HD), D ** -0.5, 0.125, ((1, 4),))
    w_value = centred(streams_of[4], (D, KV * HD), D ** -0.5, 0.125, ((1, 4),))
    w_out = centred(streams_of[5], (HEADS * HD, D), (HEADS * HD // 16) ** -0.5, 0.5, ((0, 4),))
    norm_mlp = jnp.clip(1.0 + 0.18 * jax.random.normal(streams_of[6], (D,), jnp.float32), 0.1, 1.9)
    w_gate = centred(streams_of[7], (D, FF), D ** -0.5, 0.125, ((1, 4),))
    w_up = centred(streams_of[8], (D, FF), D ** -0.5, 0.125, ((1, 4),))
    w_down = centred(streams_of[9], (FF, D), FF ** -0.5, 0.078125, ((0, 4),))
    segment_ids = draw_segment_ids(jax.random.fold_in(streams_of[12], 71), 0)
    cotangent = centred(streams_of[11], (TOKENS, D), 1.0, 6.0, ((0, 128),))
    return dict(tokens=tokens, norm_attn=norm_attn, w_query=w_query, w_key=w_key, w_value=w_value, w_out=w_out, norm_mlp=norm_mlp, w_gate=w_gate, w_up=w_up, w_down=w_down, segment_ids=segment_ids, cotangent=cotangent)


@jax.custom_vjp
def low(v):
    return lax.optimization_barrier(v.astype(jnp.bfloat16)).astype(jnp.float32)

@jax.custom_vjp
def low_back(v):
    return v

def low_keep(v):
    return (low(v), None)

def low_pass(kept, grad):
    return (grad,)

def back_keep(v):
    return (v, None)

def back_low(kept, grad):
    return (low(grad),)
low.defvjp(low_keep, low_pass)
low_back.defvjp(back_keep, back_low)
epsilon = 1e-05
masked_score = -1000000000.0
highest = lax.Precision.HIGHEST

def turn_half(values):
    half_point = values.shape[-1] // 2
    return jnp.concatenate([-values[..., half_point:], values[..., :half_point]], axis=-1)

def rotary_tables(segment, head_width):
    length = segment.shape[0]
    row_index = jnp.arange(length, dtype=jnp.int32)
    first_second = (length - jnp.sum(segment)).astype(jnp.int32)
    position = jnp.where(segment == 1, row_index - first_second, row_index).astype(jnp.float32)
    half_width = head_width // 2
    inverse = jnp.exp(jnp.arange(half_width, dtype=jnp.float32) * (-2.0 * math.log(10000.0) / head_width))
    angles = position[:, None] * inverse[None, :]
    angles = jnp.concatenate([angles, angles], axis=1)
    allowed = (segment[:, None] == segment[None, :]) & (row_index[:, None] >= row_index[None, :])
    return (jnp.cos(angles), jnp.sin(angles), allowed)

def layer_group(stream, segment, weights):
    norm_attn, w_query, w_key, w_value, w_out, norm_mlp, w_gate, w_up, w_down = weights
    length = stream.shape[0]
    group_heads = HEADS // KV
    cosine, sine_table, allowed = rotary_tables(segment, HD)
    inv_one = lax.rsqrt(lax.optimization_barrier(jnp.mean(stream * stream, axis=1, keepdims=True)) + epsilon)
    normed_one = low(stream * inv_one * norm_attn)
    queries = low_back(jnp.dot(normed_one, w_query, precision=highest)).reshape(length, KV, group_heads, HD)
    key_rows = low_back(jnp.dot(normed_one, w_key, precision=highest)).reshape(length, KV, HD)
    value_rows = low(low_back(jnp.dot(normed_one, w_value, precision=highest))).reshape(length, KV, HD)
    query_turned = low(queries * cosine[:, None, None, :] + turn_half(queries) * sine_table[:, None, None, :])
    key_turned = low(key_rows * cosine[:, None, :] + turn_half(key_rows) * sine_table[:, None, :])
    scores = low_back(jnp.einsum('qkrd,skd->krqs', query_turned, key_turned, precision=highest)) * HD ** (-0.5)
    scores = jnp.where(allowed, scores, masked_score)
    attn_prob = low(jax.nn.softmax(scores, axis=-1))
    attended = jnp.einsum('krqs,skd->qkrd', attn_prob, value_rows, precision=highest).reshape(length, HEADS * HD)
    attended = low(low_back(attended))
    middle = stream + low_back(jnp.dot(attended, w_out, precision=highest))
    inv_two = lax.rsqrt(lax.optimization_barrier(jnp.mean(middle * middle, axis=1, keepdims=True)) + epsilon)
    normed_two = low(middle * inv_two * norm_mlp)
    gate_rows = low_back(jnp.dot(normed_two, w_gate, precision=highest))
    up_rows = low_back(jnp.dot(normed_two, w_up, precision=highest))
    hidden = low(jax.nn.silu(gate_rows) * up_rows)
    return middle + low_back(jnp.dot(hidden, w_down, precision=highest))

def reference(tokens, norm_attn, w_query, w_key, w_value, w_out, norm_mlp, w_gate, w_up, w_down, segment_ids, cotangent):
    stream = tokens.astype(jnp.float32).reshape(N_DP, GROUP, D)
    segments = segment_ids.reshape(N_DP, GROUP)
    weights = (norm_attn.astype(jnp.float32), w_query.astype(jnp.float32), w_key.astype(jnp.float32), w_value.astype(jnp.float32), w_out.astype(jnp.float32), norm_mlp.astype(jnp.float32), w_gate.astype(jnp.float32), w_up.astype(jnp.float32), w_down.astype(jnp.float32))

    def forward(stream_all, weight_set):

        def one_group(group_pair):
            return layer_group(group_pair[0], group_pair[1], weight_set)
        return lax.map(jax.checkpoint(one_group), (stream_all, segments))
    layer_out, pullback = jax.vjp(forward, stream, weights)
    grad_stream, grad_weights = pullback(cotangent.astype(jnp.float32).reshape(N_DP, GROUP, D))
    return (layer_out.reshape(TOKENS, D), grad_stream.reshape(TOKENS, D), grad_weights[0], grad_weights[1], grad_weights[2], grad_weights[3], grad_weights[4], grad_weights[5], grad_weights[6], grad_weights[7], grad_weights[8])
```

```python
import math

import jax
import jax.numpy as jnp
import numpy as np
from jax import lax
from jax.experimental import pallas as pl
from jax.experimental.pallas import tpu as pltpu
from jax.sharding import PartitionSpec as P

HD = 64
BF = jnp.bfloat16
F32 = jnp.float32
MESH = pl.DeviceIdType.MESH


def place():
    dp = lax.axis_index("dp")
    tp = lax.axis_index("tp")
    return dp // 8, lax.rem(dp // 4, 2), lax.rem(dp, 4), tp


def ring(me, step):
    return lax.rem(me + step + 4, 4)


class Panel:
    def __init__(self, y_first, grad, near, second, far, last, from_x, send, recv, put):
        self.y_first = y_first
        self.grad, self.near, self.second, self.far = grad, near, second, far
        self.last, self.from_x = last, from_x
        self.send, self.recv = send, recv
        self.put = put
        y, xh, z, tp = place()
        self.xh = xh
        one, two = (y, z) if y_first else (z, y)
        steps = lambda me: (me, ring(me, 1), ring(me, 2), ring(me, -1))
        self.at = (None, steps(one), steps(two))
        self.devices = {}
        for step in (1, -1):
            along_y = (ring(y, step) * 8 + xh * 4 + z, tp)
            along_z = (y * 8 + xh * 4 + ring(z, step), tp)
            self.devices[1, step], self.devices[2, step] = (along_y, along_z) if y_first else (along_z, along_y)
        self.other = 1 - xh
        self.across = (y * 8 + self.other * 4 + z, tp)
        self.started = []

    def device(self, stage, step):
        return self.devices[stage, step]

    def part(self, stage, at, half):
        if stage == 1:
            return self.grad.at[at, half] if self.y_first else self.grad.at[:, half, at]
        return self.second.at[at, half]

    def landed(self, stage, k):
        return (self.near if stage == 1 else self.far).at[k]

    def copy(self, stage, k, at, half, step):
        sem = k + (6 if stage == 2 else 0)
        return pltpu.make_async_remote_copy(
            src_ref=self.part(stage, at, half),
            dst_ref=self.landed(stage, k),
            send_sem=self.send.at[sem],
            recv_sem=self.recv.at[sem],
            device_id=self.device(stage, step),
            device_id_type=MESH,
        )

    def go(self, stage, k, at, half, step):
        what = (stage, k, at, half, step)
        self.copy(*what).start()
        self.started.append(what)

    def arrived(self, stage, k):
        self.copy(stage, k, self.at[stage][0], 0, 1).wait_recv()

    def begin(self, stage):
        me, right, over, left = self.at[stage]
        self.go(stage, 0, over, 0, 1)
        self.go(stage, 1, over, 1, -1)
        self.go(stage, 2, right, 1, 1)
        self.go(stage, 3, left, 0, -1)

    def add(self, into, what):
        if len(into.shape) == 3:
            @pl.loop(0, into.shape[0])
            def _(i):
                into[i] = (into[i].astype(F32) + what[i].astype(F32)).astype(BF)
        else:
            into[...] = (into[...].astype(F32) + what[...].astype(F32)).astype(BF)

    def middle(self, stage):
        me, right, over, left = self.at[stage]
        for k, at, half, step in ((0, right, 0, 1), (1, left, 1, -1)):
            self.arrived(stage, k)
            self.add(self.part(stage, at, half), self.landed(stage, k))
            self.go(stage, k + 4, at, half, step)

    def end(self, stage):
        me = self.at[stage][0]
        for half, (a, b) in enumerate(((4, 3), (2, 5))):
            self.arrived(stage, a)
            self.arrived(stage, b)
            own, one, two = self.part(stage, me, half), self.landed(stage, a), self.landed(stage, b)
            if stage == 1:
                @pl.loop(0, 4)
                def _(q):
                    total = own[q].astype(F32) + one[q].astype(F32) + two[q].astype(F32)
                    self.second[q, half] = total.astype(BF)
            else:
                total = own[...].astype(F32) + one[...].astype(F32) + two[...].astype(F32)
                self.last[half] = total.astype(BF)

    def crossing(self):
        return pltpu.make_async_remote_copy(
            src_ref=self.last.at[self.other],
            dst_ref=self.from_x,
            send_sem=self.send.at[12],
            recv_sem=self.recv.at[12],
            device_id=self.across,
            device_id_type=MESH,
        )

    def cross(self):
        self.crossing().start()

    def finish(self):
        self.crossing().wait_recv()
        self.put(self.last[self.xh].astype(F32) + self.from_x[...].astype(F32))

    def sent(self, count):
        for what in self.started[:count]:
            self.copy(*what).wait_send()
        self.started = self.started[count:]

    def drain(self):
        self.sent(len(self.started))
        self.crossing().wait_send()


def dot(a, b):
    return jnp.dot(a, b, preferred_element_type=F32)


def dot_nt(a, b):
    return lax.dot_general(a, b, (((1,), (1,)), ((), ())), preferred_element_type=F32)


def dot_tn(a, b):
    return lax.dot_general(a, b, (((0,), (0,)), ((), ())), preferred_element_type=F32)


class Peers:
    def __init__(self):
        self.dp = lax.axis_index("dp")
        self.me = lax.axis_index("tp")
        self.core = self.me + 1 - 2 * lax.rem(self.me, 2)
        self.next = lax.rem(self.me + 2, 4)
        self.far = lax.rem(self.core + 2, 4)
        self.chip = self.me // 2
        self.to_core = (self.dp, self.core)
        self.to_next = (self.dp, self.next)
        self.to_far = (self.dp, self.far)


class Gather:
    def __init__(self, peers, buf, send, recv, parts):
        self.p, self.buf, self.send, self.recv, self.parts = peers, buf, send, recv, parts
        self.rows = buf.shape[1] // parts
        self.started = []

    def copy(self, kind, owner, i, device):
        at = self.buf.at[owner, pl.ds(i * self.rows, self.rows)]
        sem = kind * self.parts + i
        return pltpu.make_async_remote_copy(
            src_ref=at, dst_ref=at, send_sem=self.send.at[sem], recv_sem=self.recv.at[sem],
            device_id=device, device_id_type=MESH)

    def go(self, *what):
        self.copy(*what).start()
        self.started.append(what)

    def start(self, i):
        self.go(1, self.p.me, i, self.p.to_next)
        self.go(0, self.p.me, i, self.p.to_core)

    def near(self):
        for i in range(self.parts):
            self.copy(0, self.p.core, i, self.p.to_core).wait_recv()

    def forward(self, i):
        self.copy(1, self.p.next, i, self.p.to_next).wait_recv()
        self.go(2, self.p.next, i, self.p.to_core)

    def rest(self, i):
        self.copy(2, self.p.far, i, self.p.to_core).wait_recv()

    def drain(self):
        for what in self.started:
            self.copy(*what).wait_send()
        self.started = []


class Scatter:
    def __init__(self, peers, part, r0, r1, r2, send, recv, parts):
        self.p, self.part, self.r = peers, part, (r0, r1, r2)
        self.send, self.recv, self.parts = send, recv, parts
        self.rows = part.shape[1] // parts
        self.started = []

    def rowsof(self, i):
        return pl.ds(i * self.rows, self.rows)

    def copy(self, kind, owner, i, device):
        sem = kind * self.parts + i
        return pltpu.make_async_remote_copy(
            src_ref=self.part.at[owner, self.rowsof(i)], dst_ref=self.r[kind].at[self.rowsof(i)],
            send_sem=self.send.at[sem], recv_sem=self.recv.at[sem],
            device_id=device, device_id_type=MESH)

    def go(self, *what):
        self.copy(*what).start()
        self.started.append(what)

    def cross(self, i):
        self.go(0, self.p.far, i, self.p.to_core)

    def own(self, i):
        self.go(1, self.p.core, i, self.p.to_core)

    def combine(self, i):
        self.copy(0, self.p.far, i, self.p.to_core).wait_recv()
        at = self.part.at[self.p.next, self.rowsof(i)]
        at[...] = (at[...].astype(F32) + self.r[0][self.rowsof(i)].astype(F32)).astype(BF)
        self.go(2, self.p.next, i, self.p.to_next)

    def total(self, i):
        self.copy(1, self.p.core, i, self.p.to_core).wait_recv()
        self.copy(2, self.p.next, i, self.p.to_next).wait_recv()
        rows = self.rowsof(i)
        return (self.part[self.p.me, rows].astype(F32) + self.r[1][rows].astype(F32)
                + self.r[2][rows].astype(F32))

    def drain(self):
        for what in self.started:
            self.copy(*what).wait_send()
        self.started = []


def rope_tables():
    inverse = np.exp(np.arange(32, dtype=np.float64) * (-2.0 * math.log(10000.0) / 64))
    angles = np.arange(512, dtype=np.float64)[:, None] * np.tile(inverse, 4)[None, :]
    return (np.cos(angles).astype(np.float32), np.sin(angles).astype(np.float32),
            np.tile(inverse, 4)[None, :].astype(np.float32))


def lanes(shape):
    return lax.broadcasted_iota(jnp.int32, shape, len(shape) - 1)


def turned(values):
    low = lax.rem(lanes(values.shape), 64) < 32
    return jnp.where(low, pltpu.roll(values, 96, 1), pltpu.roll(values, 32, 1))


def split_heads(pair):
    left = lanes(pair.shape) < 64
    zero = jnp.zeros_like(pair)
    return jnp.concatenate([jnp.where(left, pair, zero), jnp.where(left, zero, pair)], axis=0)


BLOCKS = ((0, 256, 256), (256, 256, 512))
FF_TILES = ((0, 512), (512, 512), (1024, 384))


def mask_bias(bias, first, start, rows, keys):
    row = lax.broadcasted_iota(jnp.int32, (rows, keys), 0) + start
    key = lax.broadcasted_iota(jnp.int32, (rows, keys), 1)
    allowed = (key <= row) & ((row < first) == (key < first))
    bias[...] = jnp.where(allowed, 0.0, -1e9).astype(F32)


def inverse_rms(rows):
    return lax.rsqrt(jnp.mean(rows * rows, axis=1, keepdims=True) + 1e-5)


def chip_rows(buf, chip):
    return buf[pl.ds(chip * 2, 2)].reshape(256, buf.shape[2])


def forward_kernel(x, gain1, gain2, cos0, sin0, inv, seg, dy_own, *refs):
    hbm_w, refs = refs[:7], refs[7:]
    outs, refs = refs[:15], refs[15:]
    (a1_o, a2_o, dy_o, hid_o, dg_o, du_o, q_o, k_o, v_o, o_o, lse_o, x2_o, cos_o, sin_o, cnt_o) = outs
    (A1, A2, DY, Wq, Wk, Wv, Wo, Wd, Wg, Wu, Q, K, V, O, LSE, PM, R0, R1, R2, DH, HID, DG, DU, X2, COS, SIN,
     CNT, B0, B1, wsem, osem, g1s, g1r, g2s, g2r, g3s, g3r, ss, sr, cs, cr) = refs
    weights = (Wq, Wk, Wv, Wo, Wd, Wg, Wu)
    loads = [pltpu.make_async_copy(h, w, wsem.at[i]) for i, (h, w) in enumerate(zip(hbm_w, weights))]
    p = Peers()
    barrier = pltpu.get_barrier_semaphore()
    for device in (p.to_core, p.to_next, p.to_far):
        pl.semaphore_signal(barrier, inc=1, device_id=device, device_id_type=MESH)
    for load in loads:
        load.start()
    stored = []

    def keep(src, dst):
        copy = pltpu.make_async_copy(src, dst, osem.at[len(stored)])
        copy.start()
        stored.append(copy)

    stream = x[...].astype(F32)
    A1[p.me] = (stream * inverse_rms(stream) * gain1[...]).astype(BF)
    DY[p.me] = dy_own[...]
    CNT[p.me] = jnp.broadcast_to(jnp.sum(seg[...], axis=1, keepdims=True), (8, 128))
    pl.semaphore_wait(barrier, 3)
    first_in = Gather(p, A1, g1s, g1r, 2)
    for i in range(2):
        first_in.start(i)
    counts = [pltpu.make_async_remote_copy(
        src_ref=CNT.at[p.me], dst_ref=CNT.at[p.me], send_sem=cs.at[i], recv_sem=cr.at[i],
        device_id=device, device_id_type=MESH) for i, device in enumerate((p.to_core, p.to_next, p.to_far))]
    for copy in counts:
        copy.start()
    dy_in = Gather(p, DY, g2s, g2r, 2)
    for i in range(2):
        dy_in.start(i)
    for i, owner in enumerate((p.core, p.next, p.far)):
        pltpu.make_async_remote_copy(
            src_ref=CNT.at[owner], dst_ref=CNT.at[owner], send_sem=cs.at[i], recv_sem=cr.at[i],
            device_id=p.to_core, device_id_type=MESH).wait_recv()
    ones = CNT[0] + CNT[1] + CNT[2] + CNT[3]
    first = 512 - ones[0:1, 0:1]
    angle = first.astype(F32) * inv[...]
    cos_n, sin_n = jnp.cos(angle), jnp.sin(angle)
    row = lax.broadcasted_iota(jnp.int32, (512, 128), 0)
    c0, s0 = cos0[...], sin0[...]
    COS[...] = jnp.where(row < first, c0, c0 * cos_n + s0 * sin_n)
    sine = jnp.where(row < first, s0, s0 * cos_n - c0 * sin_n)
    SIN[...] = jnp.where(lax.rem(lanes((512, 128)), 64) < 32, -sine, sine)
    for bias, block in zip((B0, B1), BLOCKS):
        mask_bias(bias, first, *block)
    keep(COS, cos_o)
    keep(SIN, sin_o)
    keep(CNT, cnt_o)

    def project(chip):
        rows = pl.ds(pl.multiple_of(chip * 256, 256), 256)
        a = chip_rows(A1, chip)
        cos, sin = COS[rows], SIN[rows]
        for j in range(2):
            q = dot(a, Wq[:, pl.ds(256 * j, 256)])
            for h in range(2):
                pair = q[:, 128 * h:128 * h + 128]
                Q[rows, pl.ds(256 * j + 128 * h, 128)] = (pair * cos + turned(pair) * sin).astype(BF)
        k = dot(a, Wk[...])
        kk = jnp.concatenate([k, k], axis=1)
        K[rows] = (kk * cos + turned(kk) * sin).astype(BF)
        v = dot(a, Wv[...]).astype(BF)
        V[rows] = jnp.concatenate([v, v], axis=1)

    for load in loads[:3]:
        load.wait()
    first_in.near()
    project(p.chip)
    for i in range(2):
        first_in.forward(i)
    for i in range(2):
        first_in.rest(i)
    project(1 - p.chip)
    keep(A1, a1_o)
    keep(Q, q_o)
    keep(K, k_o)
    keep(V, v_o)

    zero = jnp.zeros((512, 128), BF)
    left = lanes((512, 128)) < 64
    for j in range(4):
        for bias, (start, rows, keys) in zip((B0, B1), BLOCKS):
            qs = split_heads(Q[pl.ds(start, rows), pl.ds(128 * j, 128)])
            s = dot_nt(qs, K[:keys]) * 0.125
            s = (s.reshape(2, rows, keys) + bias[...][None]).reshape(2 * rows, keys)
            top = jnp.max(s, axis=1, keepdims=True)
            e = jnp.exp(s - top)
            total = jnp.sum(e, axis=1, keepdims=True)
            lse = top + jnp.log(total)
            eb = (e / total).astype(BF)
            vl = jnp.where(left[:keys], V[:keys], zero[:keys])
            vr = jnp.where(left[:keys], zero[:keys], V[:keys])
            o = dot(eb[:rows], vl) + dot(eb[rows:], vr)
            O[pl.ds(start, rows), pl.ds(128 * j, 128)] = o.astype(BF)
            lane = lanes((rows, 128))
            old = LSE[pl.ds(start, rows)] if j else jnp.zeros((rows, 128), F32)
            LSE[pl.ds(start, rows)] = jnp.where(lane == 2 * j, lse[:rows], jnp.where(lane == 2 * j + 1, lse[rows:], old))
    keep(O, o_o)
    keep(LSE, lse_o)

    def spread(chip):
        rows = pl.ds(pl.multiple_of(chip * 256, 256), 256)
        for j in range(4):
            cols = pl.ds(512 * j, 512)
            PM[pl.ds(chip * 2, 2), :, cols] = dot(O[rows], Wo[:, cols]).astype(BF).reshape(2, 128, 512)

    loads[3].wait()
    scatter = Scatter(p, PM, R0, R1, R2, ss, sr, 2)
    spread(1 - p.chip)
    for i in range(2):
        scatter.cross(i)
    spread(p.chip)
    for i in range(2):
        scatter.own(i)
    for i in range(2):
        scatter.combine(i)
    loads[4].wait()
    dy_in.near()
    for i in range(2):
        dy_in.forward(i)
    for i in range(2):
        dy_in.rest(i)
    keep(DY, dy_o)
    dy = DY[...].reshape(512, 2048)
    for start, width in FF_TILES:
        DH[:, pl.ds(start, width)] = dot_nt(dy, Wd[pl.ds(start, width)])
    second_in = Gather(p, A2, g3s, g3r, 2)
    for i in range(2):
        rows = scatter.rowsof(i)
        x2 = x[rows].astype(F32) + scatter.total(i)
        X2[rows] = x2
        A2[p.me, rows] = (x2 * inverse_rms(x2) * gain2[...]).astype(BF)
        second_in.start(i)
    keep(X2, x2_o)

    def mlp(chip):
        rows = pl.ds(pl.multiple_of(chip * 256, 256), 256)
        a = chip_rows(A2, chip)
        for start, width in FF_TILES:
            cols = pl.ds(start, width)
            g = dot(a, Wg[:, cols])
            u = dot(a, Wu[:, cols])
            dh = DH[rows, cols]
            sg = jax.nn.sigmoid(g)
            act = g * sg
            HID[rows, cols] = (act * u).astype(BF)
            DU[rows, cols] = (dh * act).astype(BF)
            DG[rows, cols] = (dh * u * (sg + act * (1.0 - sg))).astype(BF)

    loads[5].wait()
    loads[6].wait()
    second_in.near()
    mlp(p.chip)
    for i in range(2):
        second_in.forward(i)
    for i in range(2):
        second_in.rest(i)
    keep(A2, a2_o)
    mlp(1 - p.chip)
    keep(HID, hid_o)
    keep(DG, dg_o)
    keep(DU, du_o)
    for copy in stored:
        copy.wait()
    for copy in counts:
        copy.wait_send()
    for what in (first_in, dy_in, second_in, scatter):
        what.drain()


def forward(tokens, norm_attn, norm_mlp, segment_ids, cotangent, w_query, w_key, w_value, w_out, w_down, w_gate, w_up):
    cos0, sin0, inv = rope_tables()
    rows4 = (4, 128, 2048)
    spec = lambda shape, kind: jax.ShapeDtypeStruct(shape, kind)
    outs = [spec(rows4, BF)] * 3 + [spec((512, 1408), BF)] * 3 + [
        spec((512, 512), BF), spec((512, 128), BF), spec((512, 128), BF), spec((512, 512), BF),
        spec((512, 128), F32), spec((128, 2048), F32), spec((512, 128), F32), spec((512, 128), F32),
        spec((4, 8, 128), jnp.int32)]
    vm = pltpu.VMEM
    dma = pltpu.SemaphoreType.DMA
    scratch = [vm(rows4, BF)] * 3 + [
        vm((2048, 512), BF), vm((2048, 64), BF), vm((2048, 64), BF), vm((512, 2048), BF), vm((1408, 2048), BF),
        vm((2048, 1408), BF), vm((2048, 1408), BF),
        vm((512, 512), BF), vm((512, 128), BF), vm((512, 128), BF), vm((512, 512), BF), vm((512, 128), F32),
        vm(rows4, BF), vm((128, 2048), BF), vm((128, 2048), BF), vm((128, 2048), BF), vm((512, 1408), F32),
        vm((512, 1408), BF), vm((512, 1408), BF), vm((512, 1408), BF), vm((128, 2048), F32),
        vm((512, 128), F32), vm((512, 128), F32), vm((4, 8, 128), jnp.int32), vm((256, 256), F32), vm((256, 512), F32),
        dma((7,)), dma((15,))] + [dma((6,))] * 8 + [dma((3,))] * 2
    return pl.pallas_call(
        forward_kernel,
        name="forward",
        out_shape=outs,
        in_specs=[pl.BlockSpec(memory_space=pltpu.VMEM)] * 8 + [pl.BlockSpec(memory_space=pl.ANY)] * 7,
        out_specs=[pl.BlockSpec(memory_space=pl.ANY)] * 15,
        scratch_shapes=scratch,
        compiler_params=pltpu.CompilerParams(
            collective_id=2, has_side_effects=True, vmem_limit_bytes=62 * 2**20
        ),
    )(tokens, norm_attn.reshape(1, 2048), norm_mlp.reshape(1, 2048), cos0, sin0, inv, segment_ids.reshape(1, 128),
      cotangent, w_query, w_key, w_value, w_out, w_down, w_gate, w_up)


MLP_PANELS = ((768, 640), (640, 768), (768, 640), (512, 640))


def grad_panel(grad, left, right, width, start):
    @pl.loop(0, 4)
    def _(at):
        rows = left[:, pl.ds(pl.multiple_of(at * 512, 512), 512)]
        cols = pl.ds(start, width)
        grad[at] = dot_tn(rows, right[:, cols]).astype(BF).reshape(2, 4, 64, width)


def norm_back(dn, rows, gain):
    r = inverse_rms(rows)
    e = dn * gain
    back = r * e - rows * (r * r * r) * jnp.mean(e * rows, axis=1, keepdims=True)
    return back, (dn * rows * r).astype(BF)


def backward_kernel(gain1, gain2, cnt, *refs):
    (a1_h, a2_h, dy_h, hid_h, dg_h, du_h, q_h, k_h, v_h, o_h, lse_h, x2_h, cos_h, sin_h,
     x_h, dyo_h, wq_h, wk_h, wv_h, wo_h, wd_h, wg_h, wu_h) = refs[:23]
    (lo_o, gt_o, gq_o, gk_o, gv_o, go_o, gg_o, gu_o, gd_o, gains_o) = refs[23:33]
    refs = refs[33:]
    sets, refs = (refs[:4], refs[4:8]), refs[8:]
    slots, refs = [refs[6 * i:6 * i + 6] for i in range(9)], refs[54:]
    (Gg, Ng, X0, X1, DX2F, Ra0, Ra1, Ra2, Rb0, Rb1, Rb2, Rc0, Rc1, Rc2, X2, X, DYO, E1, E2, VB,
     lsem, s2s, s2r, sls, slr, s1s, s1r, g4s, g4r, vs, vr, credit) = refs
    y, xh, z, tp = place()
    p = Peers()
    peers = [
        (ring(y, 1) * 8 + xh * 4 + z, tp), (ring(y, -1) * 8 + xh * 4 + z, tp),
        (y * 8 + xh * 4 + ring(z, 1), tp), (y * 8 + xh * 4 + ring(z, -1), tp),
        (y * 8 + (1 - xh) * 4 + z, tp), p.to_core, p.to_next, p.to_far]
    barrier = pltpu.get_barrier_semaphore()
    for device in peers:
        pl.semaphore_signal(barrier, inc=1, device_id=device, device_id_type=MESH)

    n_loads = [0]

    def load(src, dst):
        copy = pltpu.make_async_copy(src, dst, lsem.at[n_loads[0]])
        n_loads[0] += 1
        copy.start()
        return copy

    def put_down(start, width):
        def put(v):
            gd_o[pl.ds(start, width)] = v.T
        return put

    def put_cols(ref, start, width):
        def put(v):
            ref[:, pl.ds(start, width)] = v
        return put

    def put_q(v):
        gq_o[...] = v

    def put_kvo(v):
        gk_o[...] = v[:, :64]
        gv_o[...] = v[:, 64:128]
        go_o[...] = v[:, 128:].T

    def put_gain(v):
        VB[tp] = v

    puts = (put_down(0, 768), put_down(768, 640), put_cols(gg_o, 0, 640), put_cols(gg_o, 640, 768),
            put_cols(gu_o, 0, 768), put_cols(gu_o, 768, 640), put_q, put_kvo)
    pairs = []
    for j, widths in enumerate(MLP_PANELS):
        Gy, Ny, Gz, Nz = sets[j % 2]
        pair = []
        for i, (G, N, width) in enumerate(((Gy, Ny, widths[0]), (Gz, Nz, widths[1]))):
            if G.shape[4] != width:
                G, N = G.at[:, :, :, :, pl.ds(0, width)], N.at[:, :, :, pl.ds(0, width)]
            pair.append(Panel(i == 0, G, N, *slots[2 * j + i], puts[2 * j + i]))
        pairs.append(pair)
    gain_panel = Panel(True, Gg, Ng, *slots[8], put_gain)
    pairs.append([gain_panel])

    def middle(j, stage):
        for panel in pairs[j]:
            panel.middle(stage)

    def second(j):
        for i, panel in enumerate(pairs[j]):
            panel.end(1)
            if j < 2:
                for step in (1, -1):
                    pl.semaphore_signal(credit.at[2 * j + i], inc=1, device_id=panel.device(1, step), device_id_type=MESH)
            panel.begin(2)

    def cross(j):
        for panel in pairs[j]:
            panel.end(2)
            panel.cross()

    def finish(j):
        for panel in pairs[j]:
            panel.finish()

    def reuse(j):
        for i, panel in enumerate(pairs[j]):
            panel.sent(6)
            pl.semaphore_wait(credit.at[2 * j + i], 2)

    scatter2 = Scatter(p, X0, Ra0, Ra1, Ra2, s2s, s2r, 2)
    scatter_out = Scatter(p, X1, Rb0, Rb1, Rb2, sls, slr, 2)
    scatter1 = Scatter(p, X0, Rc0, Rc1, Rc2, s1s, s1r, 2)
    gather = Gather(p, DX2F, g4s, g4r, 2)

    def early(DY, HID, DG, DU, WG, WU, WD, wsem):
        l_dy, l_hid = load(dy_h, DY), load(hid_h, HID)
        l_a2, l_dg, l_du = load(a2_h, X1), load(dg_h, DG), load(du_h, DU)

        def gate_chunk(i):
            at = pl.ds(256 * i, 256)
            return [pltpu.make_async_copy(wg_h.at[at], WG.at[i % 2], wsem.at[i % 2]),
                    pltpu.make_async_copy(wu_h.at[at], WU.at[i % 2], wsem.at[2 + i % 2])]

        def down_chunk(i):
            return [pltpu.make_async_copy(wd_h.at[:, pl.ds(256 * i, 256)], WD.at[i % 2], wsem.at[4 + i % 2])]

        for i in range(2):
            for copy in gate_chunk(i) + down_chunk(i):
                copy.start()
        l_x2, l_x, l_dyo = load(x2_h, X2), load(x_h, X), load(dyo_h, DYO)
        l_dy.wait()
        l_hid.wait()
        pl.semaphore_wait(barrier, len(peers))
        starts = (0, MLP_PANELS[0][0])
        for panel, width, start in zip(pairs[0], MLP_PANELS[0], starts):
            grad_panel(panel.grad, DY, HID, width, start)
            panel.begin(1)
        l_a2.wait()
        l_dg.wait()
        a2 = X1.reshape(512, 2048)
        for panel, width, start in zip(pairs[1], MLP_PANELS[1], (0, MLP_PANELS[1][0])):
            grad_panel(panel.grad, a2, DG, width, start)
            panel.begin(1)
        l_du.wait()
        for i in range(8):
            for copy in gate_chunk(i):
                copy.wait()
            da = dot_nt(DG[...], WG[i % 2]) + dot_nt(DU[...], WU[i % 2])
            X0[:, :, pl.ds(256 * i, 256)] = da.astype(BF).reshape(4, 128, 256)
            if i < 6:
                for copy in gate_chunk(i + 2):
                    copy.start()
        for i in range(2):
            scatter2.cross(i)
        for i in range(2):
            scatter2.own(i)
        middle(0, 1)
        for i in range(2):
            scatter2.combine(i)
        l_x2.wait()
        l_x.wait()
        l_dyo.wait()
        for i in range(2):
            rows = scatter2.rowsof(i)
            back, E2[rows] = norm_back(scatter2.total(i), X2[rows], gain2[...])
            dx2 = DYO[rows].astype(F32) + back
            lo_o[rows] = X2[rows]
            X2[rows] = dx2
            DX2F[p.me, rows] = dx2.astype(BF)
            gather.start(i)
        middle(1, 1)
        second(0)
        reuse(0)
        for panel, width, start in zip(pairs[2], MLP_PANELS[2], (0, MLP_PANELS[2][0])):
            grad_panel(panel.grad, a2, DU, width, start)
            panel.begin(1)
        for i in range(8):
            for copy in down_chunk(i):
                copy.wait()
            X1[:, :, pl.ds(256 * i, 256)] = dot(HID[...], WD[i % 2]).astype(BF).reshape(4, 128, 256)
            if i < 6:
                for copy in down_chunk(i + 2):
                    copy.start()
        for i in range(2):
            scatter_out.cross(i)
        for i in range(2):
            scatter_out.own(i)

    def late(A1, Wo, Wq, Wk, Wv, Q, O, DO, DQ, K, V, DKV, LSE, COS, SIN, B0, B1, DK, DV):
        l_wo, l_q, l_k, l_v, l_lse, l_cos, l_sin, l_o, l_a1, l_wq, l_wk, l_wv = [load(*w) for w in (
            (wo_h, Wo), (q_h, Q), (k_h, K), (v_h, V), (lse_h, LSE), (cos_h, COS), (sin_h, SIN), (o_h, O),
            (a1_h, A1), (wq_h, Wq), (wk_h, Wk), (wv_h, Wv))]
        ones = cnt[0] + cnt[1] + cnt[2] + cnt[3]
        first = 512 - ones[0:1, 0:1]
        for bias, block in zip((B0, B1), BLOCKS):
            mask_bias(bias, first, *block)
        gather.near()
        for i in range(2):
            gather.forward(i)
        for i in range(2):
            scatter_out.combine(i)
        l_wo.wait()

        def back_out(chip):
            rows = pl.ds(pl.multiple_of(chip * 256, 256), 256)
            DO[rows] = dot_nt(chip_rows(DX2F, chip), Wo[...]).astype(BF)

        back_out(p.chip)
        for i in range(2):
            gather.rest(i)
        back_out(1 - p.chip)
        for copy in (l_q, l_k, l_v, l_lse, l_cos, l_sin, l_o, l_a1):
            copy.wait()
        second(1)
        zero = jnp.zeros((512, 128), BF)
        left = lanes((512, 128)) < 64

        def heads(j):
            cols = pl.ds(128 * j, 128)
            for bias, (start, rows, keys) in zip((B0, B1), BLOCKS):
                at = pl.ds(start, rows)
                qs = split_heads(Q[at, cols])
                dos = split_heads(DO[at, cols])
                s = dot_nt(qs, K[:keys]) * 0.125
                s = (s.reshape(2, rows, keys) + bias[...][None]).reshape(2 * rows, keys)
                lse = jnp.concatenate([LSE[at, 2 * j:2 * j + 1], LSE[at, 2 * j + 1:2 * j + 2]], axis=0)
                prob = jnp.exp(s - lse)
                dp = dot_nt(dos, V[:keys])
                row_dot = jnp.sum(prob * dp, axis=1, keepdims=True)
                ds = (prob * (dp - row_dot) * 0.125).astype(BF)
                dv = dot_tn(prob.astype(BF), dos)
                dk = dot_tn(ds, qs)
                if j == 0 and keys == 512:
                    DV[256:] = dv[256:]
                    DK[256:] = dk[256:]
                    DV[:256] += dv[:256]
                    DK[:256] += dk[:256]
                elif j == 0:
                    DV[:keys] = dv
                    DK[:keys] = dk
                else:
                    DV[:keys] += dv
                    DK[:keys] += dk
                kl = jnp.where(left[:keys], K[:keys], zero[:keys])
                kr = jnp.where(left[:keys], zero[:keys], K[:keys])
                dq = dot(ds[:rows], kl) + dot(ds[rows:], kr)
                DQ[at, cols] = (dq * COS[at] - turned(dq) * SIN[at]).astype(BF)

        heads(0)
        middle(0, 2)
        heads(1)
        middle(2, 1)
        cross(0)
        heads(2)
        middle(1, 2)
        heads(3)
        dk = DK[...] + pltpu.roll(DK[...], 64, 1)
        dv = DV[...] + pltpu.roll(DV[...], 64, 1)
        DKV[...] = jnp.where(left, dk * COS[...] - turned(dk) * SIN[...], dv).astype(BF)
        cross(1)
        reuse(1)
        grad_panel(pairs[3][0].grad, A1, DQ, 512, 0)
        pairs[3][0].begin(1)
        grad_z = pairs[3][1].grad
        grad_panel(grad_z.at[:, :, :, :, pl.ds(0, 128)], A1, DKV, 128, 0)
        grad_panel(grad_z.at[:, :, :, :, pl.ds(128, 512)], DX2F.reshape(512, 2048), O, 512, 0)
        pairs[3][1].begin(1)
        l_wq.wait()
        l_wk.wait()
        l_wv.wait()
        scatter2.drain()
        for i in range(4):
            at = pl.ds(512 * i, 512)
            wkv = jnp.concatenate([Wk[at], Wv[at]], axis=1)
            da = dot_nt(DQ[...], Wq[at]) + dot_nt(DKV[...], wkv)
            X0[:, :, at] = da.astype(BF).reshape(4, 128, 512)
        for i in range(2):
            scatter1.cross(i)
        for i in range(2):
            scatter1.own(i)
        second(2)
        for i in range(2):
            scatter1.combine(i)
        finish(0)
        finish(1)
        for i in range(2):
            rows = scatter_out.rowsof(i)
            lo_o[rows] = lo_o[rows] + scatter_out.total(i)
        middle(3, 1)
        middle(2, 2)
        for i in range(2):
            rows = scatter1.rowsof(i)
            back, E1[rows] = norm_back(scatter1.total(i), X[rows].astype(F32), gain1[...])
            gt_o[rows] = X2[rows] + back

    vm, dma = pltpu.VMEM, pltpu.SemaphoreType.DMA
    pl.run_scoped(early, vm((512, 2048), BF), vm((512, 1408), BF), vm((512, 1408), BF), vm((512, 1408), BF),
                  vm((2, 256, 1408), BF), vm((2, 256, 1408), BF), vm((2, 1408, 256), BF), dma((6,)))
    pl.run_scoped(late, vm((512, 2048), BF), vm((512, 2048), BF), vm((2048, 512), BF), vm((2048, 64), BF),
                  vm((2048, 64), BF), vm((512, 512), BF), vm((512, 512), BF), vm((512, 512), BF), vm((512, 512), BF),
                  vm((512, 128), BF), vm((512, 128), BF), vm((512, 128), BF), vm((512, 128), F32),
                  vm((512, 128), F32), vm((512, 128), F32), vm((256, 256), F32), vm((256, 512), F32),
                  vm((512, 128), F32), vm((512, 128), F32))
    column = lanes((128, 128))
    one, two = (column == 0).astype(BF), (column == 1).astype(BF)

    @pl.loop(0, 4)
    def _(at):
        cols = pl.ds(pl.multiple_of(at * 512, 512), 512)
        Gg[at] = (dot_tn(E1[:, cols], one) + dot_tn(E2[:, cols], two)).astype(BF).reshape(2, 4, 64, 128)

    gain_panel.begin(1)
    cross(2)
    middle(4, 1)
    second(3)
    second(4)
    finish(2)
    middle(3, 2)
    middle(4, 2)
    cross(3)
    cross(4)
    finish(4)
    exchange = [pltpu.make_async_remote_copy(
        src_ref=VB.at[p.me], dst_ref=VB.at[p.me], send_sem=vs.at[i], recv_sem=vr.at[i],
        device_id=device, device_id_type=MESH) for i, device in enumerate((p.to_core, p.to_next, p.to_far))]
    for copy in exchange:
        copy.start()
    finish(3)
    for i, owner in enumerate((p.core, p.next, p.far)):
        pltpu.make_async_remote_copy(
            src_ref=VB.at[owner], dst_ref=VB.at[owner], send_sem=vs.at[i], recv_sem=vr.at[i],
            device_id=p.to_core, device_id_type=MESH).wait_recv()
    rows = pl.ds(pl.multiple_of(16 * tp, 16), 16)
    gains_o[...] = VB[0, rows] + VB[1, rows] + VB[2, rows] + VB[3, rows]
    for copy in exchange:
        copy.wait_send()
    for pair in pairs:
        for panel in pair:
            panel.drain()
    for what in (scatter_out, scatter1, gather):
        what.drain()


def backward(kept, tokens, norm_attn, norm_mlp, cotangent, w_query, w_key, w_value, w_out, w_down, w_gate, w_up):
    (a1, a2, dy, hidden, d_gate, d_up, q, k, v, o, lse, x2, cos, sin, cnt) = kept
    vm, dma = pltpu.VMEM, pltpu.SemaphoreType.DMA
    scratch = []
    for wy, wz in MLP_PANELS[:2]:
        for w in (wy, wz):
            scratch += [vm((4, 2, 4, 64, w), BF), vm((6, 4, 64, w), BF)]
    for w in [w for pair in MLP_PANELS for w in pair] + [128]:
        scratch += [vm((4, 2, 64, w), BF), vm((6, 64, w), BF), vm((2, 64, w), BF), vm((64, w), BF), dma((13,)), dma((13,))]
    scratch += [vm((4, 2, 4, 64, 128), BF), vm((6, 4, 64, 128), BF)]
    scratch += [vm((4, 128, 2048), BF)] * 3 + [vm((128, 2048), BF)] * 9
    scratch += [vm((128, 2048), F32)] + [vm((128, 2048), BF)] * 4 + [vm((4, 64, 128), F32)]
    scratch += [dma((23,))] + [dma((6,))] * 8 + [dma((3,))] * 2 + [pltpu.SemaphoreType.REGULAR((4,))]
    shapes = ((128, 2048), (128, 2048), (64, 512), (64, 64), (64, 64), (512, 64), (64, 1408), (64, 1408), (1408, 64),
              (16, 128))
    return pl.pallas_call(
        backward_kernel,
        name="backward",
        out_shape=[jax.ShapeDtypeStruct(shape, F32) for shape in shapes],
        in_specs=[pl.BlockSpec(memory_space=pltpu.VMEM)] * 3 + [pl.BlockSpec(memory_space=pl.ANY)] * 23,
        out_specs=[pl.BlockSpec(memory_space=pltpu.VMEM)] * 10,
        scratch_shapes=scratch,
        compiler_params=pltpu.CompilerParams(
            collective_id=3, has_side_effects=True, vmem_limit_bytes=63 * 2**20
        ),
    )(norm_attn.reshape(1, 2048), norm_mlp.reshape(1, 2048), cnt,
      a1.reshape(512, 2048), a2, dy.reshape(512, 2048), hidden, d_gate, d_up, q, k, v, o, lse, x2, cos, sin,
      tokens, cotangent, w_query, w_key, w_value, w_out, w_down, w_gate, w_up)


def per_device(
    tokens,
    norm_attn,
    w_query,
    w_key,
    w_value,
    w_out,
    norm_mlp,
    w_gate,
    w_up,
    w_down,
    segment_ids,
    cotangent,
):
    weights = (w_query, w_key, w_value, w_out, w_down, w_gate, w_up)
    kept = forward(tokens, norm_attn, norm_mlp, segment_ids, cotangent, *weights)
    (layer_out, grad_tokens, g_query, g_key, g_value, g_out, g_gate, g_up, g_down, gains) = backward(
        kept, tokens, norm_attn, norm_mlp, cotangent, *weights)
    return (layer_out, grad_tokens, gains[:, 0], g_query, g_key, g_value, g_out, gains[:, 1], g_gate, g_up, g_down)


def solution(mesh):
    placed = (
        P(("dp", "tp"), None),
        P(),
        P(None, "tp"),
        P(None, "tp"),
        P(None, "tp"),
        P("tp", None),
        P(),
        P(None, "tp"),
        P(None, "tp"),
        P("tp", None),
        P(("dp", "tp")),
        P(("dp", "tp"), None),
    )
    return jax.shard_map(
        per_device,
        mesh=mesh,
        in_specs=placed,
        out_specs=(
            P(("dp", "tp"), None),
            P(("dp", "tp"), None),
            P(("dp", "tp")),
            P("dp", "tp"),
            P("dp", "tp"),
            P("dp", "tp"),
            P("tp", "dp"),
            P(("dp", "tp")),
            P("dp", "tp"),
            P("dp", "tp"),
            P("tp", "dp"),
        ),
        check_vma=False,
    )
```

```python
import math

import jax
import jax.numpy as jnp
import numpy as np
from jax import lax
from jax.experimental import pallas as pl
from jax.experimental.pallas import tpu as pltpu
from jax.sharding import PartitionSpec as P

HD = 64
BF = jnp.bfloat16
F32 = jnp.float32
MESH = pl.DeviceIdType.MESH


def place():
    dp = lax.axis_index("dp")
    tp = lax.axis_index("tp")
    return dp // 8, lax.rem(dp // 4, 2), lax.rem(dp, 4), tp


def ring(me, step):
    return lax.rem(me + step + 4, 4)


class Panel:
    def __init__(self, y_first, grad, near, second, far, last, from_x, send, recv, put):
        self.y_first = y_first
        self.grad, self.near, self.second, self.far = grad, near, second, far
        self.last, self.from_x = last, from_x
        self.send, self.recv = send, recv
        self.put = put
        y, xh, z, tp = place()
        self.xh = xh
        one, two = (y, z) if y_first else (z, y)
        steps = lambda me: (me, ring(me, 1), ring(me, 2), ring(me, -1))
        self.at = (None, steps(one), steps(two))
        self.devices = {}
        for step in (1, -1):
            along_y = (ring(y, step) * 8 + xh * 4 + z, tp)
            along_z = (y * 8 + xh * 4 + ring(z, step), tp)
            self.devices[1, step], self.devices[2, step] = (along_y, along_z) if y_first else (along_z, along_y)
        self.other = 1 - xh
        self.across = (y * 8 + self.other * 4 + z, tp)
        self.started = []

    def device(self, stage, step):
        return self.devices[stage, step]

    def part(self, stage, at, half):
        if stage == 1:
            return self.grad.at[at, half] if self.y_first else self.grad.at[:, half, at]
        return self.second.at[at, half]

    def landed(self, stage, k):
        return (self.near if stage == 1 else self.far).at[k]

    def copy(self, stage, k, at, half, step):
        sem = k + (6 if stage == 2 else 0)
        return pltpu.make_async_remote_copy(
            src_ref=self.part(stage, at, half),
            dst_ref=self.landed(stage, k),
            send_sem=self.send.at[sem],
            recv_sem=self.recv.at[sem],
            device_id=self.device(stage, step),
            device_id_type=MESH,
        )

    def go(self, stage, k, at, half, step):
        what = (stage, k, at, half, step)
        self.copy(*what).start()
        self.started.append(what)

    def arrived(self, stage, k):
        self.copy(stage, k, self.at[stage][0], 0, 1).wait_recv()

    def begin(self, stage):
        me, right, over, left = self.at[stage]
        self.go(stage, 0, over, 0, 1)
        self.go(stage, 1, over, 1, -1)
        self.go(stage, 2, right, 1, 1)
        self.go(stage, 3, left, 0, -1)

    def add(self, into, what):
        if len(into.shape) == 3:
            @pl.loop(0, into.shape[0])
            def _(i):
                into[i] = (into[i].astype(F32) + what[i].astype(F32)).astype(BF)
        else:
            into[...] = (into[...].astype(F32) + what[...].astype(F32)).astype(BF)

    def middle(self, stage):
        me, right, over, left = self.at[stage]
        for k, at, half, step in ((0, right, 0, 1), (1, left, 1, -1)):
            self.arrived(stage, k)
            self.add(self.part(stage, at, half), self.landed(stage, k))
            self.go(stage, k + 4, at, half, step)

    def end(self, stage):
        me = self.at[stage][0]
        for half, (a, b) in enumerate(((4, 3), (2, 5))):
            self.arrived(stage, a)
            self.arrived(stage, b)
            own, one, two = self.part(stage, me, half), self.landed(stage, a), self.landed(stage, b)
            if stage == 1:
                @pl.loop(0, 4)
                def _(q):
                    total = own[q].astype(F32) + one[q].astype(F32) + two[q].astype(F32)
                    self.second[q, half] = total.astype(BF)
            else:
                total = own[...].astype(F32) + one[...].astype(F32) + two[...].astype(F32)
                self.last[half] = total.astype(BF)

    def crossing(self):
        return pltpu.make_async_remote_copy(
            src_ref=self.last.at[self.other],
            dst_ref=self.from_x,
            send_sem=self.send.at[12],
            recv_sem=self.recv.at[12],
            device_id=self.across,
            device_id_type=MESH,
        )

    def cross(self):
        self.crossing().start()

    def finish(self):
        self.crossing().wait_recv()
        self.put(self.last[self.xh].astype(F32) + self.from_x[...].astype(F32))

    def sent(self, count):
        for what in self.started[:count]:
            self.copy(*what).wait_send()
        self.started = self.started[count:]

    def drain(self):
        self.sent(len(self.started))
        self.crossing().wait_send()


def dot(a, b):
    return jnp.dot(a, b, preferred_element_type=F32)


def dot_nt(a, b):
    return lax.dot_general(a, b, (((1,), (1,)), ((), ())), preferred_element_type=F32)


def dot_tn(a, b):
    return lax.dot_general(a, b, (((0,), (0,)), ((), ())), preferred_element_type=F32)


class Peers:
    def __init__(self):
        self.dp = lax.axis_index("dp")
        self.me = lax.axis_index("tp")
        self.core = self.me + 1 - 2 * lax.rem(self.me, 2)
        self.next = lax.rem(self.me + 2, 4)
        self.far = lax.rem(self.core + 2, 4)
        self.chip = self.me // 2
        self.to_core = (self.dp, self.core)
        self.to_next = (self.dp, self.next)
        self.to_far = (self.dp, self.far)


class Gather:
    def __init__(self, peers, buf, send, recv, parts):
        self.p, self.buf, self.send, self.recv, self.parts = peers, buf, send, recv, parts
        self.rows = buf.shape[1] // parts
        self.started = []

    def copy(self, kind, owner, i, device):
        at = self.buf.at[owner, pl.ds(i * self.rows, self.rows)]
        sem = kind * self.parts + i
        return pltpu.make_async_remote_copy(
            src_ref=at, dst_ref=at, send_sem=self.send.at[sem], recv_sem=self.recv.at[sem],
            device_id=device, device_id_type=MESH)

    def go(self, *what):
        self.copy(*what).start()
        self.started.append(what)

    def start(self, i):
        self.go(1, self.p.me, i, self.p.to_next)
        self.go(0, self.p.me, i, self.p.to_core)

    def near(self):
        for i in range(self.parts):
            self.copy(0, self.p.core, i, self.p.to_core).wait_recv()

    def forward(self, i):
        self.copy(1, self.p.next, i, self.p.to_next).wait_recv()
        self.go(2, self.p.next, i, self.p.to_core)

    def rest(self, i):
        self.copy(2, self.p.far, i, self.p.to_core).wait_recv()

    def drain(self):
        for what in self.started:
            self.copy(*what).wait_send()
        self.started = []


class Scatter:
    def __init__(self, peers, part, r0, r1, r2, send, recv, parts):
        self.p, self.part, self.r = peers, part, (r0, r1, r2)
        self.send, self.recv, self.parts = send, recv, parts
        self.rows = part.shape[1] // parts
        self.started = []

    def rowsof(self, i):
        return pl.ds(i * self.rows, self.rows)

    def copy(self, kind, owner, i, device):
        sem = kind * self.parts + i
        return pltpu.make_async_remote_copy(
            src_ref=self.part.at[owner, self.rowsof(i)], dst_ref=self.r[kind].at[self.rowsof(i)],
            send_sem=self.send.at[sem], recv_sem=self.recv.at[sem],
            device_id=device, device_id_type=MESH)

    def go(self, *what):
        self.copy(*what).start()
        self.started.append(what)

    def cross(self, i):
        self.go(0, self.p.far, i, self.p.to_core)

    def own(self, i):
        self.go(1, self.p.core, i, self.p.to_core)

    def combine(self, i):
        self.copy(0, self.p.far, i, self.p.to_core).wait_recv()
        at = self.part.at[self.p.next, self.rowsof(i)]
        at[...] = (at[...].astype(F32) + self.r[0][self.rowsof(i)].astype(F32)).astype(BF)
        self.go(2, self.p.next, i, self.p.to_next)

    def total(self, i):
        self.copy(1, self.p.core, i, self.p.to_core).wait_recv()
        self.copy(2, self.p.next, i, self.p.to_next).wait_recv()
        rows = self.rowsof(i)
        return (self.part[self.p.me, rows].astype(F32) + self.r[1][rows].astype(F32)
                + self.r[2][rows].astype(F32))

    def drain(self):
        for what in self.started:
            self.copy(*what).wait_send()
        self.started = []


def rope_tables():
    inverse = np.exp(np.arange(32, dtype=np.float64) * (-2.0 * math.log(10000.0) / 64))
    angles = np.arange(512, dtype=np.float64)[:, None] * np.tile(inverse, 4)[None, :]
    return (np.cos(angles).astype(np.float32), np.sin(angles).astype(np.float32),
            np.tile(inverse, 4)[None, :].astype(np.float32))


def lanes(shape):
    return lax.broadcasted_iota(jnp.int32, shape, len(shape) - 1)


def turned(values):
    low = lax.rem(lanes(values.shape), 64) < 32
    return jnp.where(low, pltpu.roll(values, 96, 1), pltpu.roll(values, 32, 1))


def split_heads(pair):
    left = lanes(pair.shape) < 64
    zero = jnp.zeros_like(pair)
    return jnp.concatenate([jnp.where(left, pair, zero), jnp.where(left, zero, pair)], axis=0)


BLOCKS = ((0, 256, 256), (256, 256, 512))
FF_TILES = ((0, 512), (512, 512), (1024, 384))


def mask_bias(bias, first, start, rows, keys):
    row = lax.broadcasted_iota(jnp.int32, (rows, keys), 0) + start
    key = lax.broadcasted_iota(jnp.int32, (rows, keys), 1)
    allowed = (key <= row) & ((row < first) == (key < first))
    bias[...] = jnp.where(allowed, 0.0, -1e9).astype(F32)


def inverse_rms(rows):
    return lax.rsqrt(jnp.mean(rows * rows, axis=1, keepdims=True) + 1e-5)


def chip_rows(buf, chip):
    return buf[pl.ds(chip * 2, 2)].reshape(256, buf.shape[2])


def forward_kernel(x, gain1, gain2, cos0, sin0, inv, seg, dy_own, *refs):
    hbm_w, refs = refs[:7], refs[7:]
    outs, refs = refs[:15], refs[15:]
    (a1_o, a2_o, dy_o, hid_o, dg_o, du_o, q_o, k_o, v_o, o_o, lse_o, x2_o, cos_o, sin_o, cnt_o) = outs
    (A1, A2, DY, Wq, Wkv, Wo, Wd, Wg, Wu, Q, K, V, O, LSE, PM, R0, R1, R2, DH, HID, DG, DU, X2, COS, SIN,
     CNT, B0, B1, wsem, osem, g1s, g1r, g2s, g2r, g3s, g3r, ss, sr, cs, cr) = refs
    weights = (Wq, Wkv.at[pl.ds(0, 64)], Wkv.at[pl.ds(64, 64)], Wo, Wd, Wg, Wu)
    loads = [pltpu.make_async_copy(h, w, wsem.at[i]) for i, (h, w) in enumerate(zip(hbm_w, weights))]
    p = Peers()
    barrier = pltpu.get_barrier_semaphore()
    for device in (p.to_core, p.to_next, p.to_far):
        pl.semaphore_signal(barrier, inc=1, device_id=device, device_id_type=MESH)
    for load in loads:
        load.start()
    stored = []

    def keep(src, dst):
        copy = pltpu.make_async_copy(src, dst, osem.at[len(stored)])
        copy.start()
        stored.append(copy)

    stream = x[...].astype(F32)
    A1[p.me] = (stream * inverse_rms(stream) * gain1[...]).astype(BF)
    DY[p.me] = dy_own[...]
    CNT[p.me] = jnp.broadcast_to(jnp.sum(seg[...], axis=1, keepdims=True), (8, 128))
    pl.semaphore_wait(barrier, 3)
    first_in = Gather(p, A1, g1s, g1r, 2)
    for i in range(2):
        first_in.start(i)
    counts = [pltpu.make_async_remote_copy(
        src_ref=CNT.at[p.me], dst_ref=CNT.at[p.me], send_sem=cs.at[i], recv_sem=cr.at[i],
        device_id=device, device_id_type=MESH) for i, device in enumerate((p.to_core, p.to_next, p.to_far))]
    for copy in counts:
        copy.start()
    dy_in = Gather(p, DY, g2s, g2r, 2)
    for i in range(2):
        dy_in.start(i)
    for i, owner in enumerate((p.core, p.next, p.far)):
        pltpu.make_async_remote_copy(
            src_ref=CNT.at[owner], dst_ref=CNT.at[owner], send_sem=cs.at[i], recv_sem=cr.at[i],
            device_id=p.to_core, device_id_type=MESH).wait_recv()
    ones = CNT[0] + CNT[1] + CNT[2] + CNT[3]
    first = 512 - ones[0:1, 0:1]
    angle = first.astype(F32) * inv[...]
    cos_n, sin_n = jnp.cos(angle), jnp.sin(angle)
    row = lax.broadcasted_iota(jnp.int32, (512, 128), 0)
    c0, s0 = cos0[...], sin0[...]
    COS[...] = jnp.where(row < first, c0, c0 * cos_n + s0 * sin_n)
    sine = jnp.where(row < first, s0, s0 * cos_n - c0 * sin_n)
    SIN[...] = jnp.where(lax.rem(lanes((512, 128)), 64) < 32, -sine, sine)
    for bias, block in zip((B0, B1), BLOCKS):
        mask_bias(bias, first, *block)
    keep(COS, cos_o)
    keep(SIN, sin_o)
    keep(CNT, cnt_o)

    def project(chip):
        rows = pl.ds(pl.multiple_of(chip * 256, 256), 256)
        a = chip_rows(A1, chip)
        cos, sin = COS[rows], SIN[rows]
        for j in range(2):
            q = dot(a, Wq[:, pl.ds(256 * j, 256)])
            for h in range(2):
                pair = q[:, 128 * h:128 * h + 128]
                Q[rows, pl.ds(256 * j + 128 * h, 128)] = (pair * cos + turned(pair) * sin).astype(BF)
        kv = dot_nt(a, Wkv[...])
        vk = pltpu.roll(kv, 64, 1)
        k_lane = lanes(kv.shape) < 64
        kk = jnp.where(k_lane, kv, vk)
        K[rows] = (kk * cos + turned(kk) * sin).astype(BF)
        V[rows] = jnp.where(k_lane, vk, kv).astype(BF)

    for load in loads[:3]:
        load.wait()
    first_in.near()
    project(p.chip)
    for i in range(2):
        first_in.forward(i)
    for i in range(2):
        first_in.rest(i)
    project(1 - p.chip)
    keep(A1, a1_o)
    keep(Q, q_o)
    keep(K, k_o)
    keep(V, v_o)

    zero = jnp.zeros((512, 128), BF)
    left = lanes((512, 128)) < 64
    for j in range(4):
        for bias, (start, rows, keys) in zip((B0, B1), BLOCKS):
            qs = split_heads(Q[pl.ds(start, rows), pl.ds(128 * j, 128)])
            s = dot_nt(qs, K[:keys]) * 0.125
            s = (s.reshape(2, rows, keys) + bias[...][None]).reshape(2 * rows, keys)
            top = jnp.max(s, axis=1, keepdims=True)
            e = jnp.exp(s - top)
            total = jnp.sum(e, axis=1, keepdims=True)
            lse = top + jnp.log(total)
            eb = (e / total).astype(BF)
            vl = jnp.where(left[:keys], V[:keys], zero[:keys])
            vr = jnp.where(left[:keys], zero[:keys], V[:keys])
            o = dot(eb[:rows], vl) + dot(eb[rows:], vr)
            O[pl.ds(start, rows), pl.ds(128 * j, 128)] = o.astype(BF)
            lane = lanes((rows, 128))
            old = LSE[pl.ds(start, rows)] if j else jnp.zeros((rows, 128), F32)
            LSE[pl.ds(start, rows)] = jnp.where(lane == 2 * j, lse[:rows], jnp.where(lane == 2 * j + 1, lse[rows:], old))
    keep(O, o_o)
    keep(LSE, lse_o)

    def spread(chip):
        rows = pl.ds(pl.multiple_of(chip * 256, 256), 256)
        for j in range(4):
            cols = pl.ds(512 * j, 512)
            PM[pl.ds(chip * 2, 2), :, cols] = dot(O[rows], Wo[:, cols]).astype(BF).reshape(2, 128, 512)

    loads[3].wait()
    scatter = Scatter(p, PM, R0, R1, R2, ss, sr, 2)
    spread(1 - p.chip)
    for i in range(2):
        scatter.cross(i)
    spread(p.chip)
    for i in range(2):
        scatter.own(i)
    for i in range(2):
        scatter.combine(i)
    loads[4].wait()
    dy_in.near()
    for i in range(2):
        dy_in.forward(i)
    for i in range(2):
        dy_in.rest(i)
    keep(DY, dy_o)
    dy = DY[...].reshape(512, 2048)
    for start, width in FF_TILES:
        DH[:, pl.ds(start, width)] = dot_nt(dy, Wd[pl.ds(start, width)])
    second_in = Gather(p, A2, g3s, g3r, 2)
    for i in range(2):
        rows = scatter.rowsof(i)
        x2 = x[rows].astype(F32) + scatter.total(i)
        X2[rows] = x2
        A2[p.me, rows] = (x2 * inverse_rms(x2) * gain2[...]).astype(BF)
        second_in.start(i)
    keep(X2, x2_o)

    def mlp(chip):
        rows = pl.ds(pl.multiple_of(chip * 256, 256), 256)
        a = chip_rows(A2, chip)
        for start, width in FF_TILES:
            cols = pl.ds(start, width)
            g = dot(a, Wg[:, cols])
            u = dot(a, Wu[:, cols])
            dh = DH[rows, cols]
            sg = jax.nn.sigmoid(g)
            act = g * sg
            HID[rows, cols] = (act * u).astype(BF)
            DU[rows, cols] = (dh * act).astype(BF)
            DG[rows, cols] = (dh * u * (sg + act * (1.0 - sg))).astype(BF)

    loads[5].wait()
    loads[6].wait()
    second_in.near()
    mlp(p.chip)
    for i in range(2):
        second_in.forward(i)
    for i in range(2):
        second_in.rest(i)
    keep(A2, a2_o)
    mlp(1 - p.chip)
    keep(HID, hid_o)
    keep(DG, dg_o)
    keep(DU, du_o)
    for copy in stored:
        copy.wait()
    for copy in counts:
        copy.wait_send()
    for what in (first_in, dy_in, second_in, scatter):
        what.drain()


def forward(tokens, norm_attn, norm_mlp, segment_ids, cotangent, w_query, w_key, w_value, w_out, w_down, w_gate, w_up):
    cos0, sin0, inv = rope_tables()
    rows4 = (4, 128, 2048)
    spec = lambda shape, kind: jax.ShapeDtypeStruct(shape, kind)
    outs = [spec(rows4, BF)] * 3 + [spec((512, 1408), BF)] * 3 + [
        spec((512, 512), BF), spec((512, 128), BF), spec((512, 128), BF), spec((512, 512), BF),
        spec((512, 128), F32), spec((128, 2048), F32), spec((512, 128), F32), spec((512, 128), F32),
        spec((4, 8, 128), jnp.int32)]
    vm = pltpu.VMEM
    dma = pltpu.SemaphoreType.DMA
    scratch = [vm(rows4, BF)] * 3 + [
        vm((2048, 512), BF), vm((128, 2048), BF), vm((512, 2048), BF), vm((1408, 2048), BF),
        vm((2048, 1408), BF), vm((2048, 1408), BF),
        vm((512, 512), BF), vm((512, 128), BF), vm((512, 128), BF), vm((512, 512), BF), vm((512, 128), F32),
        vm(rows4, BF), vm((128, 2048), BF), vm((128, 2048), BF), vm((128, 2048), BF), vm((512, 1408), F32),
        vm((512, 1408), BF), vm((512, 1408), BF), vm((512, 1408), BF), vm((128, 2048), F32),
        vm((512, 128), F32), vm((512, 128), F32), vm((4, 8, 128), jnp.int32), vm((256, 256), F32), vm((256, 512), F32),
        dma((7,)), dma((15,))] + [dma((6,))] * 8 + [dma((3,))] * 2
    return pl.pallas_call(
        forward_kernel,
        name="forward",
        out_shape=outs,
        in_specs=[pl.BlockSpec(memory_space=pltpu.VMEM)] * 8 + [pl.BlockSpec(memory_space=pl.ANY)] * 7,
        out_specs=[pl.BlockSpec(memory_space=pl.ANY)] * 15,
        scratch_shapes=scratch,
        compiler_params=pltpu.CompilerParams(
            collective_id=2, has_side_effects=True, vmem_limit_bytes=62 * 2**20
        ),
    )(tokens, norm_attn.reshape(1, 2048), norm_mlp.reshape(1, 2048), cos0, sin0, inv, segment_ids.reshape(1, 128),
      cotangent, w_query, w_key.T, w_value.T, w_out, w_down, w_gate, w_up)


MLP_PANELS = ((768, 640), (640, 768), (768, 640), (512, 640))


def grad_panel(grad, left, right, width, start):
    @pl.loop(0, 4)
    def _(at):
        rows = left[:, pl.ds(pl.multiple_of(at * 512, 512), 512)]
        cols = pl.ds(start, width)
        grad[at] = dot_tn(rows, right[:, cols]).astype(BF).reshape(2, 4, 64, width)


def grad_begin(panel, left, right, width, start):
    me, after, over, before = panel.at[1]
    for at, sends in ((over, ((0, over, 0, 1), (1, over, 1, -1))), (after, ((2, after, 1, 1),)),
                      (before, ((3, before, 0, -1),)), (me, ())):
        rows = left[:, pl.ds(pl.multiple_of(at * 512, 512), 512)]
        cols = pl.ds(start, width)
        panel.grad[at] = dot_tn(rows, right[:, cols]).astype(BF).reshape(2, 4, 64, width)
        for what in sends:
            panel.go(1, *what)


def norm_back(dn, rows, gain):
    r = inverse_rms(rows)
    e = dn * gain
    back = r * e - rows * (r * r * r) * jnp.mean(e * rows, axis=1, keepdims=True)
    return back, jnp.sum(dn * rows * r, axis=0, keepdims=True)


def backward_kernel(gain1, gain2, cnt, *refs):
    (a1_h, a2_h, dy_h, hid_h, dg_h, du_h, q_h, k_h, v_h, o_h, lse_h, x2_h, cos_h, sin_h,
     x_h, dyo_h, wq_h, wk_h, wv_h, wo_h, wd_h, wg_h, wu_h) = refs[:23]
    (lo_o, gt_o, gq_o, gk_o, gv_o, go_o, gg_o, gu_o, gd_o, gains_o) = refs[23:33]
    refs = refs[33:]
    sets, refs = (refs[:4], refs[4:8]), refs[8:]
    slots, refs = [refs[6 * i:6 * i + 6] for i in range(8)], refs[48:]
    (X0, X1, X3, DX2F, Ra0, Ra1, Ra2, Rb0, Rb1, Rb2, Rc0, Rc1, Rc2, X2, X, DYO, GA,
     lsem, s2s, s2r, sls, slr, s1s, s1r, g4s, g4r, gs, gr, credit) = refs
    y, xh, z, tp = place()
    p = Peers()
    peers = [
        (ring(y, 1) * 8 + xh * 4 + z, tp), (ring(y, -1) * 8 + xh * 4 + z, tp),
        (y * 8 + xh * 4 + ring(z, 1), tp), (y * 8 + xh * 4 + ring(z, -1), tp),
        (ring(y, 2) * 8 + xh * 4 + z, tp), (y * 8 + xh * 4 + ring(z, 2), tp),
        (y * 8 + (1 - xh) * 4 + z, tp), p.to_core, p.to_next, p.to_far]
    barrier = pltpu.get_barrier_semaphore()
    for device in peers:
        pl.semaphore_signal(barrier, inc=1, device_id=device, device_id_type=MESH)

    n_loads = [0]

    def load(src, dst):
        copy = pltpu.make_async_copy(src, dst, lsem.at[n_loads[0]])
        n_loads[0] += 1
        copy.start()
        return copy

    def put_cols(ref, start, width):
        def put(v):
            ref[:, pl.ds(start, width)] = v
        return put

    def put_q(v):
        gq_o[...] = v

    def put_kvo(v):
        gk_o[...] = v[:, :64]
        gv_o[...] = v[:, 64:128]
        go_o[...] = v[:, 128:]

    puts = (put_cols(gd_o, 0, 768), put_cols(gd_o, 768, 640), put_cols(gg_o, 0, 640), put_cols(gg_o, 640, 768),
            put_cols(gu_o, 0, 768), put_cols(gu_o, 768, 640), put_q, put_kvo)
    pairs = []
    for j, widths in enumerate(MLP_PANELS):
        Gy, Ny, Gz, Nz = sets[j % 2]
        pair = []
        for i, (G, N, width) in enumerate(((Gy, Ny, widths[0]), (Gz, Nz, widths[1]))):
            if G.shape[4] != width:
                G, N = G.at[:, :, :, :, pl.ds(0, width)], N.at[:, :, :, pl.ds(0, width)]
            pair.append(Panel(i == 0, G, N, *slots[2 * j + i], puts[2 * j + i]))
        pairs.append(pair)

    stages = ((peers[0], peers[1], peers[4]), (peers[2], peers[3], peers[5]), (peers[6],), (p.to_core, p.to_next, p.to_far))

    def gain_copy(stage, i):
        sem = 3 * stage + i
        return pltpu.make_async_remote_copy(
            src_ref=GA.at[stage, 0], dst_ref=GA.at[stage, i + 1], send_sem=gs.at[sem], recv_sem=gr.at[sem],
            device_id=stages[stage][i], device_id_type=MESH)

    def gain_send(stage):
        for i in range(len(stages[stage])):
            gain_copy(stage, i).start()

    def gain_sum(stage):
        total = GA[stage, 0]
        for i in range(len(stages[stage])):
            gain_copy(stage, i).wait_recv()
            total = total + GA[stage, i + 1]
        return total

    def gain_next(stage):
        GA[stage + 1, 0] = gain_sum(stage)
        gain_send(stage + 1)

    def middle(j, stage):
        for panel in pairs[j]:
            panel.middle(stage)

    def second(j):
        for i, panel in enumerate(pairs[j]):
            panel.end(1)
            if j < 2:
                for step in (1, -1):
                    pl.semaphore_signal(credit.at[2 * j + i], inc=1, device_id=panel.device(1, step), device_id_type=MESH)
            panel.begin(2)

    def cross(j):
        for panel in pairs[j]:
            panel.end(2)
            panel.cross()

    def finish(j):
        for panel in pairs[j]:
            panel.finish()

    def reuse(j):
        for i, panel in enumerate(pairs[j]):
            panel.sent(6)
            pl.semaphore_wait(credit.at[2 * j + i], 2)

    scatter2 = Scatter(p, X0, Ra0, Ra1, Ra2, s2s, s2r, 2)
    scatter_out = Scatter(p, X3, Rb0, Rb1, Rb2, sls, slr, 2)
    scatter1 = Scatter(p, X0, Rc0, Rc1, Rc2, s1s, s1r, 2)
    gather = Gather(p, DX2F, g4s, g4r, 2)

    def early(DY, HID, DG, DU, WG, WU, WD, wsem):
        l_dy, l_hid = load(dy_h, DY), load(hid_h, HID)
        l_a2, l_dg, l_du = load(a2_h, X1), load(dg_h, DG), load(du_h, DU)

        def gate_chunk(i):
            at = pl.ds(256 * i, 256)
            return [pltpu.make_async_copy(wg_h.at[at], WG.at[i % 2], wsem.at[i % 2]),
                    pltpu.make_async_copy(wu_h.at[at], WU.at[i % 2], wsem.at[2 + i % 2])]

        def down_chunk(i):
            return [pltpu.make_async_copy(wd_h.at[:, pl.ds(256 * i, 256)], WD.at[i % 2], wsem.at[4 + i % 2])]

        for i in range(2):
            for copy in gate_chunk(i) + down_chunk(i):
                copy.start()
        l_x2, l_x, l_dyo = load(x2_h, X2), load(x_h, X), load(dyo_h, DYO)
        l_dy.wait()
        l_hid.wait()
        GA[0, 0] = jnp.zeros((8, 2048), F32)
        pl.semaphore_wait(barrier, len(peers))
        grad_begin(pairs[0][0], DY, HID, 768, 0)
        grad_panel(pairs[0][1].grad, DY, HID, 640, 768)
        pairs[0][1].begin(1)
        l_dg.wait()
        l_du.wait()
        for i in range(8):
            for copy in gate_chunk(i):
                copy.wait()
            da = dot_nt(DG[...], WG[i % 2]) + dot_nt(DU[...], WU[i % 2])
            X0[:, :, pl.ds(256 * i, 256)] = da.astype(BF).reshape(4, 128, 256)
            if i < 6:
                for copy in gate_chunk(i + 2):
                    copy.start()
        for i in range(2):
            scatter2.cross(i)
        for i in range(2):
            scatter2.own(i)
        middle(0, 1)
        for i in range(2):
            scatter2.combine(i)
        l_a2.wait()
        a2 = X1.reshape(512, 2048)
        grad_begin(pairs[1][0], a2, DG, 640, 0)
        grad_panel(pairs[1][1].grad, a2, DG, 768, 640)
        pairs[1][1].begin(1)
        for i in range(8):
            for copy in down_chunk(i):
                copy.wait()
            X3[:, :, pl.ds(256 * i, 256)] = dot(HID[...], WD[i % 2]).astype(BF).reshape(4, 128, 256)
            if i < 6:
                for copy in down_chunk(i + 2):
                    copy.start()
        for i in range(2):
            scatter_out.cross(i)
        for i in range(2):
            scatter_out.own(i)
        second(0)
        l_x2.wait()
        l_x.wait()
        l_dyo.wait()
        for i in range(2):
            rows = scatter2.rowsof(i)
            back, gain = norm_back(scatter2.total(i), X2[rows], gain2[...])
            GA[0, 0, 1:2] += gain
            dx2 = DYO[rows].astype(F32) + back
            lo_o[rows] = X2[rows]
            X2[rows] = dx2
            DX2F[p.me, rows] = dx2.astype(BF)
            gather.start(i)
        for i in range(2):
            scatter_out.combine(i)
        reuse(0)
        grad_panel(pairs[2][0].grad, a2, DU, 768, 0)
        grad_panel(pairs[2][1].grad, a2, DU, 640, 768)
        middle(1, 1)
        for panel in pairs[2]:
            panel.begin(1)
        middle(0, 2)

    def late(A1, Wo, Wq, Wkv, Q, O, DO, DQ, K, V, DKV, LSE, COS, SIN, B0, B1, DK, DV):
        l_wo, l_q, l_k, l_v, l_lse, l_cos, l_sin, l_o, l_a1, l_wq, l_wk, l_wv = [load(*w) for w in (
            (wo_h, Wo), (q_h, Q), (k_h, K), (v_h, V), (lse_h, LSE), (cos_h, COS), (sin_h, SIN), (o_h, O),
            (a1_h, A1), (wq_h, Wq), (wk_h, Wkv.at[pl.ds(0, 64)]), (wv_h, Wkv.at[pl.ds(64, 64)]))]
        ones = cnt[0] + cnt[1] + cnt[2] + cnt[3]
        first = 512 - ones[0:1, 0:1]
        for bias, block in zip((B0, B1), BLOCKS):
            mask_bias(bias, first, *block)
        gather.near()
        for i in range(2):
            gather.forward(i)
        l_wo.wait()

        def back_out(chip):
            rows = pl.ds(pl.multiple_of(chip * 256, 256), 256)
            DO[rows] = dot_nt(chip_rows(DX2F, chip), Wo[...]).astype(BF)

        back_out(p.chip)
        for i in range(2):
            gather.rest(i)
        back_out(1 - p.chip)
        for copy in (l_q, l_k, l_v, l_lse, l_cos, l_sin, l_o, l_a1):
            copy.wait()
        zero = jnp.zeros((512, 128), BF)
        left = lanes((512, 128)) < 64

        def heads(j):
            cols = pl.ds(128 * j, 128)
            for bias, (start, rows, keys) in zip((B0, B1), BLOCKS):
                at = pl.ds(start, rows)
                qs = split_heads(Q[at, cols])
                dos = split_heads(DO[at, cols])
                s = dot_nt(qs, K[:keys]) * 0.125
                s = (s.reshape(2, rows, keys) + bias[...][None]).reshape(2 * rows, keys)
                lse = jnp.concatenate([LSE[at, 2 * j:2 * j + 1], LSE[at, 2 * j + 1:2 * j + 2]], axis=0)
                prob = jnp.exp(s - lse)
                dp = dot_nt(dos, V[:keys])
                row_dot = jnp.sum(prob * dp, axis=1, keepdims=True)
                ds = (prob * (dp - row_dot) * 0.125).astype(BF)
                dv = dot_tn(prob.astype(BF), dos)
                dk = dot_tn(ds, qs)
                if j == 0 and keys == 512:
                    DV[256:] = dv[256:]
                    DK[256:] = dk[256:]
                    DV[:256] += dv[:256]
                    DK[:256] += dk[:256]
                elif j == 0:
                    DV[:keys] = dv
                    DK[:keys] = dk
                else:
                    DV[:keys] += dv
                    DK[:keys] += dk
                kl = jnp.where(left[:keys], K[:keys], zero[:keys])
                kr = jnp.where(left[:keys], zero[:keys], K[:keys])
                dq = dot(ds[:rows], kl) + dot(ds[rows:], kr)
                DQ[at, cols] = (dq * COS[at] - turned(dq) * SIN[at]).astype(BF)

        heads(0)
        heads(1)
        cross(0)
        heads(2)
        heads(3)
        dk = DK[...] + pltpu.roll(DK[...], 64, 1)
        dv = DV[...] + pltpu.roll(DV[...], 64, 1)
        DKV[...] = jnp.where(left, dk * COS[...] - turned(dk) * SIN[...], dv).astype(BF)
        l_wq.wait()
        l_wk.wait()
        l_wv.wait()
        scatter2.drain()
        for i in range(4):
            at = pl.ds(512 * i, 512)
            da = dot_nt(DQ[...], Wq[at]) + dot(DKV[...], Wkv[:, at])
            X0[:, :, at] = da.astype(BF).reshape(4, 128, 512)
        for i in range(2):
            scatter1.cross(i)
        for i in range(2):
            scatter1.own(i)
        for i in range(2):
            scatter1.combine(i)
        second(1)
        reuse(1)
        grad_panel(pairs[3][0].grad, A1, DQ, 512, 0)
        grad_z = pairs[3][1].grad
        grad_panel(grad_z.at[:, :, :, :, pl.ds(0, 128)], A1, DKV, 128, 0)
        grad_panel(grad_z.at[:, :, :, :, pl.ds(128, 512)], DX2F.reshape(512, 2048), O, 512, 0)
        middle(2, 1)
        for panel in pairs[3]:
            panel.begin(1)
        middle(1, 2)
        for i in range(2):
            rows = scatter_out.rowsof(i)
            lo_o[rows] = lo_o[rows] + scatter_out.total(i)
        for i in range(2):
            rows = scatter1.rowsof(i)
            back, gain = norm_back(scatter1.total(i), X[rows].astype(F32), gain1[...])
            GA[0, 0, 0:1] += gain
            gt_o[rows] = X2[rows] + back
        gain_send(0)

    vm, dma = pltpu.VMEM, pltpu.SemaphoreType.DMA
    pl.run_scoped(early, vm((512, 2048), BF), vm((512, 1408), BF), vm((512, 1408), BF), vm((512, 1408), BF),
                  vm((2, 256, 1408), BF), vm((2, 256, 1408), BF), vm((2, 1408, 256), BF), dma((6,)))
    pl.run_scoped(late, vm((512, 2048), BF), vm((512, 2048), BF), vm((2048, 512), BF), vm((128, 2048), BF),
                  vm((512, 512), BF), vm((512, 512), BF), vm((512, 512), BF), vm((512, 512), BF),
                  vm((512, 128), BF), vm((512, 128), BF), vm((512, 128), BF), vm((512, 128), F32),
                  vm((512, 128), F32), vm((512, 128), F32), vm((256, 256), F32), vm((256, 512), F32),
                  vm((512, 128), F32), vm((512, 128), F32))
    second(2)
    gain_next(0)
    finish(0)
    cross(1)
    middle(3, 1)
    gain_next(1)
    middle(2, 2)
    finish(1)
    second(3)
    gain_next(2)
    cross(2)
    middle(3, 2)
    finish(2)
    gains_o[...] = pltpu.roll(gain_sum(3), lax.rem(2048 - (p.dp * 64 + tp * 16), 2048), 1)[:, :16]
    cross(3)
    finish(3)
    for stage in range(4):
        for i in range(len(stages[stage])):
            gain_copy(stage, i).wait_send()
    for pair in pairs:
        for panel in pair:
            panel.drain()
    for what in (scatter_out, scatter1, gather):
        what.drain()


def backward(kept, tokens, norm_attn, norm_mlp, cotangent, w_query, w_key, w_value, w_out, w_down, w_gate, w_up):
    (a1, a2, dy, hidden, d_gate, d_up, q, k, v, o, lse, x2, cos, sin, cnt) = kept
    vm, dma = pltpu.VMEM, pltpu.SemaphoreType.DMA
    scratch = []
    for wy, wz in MLP_PANELS[:2]:
        for w in (wy, wz):
            scratch += [vm((4, 2, 4, 64, w), BF), vm((6, 4, 64, w), BF)]
    for w in [w for pair in MLP_PANELS for w in pair]:
        scratch += [vm((4, 2, 64, w), BF), vm((6, 64, w), BF), vm((2, 64, w), BF), vm((64, w), BF), dma((13,)), dma((13,))]
    scratch += [vm((4, 128, 2048), BF)] * 4 + [vm((128, 2048), BF)] * 9
    scratch += [vm((128, 2048), F32)] + [vm((128, 2048), BF)] * 2 + [vm((4, 4, 8, 2048), F32)]
    scratch += [dma((23,))] + [dma((6,))] * 8 + [dma((12,))] * 2 + [pltpu.SemaphoreType.REGULAR((4,))]
    shapes = ((128, 2048), (128, 2048), (64, 512), (64, 64), (64, 64), (64, 512), (64, 1408), (64, 1408), (64, 1408),
              (8, 16))
    return pl.pallas_call(
        backward_kernel,
        name="backward",
        out_shape=[jax.ShapeDtypeStruct(shape, F32) for shape in shapes],
        in_specs=[pl.BlockSpec(memory_space=pltpu.VMEM)] * 3 + [pl.BlockSpec(memory_space=pl.ANY)] * 23,
        out_specs=[pl.BlockSpec(memory_space=pltpu.VMEM)] * 10,
        scratch_shapes=scratch,
        compiler_params=pltpu.CompilerParams(
            collective_id=3, has_side_effects=True, vmem_limit_bytes=63 * 2**20
        ),
    )(norm_attn.reshape(1, 2048), norm_mlp.reshape(1, 2048), cnt,
      a1.reshape(512, 2048), a2, dy.reshape(512, 2048), hidden, d_gate, d_up, q, k, v, o, lse, x2, cos, sin,
      tokens, cotangent, w_query, w_key.T, w_value.T, w_out, w_down, w_gate, w_up)


def deliver_kernel(gains, *refs):
    ins, outs, (one, two), sem = refs[:9], refs[9:18], refs[18:20], refs[20]
    copies = [pltpu.make_async_copy(i, o, sem.at[n]) for n, (i, o) in enumerate(zip(ins, outs))]
    for copy in copies:
        copy.start()
    one[...] = gains[0:1]
    two[...] = gains[1:2]
    for copy in copies:
        copy.wait()


def deliver(parts):
    *arrays, gains = parts
    shapes = [jax.ShapeDtypeStruct(a.shape, F32) for a in arrays] + [jax.ShapeDtypeStruct((1, 16), F32)] * 2
    return pl.pallas_call(
        deliver_kernel,
        name="deliver",
        out_shape=shapes,
        in_specs=[pl.BlockSpec(memory_space=pltpu.VMEM)] * 10,
        out_specs=[pl.BlockSpec(memory_space=pl.ANY)] * 9 + [pl.BlockSpec(memory_space=pltpu.VMEM)] * 2,
        scratch_shapes=[pltpu.SemaphoreType.DMA((9,))],
    )(gains, *arrays)


def per_device(
    tokens,
    norm_attn,
    w_query,
    w_key,
    w_value,
    w_out,
    norm_mlp,
    w_gate,
    w_up,
    w_down,
    segment_ids,
    cotangent,
):
    weights = (w_query, w_key, w_value, w_out, w_down, w_gate, w_up)
    kept = forward(tokens, norm_attn, norm_mlp, segment_ids, cotangent, *weights)
    (layer_out, grad_tokens, g_query, g_key, g_value, g_out, g_gate, g_up, g_down, gain1, gain2) = deliver(backward(
        kept, tokens, norm_attn, norm_mlp, cotangent, *weights))
    return (layer_out, grad_tokens, gain1.reshape(16), g_query, g_key, g_value, g_out.T, gain2.reshape(16), g_gate, g_up,
            g_down.T)


def solution(mesh):
    placed = (
        P(("dp", "tp"), None),
        P(),
        P(None, "tp"),
        P(None, "tp"),
        P(None, "tp"),
        P("tp", None),
        P(),
        P(None, "tp"),
        P(None, "tp"),
        P("tp", None),
        P(("dp", "tp")),
        P(("dp", "tp"), None),
    )
    return jax.shard_map(
        per_device,
        mesh=mesh,
        in_specs=placed,
        out_specs=(
            P(("dp", "tp"), None),
            P(("dp", "tp"), None),
            P(("dp", "tp")),
            P("dp", "tp"),
            P("dp", "tp"),
            P("dp", "tp"),
            P("tp", "dp"),
            P(("dp", "tp")),
            P("dp", "tp"),
            P("dp", "tp"),
            P("tp", "dp"),
        ),
        check_vma=False,
    )
```

```python
import math

import jax
import jax.numpy as jnp
import numpy as np
from jax import lax
from jax.experimental import pallas as pl
from jax.experimental.pallas import tpu as pltpu
from jax.sharding import PartitionSpec as P

HD = 64
BF = jnp.bfloat16
F32 = jnp.float32
MESH = pl.DeviceIdType.MESH


def place():
    dp = lax.axis_index("dp")
    tp = lax.axis_index("tp")
    return dp // 8, lax.rem(dp // 4, 2), lax.rem(dp, 4), tp


def ring(me, step):
    return lax.rem(me + step + 4, 4)


class Panel:
    def __init__(self, y_first, grad, near, second, far, last, from_x, send, recv, put):
        self.y_first = y_first
        self.grad, self.near, self.second, self.far = grad, near, second, far
        self.last, self.from_x = last, from_x
        self.send, self.recv = send, recv
        self.put = put
        y, xh, z, tp = place()
        self.xh = xh
        one, two = (y, z) if y_first else (z, y)
        steps = lambda me: (me, ring(me, 1), ring(me, 2), ring(me, -1))
        self.at = (None, steps(one), steps(two))
        self.devices = {}
        for step in (1, -1):
            along_y = (ring(y, step) * 8 + xh * 4 + z, tp)
            along_z = (y * 8 + xh * 4 + ring(z, step), tp)
            self.devices[1, step], self.devices[2, step] = (along_y, along_z) if y_first else (along_z, along_y)
        self.other = 1 - xh
        self.across = (y * 8 + self.other * 4 + z, tp)
        self.started = []

    def device(self, stage, step):
        return self.devices[stage, step]

    def part(self, stage, at, half):
        if stage == 1:
            return self.grad.at[at, half] if self.y_first else self.grad.at[:, half, at]
        return self.second.at[at, half]

    def landed(self, stage, k):
        return (self.near if stage == 1 else self.far).at[k]

    def copy(self, stage, k, at, half, step):
        sem = k + (6 if stage == 2 else 0)
        return pltpu.make_async_remote_copy(
            src_ref=self.part(stage, at, half),
            dst_ref=self.landed(stage, k),
            send_sem=self.send.at[sem],
            recv_sem=self.recv.at[sem],
            device_id=self.device(stage, step),
            device_id_type=MESH,
        )

    def go(self, stage, k, at, half, step):
        what = (stage, k, at, half, step)
        self.copy(*what).start()
        self.started.append(what)

    def arrived(self, stage, k):
        self.copy(stage, k, self.at[stage][0], 0, 1).wait_recv()

    def begin(self, stage):
        me, right, over, left = self.at[stage]
        self.go(stage, 0, over, 0, 1)
        self.go(stage, 1, over, 1, -1)
        self.go(stage, 2, right, 1, 1)
        self.go(stage, 3, left, 0, -1)

    def add(self, into, what):
        if len(into.shape) == 3:
            @pl.loop(0, into.shape[0])
            def _(i):
                into[i] = (into[i].astype(F32) + what[i].astype(F32)).astype(BF)
        else:
            into[...] = (into[...].astype(F32) + what[...].astype(F32)).astype(BF)

    def middle(self, stage):
        me, right, over, left = self.at[stage]
        for k, at, half, step in ((0, right, 0, 1), (1, left, 1, -1)):
            self.arrived(stage, k)
            self.add(self.part(stage, at, half), self.landed(stage, k))
            self.go(stage, k + 4, at, half, step)

    def end(self, stage):
        me = self.at[stage][0]
        for half, (a, b) in enumerate(((4, 3), (2, 5))):
            self.arrived(stage, a)
            self.arrived(stage, b)
            own, one, two = self.part(stage, me, half), self.landed(stage, a), self.landed(stage, b)
            if stage == 1:
                @pl.loop(0, 4)
                def _(q):
                    total = own[q].astype(F32) + one[q].astype(F32) + two[q].astype(F32)
                    self.second[q, half] = total.astype(BF)
            else:
                total = own[...].astype(F32) + one[...].astype(F32) + two[...].astype(F32)
                self.last[half] = total.astype(BF)

    def crossing(self):
        return pltpu.make_async_remote_copy(
            src_ref=self.last.at[self.other],
            dst_ref=self.from_x,
            send_sem=self.send.at[12],
            recv_sem=self.recv.at[12],
            device_id=self.across,
            device_id_type=MESH,
        )

    def cross(self):
        self.crossing().start()

    def finish(self):
        self.crossing().wait_recv()
        self.put(self.last[self.xh].astype(F32) + self.from_x[...].astype(F32))

    def sent(self, count):
        for what in self.started[:count]:
            self.copy(*what).wait_send()
        self.started = self.started[count:]

    def drain(self):
        self.sent(len(self.started))
        self.crossing().wait_send()


def dot(a, b):
    return jnp.dot(a, b, preferred_element_type=F32)


def dot_nt(a, b):
    return lax.dot_general(a, b, (((1,), (1,)), ((), ())), preferred_element_type=F32)


def dot_tn(a, b):
    return lax.dot_general(a, b, (((0,), (0,)), ((), ())), preferred_element_type=F32)


class Peers:
    def __init__(self):
        self.dp = lax.axis_index("dp")
        self.me = lax.axis_index("tp")
        self.core = self.me + 1 - 2 * lax.rem(self.me, 2)
        self.next = lax.rem(self.me + 2, 4)
        self.far = lax.rem(self.core + 2, 4)
        self.chip = self.me // 2
        self.to_core = (self.dp, self.core)
        self.to_next = (self.dp, self.next)
        self.to_far = (self.dp, self.far)


class Gather:
    def __init__(self, peers, buf, send, recv, parts):
        self.p, self.buf, self.send, self.recv, self.parts = peers, buf, send, recv, parts
        self.rows = buf.shape[1] // parts
        self.started = []

    def copy(self, kind, owner, i, device):
        at = self.buf.at[owner, pl.ds(i * self.rows, self.rows)]
        sem = kind * self.parts + i
        return pltpu.make_async_remote_copy(
            src_ref=at, dst_ref=at, send_sem=self.send.at[sem], recv_sem=self.recv.at[sem],
            device_id=device, device_id_type=MESH)

    def go(self, *what):
        self.copy(*what).start()
        self.started.append(what)

    def start(self, i):
        self.go(1, self.p.me, i, self.p.to_next)
        self.go(0, self.p.me, i, self.p.to_core)

    def near(self):
        for i in range(self.parts):
            self.copy(0, self.p.core, i, self.p.to_core).wait_recv()

    def forward(self, i):
        self.copy(1, self.p.next, i, self.p.to_next).wait_recv()
        self.go(2, self.p.next, i, self.p.to_core)

    def rest(self, i):
        self.copy(2, self.p.far, i, self.p.to_core).wait_recv()

    def drain(self):
        for what in self.started:
            self.copy(*what).wait_send()
        self.started = []


class Scatter:
    def __init__(self, peers, part, r0, r1, r2, send, recv, parts):
        self.p, self.part, self.r = peers, part, (r0, r1, r2)
        self.send, self.recv, self.parts = send, recv, parts
        self.rows = part.shape[1] // parts
        self.started = []

    def rowsof(self, i):
        return pl.ds(i * self.rows, self.rows)

    def copy(self, kind, owner, i, device):
        sem = kind * self.parts + i
        return pltpu.make_async_remote_copy(
            src_ref=self.part.at[owner, self.rowsof(i)], dst_ref=self.r[kind].at[self.rowsof(i)],
            send_sem=self.send.at[sem], recv_sem=self.recv.at[sem],
            device_id=device, device_id_type=MESH)

    def go(self, *what):
        self.copy(*what).start()
        self.started.append(what)

    def cross(self, i):
        self.go(0, self.p.far, i, self.p.to_core)

    def own(self, i):
        self.go(1, self.p.core, i, self.p.to_core)

    def combine(self, i):
        self.copy(0, self.p.far, i, self.p.to_core).wait_recv()
        at = self.part.at[self.p.next, self.rowsof(i)]
        at[...] = (at[...].astype(F32) + self.r[0][self.rowsof(i)].astype(F32)).astype(BF)
        self.go(2, self.p.next, i, self.p.to_next)

    def total(self, i):
        self.copy(1, self.p.core, i, self.p.to_core).wait_recv()
        self.copy(2, self.p.next, i, self.p.to_next).wait_recv()
        rows = self.rowsof(i)
        return (self.part[self.p.me, rows].astype(F32) + self.r[1][rows].astype(F32)
                + self.r[2][rows].astype(F32))

    def drain(self):
        for what in self.started:
            self.copy(*what).wait_send()
        self.started = []


def rope_tables():
    inverse = np.exp(np.arange(32, dtype=np.float64) * (-2.0 * math.log(10000.0) / 64))
    angles = np.arange(512, dtype=np.float64)[:, None] * np.tile(inverse, 4)[None, :]
    return (np.cos(angles).astype(np.float32), np.sin(angles).astype(np.float32),
            np.tile(inverse, 4)[None, :].astype(np.float32))


def lanes(shape):
    return lax.broadcasted_iota(jnp.int32, shape, len(shape) - 1)


def turned(values):
    low = lax.rem(lanes(values.shape), 64) < 32
    return jnp.where(low, pltpu.roll(values, 96, 1), pltpu.roll(values, 32, 1))


def split_heads(pair):
    left = lanes(pair.shape) < 64
    zero = jnp.zeros_like(pair)
    return jnp.concatenate([jnp.where(left, pair, zero), jnp.where(left, zero, pair)], axis=0)


BLOCKS = ((0, 256, 256), (256, 256, 512))
FF_TILES = ((0, 512), (512, 512), (1024, 384))


def mask_bias(bias, first, start, rows, keys):
    row = lax.broadcasted_iota(jnp.int32, (rows, keys), 0) + start
    key = lax.broadcasted_iota(jnp.int32, (rows, keys), 1)
    allowed = (key <= row) & ((row < first) == (key < first))
    bias[...] = jnp.where(allowed, 0.0, -1e9).astype(F32)


def inverse_rms(rows):
    return lax.rsqrt(jnp.mean(rows * rows, axis=1, keepdims=True) + 1e-5)


def chip_rows(buf, chip):
    return buf[pl.ds(chip * 2, 2)].reshape(256, buf.shape[2])


def forward_kernel(x, gain1, gain2, cos0, sin0, inv, seg, dy_own, *refs):
    hbm_w, refs = refs[:7], refs[7:]
    outs, refs = refs[:15], refs[15:]
    (a1_o, a2_o, dy_o, hid_o, dg_o, du_o, q_o, k_o, v_o, o_o, lse_o, x2_o, cos_o, sin_o, cnt_o) = outs
    (A1, A2, DY, Wq, Wkv, Wo, Wd, Wg, Wu, Q, K, V, O, LSE, PM, R0, R1, R2, DH, HID, DG, DU, X2, COS, SIN,
     CNT, B0, B1, wsem, osem, g1s, g1r, g2s, g2r, g3s, g3r, ss, sr, cs, cr) = refs
    weights = (Wq, Wkv.at[pl.ds(0, 64)], Wkv.at[pl.ds(64, 64)], Wo, Wd, Wg, Wu)
    loads = [pltpu.make_async_copy(h, w, wsem.at[i]) for i, (h, w) in enumerate(zip(hbm_w, weights))]
    p = Peers()
    barrier = pltpu.get_barrier_semaphore()
    for device in (p.to_core, p.to_next, p.to_far):
        pl.semaphore_signal(barrier, inc=1, device_id=device, device_id_type=MESH)
    for load in loads:
        load.start()
    stored = []

    def keep(src, dst):
        copy = pltpu.make_async_copy(src, dst, osem.at[len(stored)])
        copy.start()
        stored.append(copy)

    stream = x[...].astype(F32)
    A1[p.me] = (stream * inverse_rms(stream) * gain1[...]).astype(BF)
    DY[p.me] = dy_own[...]
    CNT[p.me] = jnp.broadcast_to(jnp.sum(seg[...], axis=1, keepdims=True), (8, 128))
    pl.semaphore_wait(barrier, 3)
    first_in = Gather(p, A1, g1s, g1r, 2)
    for i in range(2):
        first_in.start(i)
    counts = [pltpu.make_async_remote_copy(
        src_ref=CNT.at[p.me], dst_ref=CNT.at[p.me], send_sem=cs.at[i], recv_sem=cr.at[i],
        device_id=device, device_id_type=MESH) for i, device in enumerate((p.to_core, p.to_next, p.to_far))]
    for copy in counts:
        copy.start()
    dy_in = Gather(p, DY, g2s, g2r, 2)
    for i in range(2):
        dy_in.start(i)
    for i, owner in enumerate((p.core, p.next, p.far)):
        pltpu.make_async_remote_copy(
            src_ref=CNT.at[owner], dst_ref=CNT.at[owner], send_sem=cs.at[i], recv_sem=cr.at[i],
            device_id=p.to_core, device_id_type=MESH).wait_recv()
    ones = CNT[0] + CNT[1] + CNT[2] + CNT[3]
    first = 512 - ones[0:1, 0:1]
    angle = first.astype(F32) * inv[...]
    cos_n, sin_n = jnp.cos(angle), jnp.sin(angle)
    row = lax.broadcasted_iota(jnp.int32, (512, 128), 0)
    c0, s0 = cos0[...], sin0[...]
    COS[...] = jnp.where(row < first, c0, c0 * cos_n + s0 * sin_n)
    sine = jnp.where(row < first, s0, s0 * cos_n - c0 * sin_n)
    SIN[...] = jnp.where(lax.rem(lanes((512, 128)), 64) < 32, -sine, sine)
    for bias, block in zip((B0, B1), BLOCKS):
        mask_bias(bias, first, *block)
    keep(COS, cos_o)
    keep(SIN, sin_o)
    keep(CNT, cnt_o)

    def project(chip):
        rows = pl.ds(pl.multiple_of(chip * 256, 256), 256)
        a = chip_rows(A1, chip)
        cos, sin = COS[rows], SIN[rows]
        for j in range(2):
            q = dot(a, Wq[:, pl.ds(256 * j, 256)])
            for h in range(2):
                pair = q[:, 128 * h:128 * h + 128]
                Q[rows, pl.ds(256 * j + 128 * h, 128)] = (pair * cos + turned(pair) * sin).astype(BF)
        kv = dot_nt(a, Wkv[...])
        vk = pltpu.roll(kv, 64, 1)
        k_lane = lanes(kv.shape) < 64
        kk = jnp.where(k_lane, kv, vk)
        K[rows] = (kk * cos + turned(kk) * sin).astype(BF)
        V[rows] = jnp.where(k_lane, vk, kv).astype(BF)

    for load in loads[:3]:
        load.wait()
    first_in.near()
    project(p.chip)
    for i in range(2):
        first_in.forward(i)
    for i in range(2):
        first_in.rest(i)
    project(1 - p.chip)
    keep(A1, a1_o)
    keep(Q, q_o)
    keep(K, k_o)
    keep(V, v_o)

    zero = jnp.zeros((512, 128), BF)
    left = lanes((512, 128)) < 64
    for j in range(4):
        for bias, (start, rows, keys) in zip((B0, B1), BLOCKS):
            qs = split_heads(Q[pl.ds(start, rows), pl.ds(128 * j, 128)])
            s = dot_nt(qs, K[:keys]) * 0.125
            s = (s.reshape(2, rows, keys) + bias[...][None]).reshape(2 * rows, keys)
            top = jnp.max(s, axis=1, keepdims=True)
            e = jnp.exp(s - top)
            total = jnp.sum(e, axis=1, keepdims=True)
            lse = top + jnp.log(total)
            eb = (e / total).astype(BF)
            vl = jnp.where(left[:keys], V[:keys], zero[:keys])
            vr = jnp.where(left[:keys], zero[:keys], V[:keys])
            o = dot(eb[:rows], vl) + dot(eb[rows:], vr)
            O[pl.ds(start, rows), pl.ds(128 * j, 128)] = o.astype(BF)
            lane = lanes((rows, 128))
            old = LSE[pl.ds(start, rows)] if j else jnp.zeros((rows, 128), F32)
            LSE[pl.ds(start, rows)] = jnp.where(lane == 2 * j, lse[:rows], jnp.where(lane == 2 * j + 1, lse[rows:], old))
    keep(O, o_o)
    keep(LSE, lse_o)

    def spread(chip):
        rows = pl.ds(pl.multiple_of(chip * 256, 256), 256)
        for j in range(4):
            cols = pl.ds(512 * j, 512)
            PM[pl.ds(chip * 2, 2), :, cols] = dot(O[rows], Wo[:, cols]).astype(BF).reshape(2, 128, 512)

    loads[3].wait()
    scatter = Scatter(p, PM, R0, R1, R2, ss, sr, 2)
    spread(1 - p.chip)
    for i in range(2):
        scatter.cross(i)
    spread(p.chip)
    for i in range(2):
        scatter.own(i)
    for i in range(2):
        scatter.combine(i)
    loads[4].wait()
    dy_in.near()
    for i in range(2):
        dy_in.forward(i)
    for i in range(2):
        dy_in.rest(i)
    keep(DY, dy_o)
    dy = DY[...].reshape(512, 2048)
    for start, width in FF_TILES:
        DH[:, pl.ds(start, width)] = dot_nt(dy, Wd[pl.ds(start, width)])
    second_in = Gather(p, A2, g3s, g3r, 2)
    for i in range(2):
        rows = scatter.rowsof(i)
        x2 = x[rows].astype(F32) + scatter.total(i)
        X2[rows] = x2
        A2[p.me, rows] = (x2 * inverse_rms(x2) * gain2[...]).astype(BF)
        second_in.start(i)
    keep(X2, x2_o)

    def mlp(chip):
        rows = pl.ds(pl.multiple_of(chip * 256, 256), 256)
        a = chip_rows(A2, chip)
        for start, width in FF_TILES:
            cols = pl.ds(start, width)
            g = dot(a, Wg[:, cols])
            u = dot(a, Wu[:, cols])
            dh = DH[rows, cols]
            sg = jax.nn.sigmoid(g)
            act = g * sg
            HID[rows, cols] = (act * u).astype(BF)
            DU[rows, cols] = (dh * act).astype(BF)
            DG[rows, cols] = (dh * u * (sg + act * (1.0 - sg))).astype(BF)

    loads[5].wait()
    loads[6].wait()
    second_in.near()
    mlp(p.chip)
    for i in range(2):
        second_in.forward(i)
    for i in range(2):
        second_in.rest(i)
    keep(A2, a2_o)
    mlp(1 - p.chip)
    keep(HID, hid_o)
    keep(DG, dg_o)
    keep(DU, du_o)
    for copy in stored:
        copy.wait()
    for copy in counts:
        copy.wait_send()
    for what in (first_in, dy_in, second_in, scatter):
        what.drain()


def forward(tokens, norm_attn, norm_mlp, segment_ids, cotangent, w_query, w_key, w_value, w_out, w_down, w_gate, w_up):
    cos0, sin0, inv = rope_tables()
    rows4 = (4, 128, 2048)
    spec = lambda shape, kind: jax.ShapeDtypeStruct(shape, kind)
    outs = [spec(rows4, BF)] * 3 + [spec((512, 1408), BF)] * 3 + [
        spec((512, 512), BF), spec((512, 128), BF), spec((512, 128), BF), spec((512, 512), BF),
        spec((512, 128), F32), spec((128, 2048), F32), spec((512, 128), F32), spec((512, 128), F32),
        spec((4, 8, 128), jnp.int32)]
    vm = pltpu.VMEM
    dma = pltpu.SemaphoreType.DMA
    scratch = [vm(rows4, BF)] * 3 + [
        vm((2048, 512), BF), vm((128, 2048), BF), vm((512, 2048), BF), vm((1408, 2048), BF),
        vm((2048, 1408), BF), vm((2048, 1408), BF),
        vm((512, 512), BF), vm((512, 128), BF), vm((512, 128), BF), vm((512, 512), BF), vm((512, 128), F32),
        vm(rows4, BF), vm((128, 2048), BF), vm((128, 2048), BF), vm((128, 2048), BF), vm((512, 1408), F32),
        vm((512, 1408), BF), vm((512, 1408), BF), vm((512, 1408), BF), vm((128, 2048), F32),
        vm((512, 128), F32), vm((512, 128), F32), vm((4, 8, 128), jnp.int32), vm((256, 256), F32), vm((256, 512), F32),
        dma((7,)), dma((15,))] + [dma((6,))] * 8 + [dma((3,))] * 2
    return pl.pallas_call(
        forward_kernel,
        name="forward",
        out_shape=outs,
        in_specs=[pl.BlockSpec(memory_space=pltpu.VMEM)] * 8 + [pl.BlockSpec(memory_space=pl.ANY)] * 7,
        out_specs=[pl.BlockSpec(memory_space=pl.ANY)] * 15,
        scratch_shapes=scratch,
        compiler_params=pltpu.CompilerParams(
            collective_id=2, has_side_effects=True, vmem_limit_bytes=62 * 2**20
        ),
    )(tokens, norm_attn.reshape(1, 2048), norm_mlp.reshape(1, 2048), cos0, sin0, inv, segment_ids.reshape(1, 128),
      cotangent, w_query, w_key.T, w_value.T, w_out, w_down, w_gate, w_up)


MLP_PANELS = ((768, 640), (640, 768), (768, 640), (512, 640))


def grad_panel(grad, left, right, width, start):
    @pl.loop(0, 4)
    def _(at):
        rows = left[:, pl.ds(pl.multiple_of(at * 512, 512), 512)]
        cols = pl.ds(start, width)
        grad[at] = dot_tn(rows, right[:, cols]).astype(BF).reshape(2, 4, 64, width)


def grad_begin(panel, left, right, width, start):
    me, after, over, before = panel.at[1]
    for at, sends in ((over, ((0, over, 0, 1), (1, over, 1, -1))), (after, ((2, after, 1, 1),)),
                      (before, ((3, before, 0, -1),)), (me, ())):
        rows = left[:, pl.ds(pl.multiple_of(at * 512, 512), 512)]
        cols = pl.ds(start, width)
        panel.grad[at] = dot_tn(rows, right[:, cols]).astype(BF).reshape(2, 4, 64, width)
        for what in sends:
            panel.go(1, *what)


def norm_back(dn, rows, gain):
    r = inverse_rms(rows)
    e = dn * gain
    back = r * e - rows * (r * r * r) * jnp.mean(e * rows, axis=1, keepdims=True)
    return back, jnp.sum(dn * rows * r, axis=0, keepdims=True)


def backward_kernel(gain1, gain2, cnt, *refs):
    (a1_h, a2_h, dy_h, hid_h, dg_h, du_h, q_h, k_h, v_h, o_h, lse_h, x2_h, cos_h, sin_h,
     x_h, dyo_h, wq_h, wk_h, wv_h, wo_h, wd_h, wg_h, wu_h) = refs[:23]
    (lo_o, gt_o, gq_o, gk_o, gv_o, go_o, gg_o, gu_o, gd_o, gains_o) = refs[23:33]
    refs = refs[33:]
    sets, refs = (refs[:4], refs[4:8]), refs[8:]
    slots, refs = [refs[6 * i:6 * i + 6] for i in range(8)], refs[48:]
    (X0, X1, X3, DX2F, Ra0, Ra1, Ra2, Rb0, Rb1, Rb2, Rc0, Rc1, Rc2, X2, X, DYO, GA,
     lsem, s2s, s2r, sls, slr, s1s, s1r, g4s, g4r, gs, gr, credit) = refs
    y, xh, z, tp = place()
    p = Peers()
    peers = [
        (ring(y, 1) * 8 + xh * 4 + z, tp), (ring(y, -1) * 8 + xh * 4 + z, tp),
        (y * 8 + xh * 4 + ring(z, 1), tp), (y * 8 + xh * 4 + ring(z, -1), tp),
        (ring(y, 2) * 8 + xh * 4 + z, tp), (y * 8 + xh * 4 + ring(z, 2), tp),
        (y * 8 + (1 - xh) * 4 + z, tp), p.to_core, p.to_next, p.to_far]
    barrier = pltpu.get_barrier_semaphore()
    for device in peers:
        pl.semaphore_signal(barrier, inc=1, device_id=device, device_id_type=MESH)

    n_loads = [0]

    def load(src, dst):
        copy = pltpu.make_async_copy(src, dst, lsem.at[n_loads[0]])
        n_loads[0] += 1
        copy.start()
        return copy

    def put_cols(ref, start, width):
        def put(v):
            ref[:, pl.ds(start, width)] = v
        return put

    def put_q(v):
        gq_o[...] = v

    def put_kvo(v):
        gk_o[...] = v[:, :64]
        gv_o[...] = v[:, 64:128]
        go_o[...] = v[:, 128:]

    puts = (put_cols(gd_o, 0, 768), put_cols(gd_o, 768, 640), put_cols(gg_o, 0, 640), put_cols(gg_o, 640, 768),
            put_cols(gu_o, 0, 768), put_cols(gu_o, 768, 640), put_q, put_kvo)
    pairs = []
    for j, widths in enumerate(MLP_PANELS):
        Gy, Ny, Gz, Nz = sets[j % 2]
        pair = []
        for i, (G, N, width) in enumerate(((Gy, Ny, widths[0]), (Gz, Nz, widths[1]))):
            if G.shape[4] != width:
                G, N = G.at[:, :, :, :, pl.ds(0, width)], N.at[:, :, :, pl.ds(0, width)]
            pair.append(Panel(i == 0, G, N, *slots[2 * j + i], puts[2 * j + i]))
        pairs.append(pair)

    stages = ((peers[0], peers[1], peers[4]), (peers[2], peers[3], peers[5]), (peers[6],), (p.to_core, p.to_next, p.to_far))

    def gain_copy(stage, i):
        sem = 3 * stage + i
        return pltpu.make_async_remote_copy(
            src_ref=GA.at[stage, 0], dst_ref=GA.at[stage, i + 1], send_sem=gs.at[sem], recv_sem=gr.at[sem],
            device_id=stages[stage][i], device_id_type=MESH)

    def gain_send(stage):
        for i in range(len(stages[stage])):
            gain_copy(stage, i).start()

    def gain_sum(stage):
        total = GA[stage, 0]
        for i in range(len(stages[stage])):
            gain_copy(stage, i).wait_recv()
            total = total + GA[stage, i + 1]
        return total

    def gain_next(stage):
        GA[stage + 1, 0] = gain_sum(stage)
        gain_send(stage + 1)

    def second(j, i):
        panel = pairs[j][i]
        panel.end(1)
        if j < 2:
            for step in (1, -1):
                pl.semaphore_signal(credit.at[2 * j + i], inc=1, device_id=panel.device(1, step), device_id_type=MESH)
        panel.begin(2)

    def cross(j, i):
        pairs[j][i].end(2)
        pairs[j][i].cross()

    def reuse(j, i):
        pairs[j][i].sent(6)
        pl.semaphore_wait(credit.at[2 * j + i], 2)

    scatter2 = Scatter(p, X0, Ra0, Ra1, Ra2, s2s, s2r, 2)
    scatter_out = Scatter(p, X3, Rb0, Rb1, Rb2, sls, slr, 2)
    scatter1 = Scatter(p, X0, Rc0, Rc1, Rc2, s1s, s1r, 2)
    gather = Gather(p, DX2F, g4s, g4r, 2)

    def early(DY, HID, DG, DU, WG, WU, WD, wsem):
        l_dy, l_hid = load(dy_h, DY), load(hid_h, HID)
        l_a2, l_dg, l_du = load(a2_h, X1), load(dg_h, DG), load(du_h, DU)

        def gate_chunk(i):
            at = pl.ds(256 * i, 256)
            return [pltpu.make_async_copy(wg_h.at[at], WG.at[i % 2], wsem.at[i % 2]),
                    pltpu.make_async_copy(wu_h.at[at], WU.at[i % 2], wsem.at[2 + i % 2])]

        def down_chunk(i):
            return [pltpu.make_async_copy(wd_h.at[:, pl.ds(256 * i, 256)], WD.at[i % 2], wsem.at[4 + i % 2])]

        for i in range(2):
            for copy in gate_chunk(i) + down_chunk(i):
                copy.start()
        l_x2, l_x, l_dyo = load(x2_h, X2), load(x_h, X), load(dyo_h, DYO)
        l_dy.wait()
        l_hid.wait()
        GA[0, 0] = jnp.zeros((8, 2048), F32)
        pl.semaphore_wait(barrier, len(peers))
        grad_begin(pairs[0][0], DY, HID, 768, 0)
        grad_panel(pairs[0][1].grad, DY, HID, 640, 768)
        pairs[0][1].begin(1)
        l_dg.wait()
        l_du.wait()
        for i in range(8):
            for copy in gate_chunk(i):
                copy.wait()
            da = dot_nt(DG[...], WG[i % 2]) + dot_nt(DU[...], WU[i % 2])
            X0[:, :, pl.ds(256 * i, 256)] = da.astype(BF).reshape(4, 128, 256)
            if i < 6:
                for copy in gate_chunk(i + 2):
                    copy.start()
        pairs[0][0].middle(1)
        pairs[0][1].middle(1)
        for i in range(2):
            scatter2.cross(i)
        for i in range(2):
            scatter2.own(i)
        l_a2.wait()
        a2 = X1.reshape(512, 2048)
        grad_begin(pairs[1][0], a2, DG, 640, 0)
        grad_panel(pairs[1][1].grad, a2, DG, 768, 640)
        pairs[1][1].begin(1)
        for i in range(2):
            scatter2.combine(i)
        for i in range(8):
            for copy in down_chunk(i):
                copy.wait()
            X3[:, :, pl.ds(256 * i, 256)] = dot(HID[...], WD[i % 2]).astype(BF).reshape(4, 128, 256)
            if i < 6:
                for copy in down_chunk(i + 2):
                    copy.start()
        for i in range(2):
            scatter_out.cross(i)
        for i in range(2):
            scatter_out.own(i)
        l_x2.wait()
        l_x.wait()
        l_dyo.wait()

        def middle_rows(i):
            rows = scatter2.rowsof(i)
            back, gain = norm_back(scatter2.total(i), X2[rows], gain2[...])
            GA[0, 0, 1:2] += gain
            dx2 = DYO[rows].astype(F32) + back
            lo_o[rows] = X2[rows]
            X2[rows] = dx2
            DX2F[p.me, rows] = dx2.astype(BF)
            gather.start(i)

        middle_rows(0)
        second(0, 1)
        second(0, 0)
        middle_rows(1)
        for i in range(2):
            scatter_out.combine(i)
        reuse(0, 0)
        grad_begin(pairs[2][0], a2, DU, 768, 0)
        pairs[1][1].middle(1)
        pairs[1][0].middle(1)
        reuse(0, 1)
        grad_panel(pairs[2][1].grad, a2, DU, 640, 768)
        pairs[2][1].begin(1)

    def late(A1, Wo, Wq, Wkv, Q, O, DO, DQ, K, V, DKV, LSE, COS, SIN, B0, B1, DK, DV):
        l_wo, l_q, l_k, l_v, l_lse, l_cos, l_sin, l_o, l_a1, l_wq, l_wk, l_wv = [load(*w) for w in (
            (wo_h, Wo), (q_h, Q), (k_h, K), (v_h, V), (lse_h, LSE), (cos_h, COS), (sin_h, SIN), (o_h, O),
            (a1_h, A1), (wq_h, Wq), (wk_h, Wkv.at[pl.ds(0, 64)]), (wv_h, Wkv.at[pl.ds(64, 64)]))]
        ones = cnt[0] + cnt[1] + cnt[2] + cnt[3]
        first = 512 - ones[0:1, 0:1]
        for bias, block in zip((B0, B1), BLOCKS):
            mask_bias(bias, first, *block)
        gather.near()
        gather.forward(0)
        l_wo.wait()

        def back_out(chip):
            rows = pl.ds(pl.multiple_of(chip * 256, 256), 256)
            DO[rows] = dot_nt(chip_rows(DX2F, chip), Wo[...]).astype(BF)

        back_out(p.chip)
        gather.forward(1)
        pairs[0][1].middle(2)
        for i in range(2):
            gather.rest(i)
        back_out(1 - p.chip)
        for copy in (l_q, l_k, l_v, l_lse, l_cos, l_sin, l_o, l_a1):
            copy.wait()
        zero = jnp.zeros((512, 128), BF)
        left = lanes((512, 128)) < 64

        def heads(j):
            cols = pl.ds(128 * j, 128)
            for bias, (start, rows, keys) in zip((B0, B1), BLOCKS):
                at = pl.ds(start, rows)
                qs = split_heads(Q[at, cols])
                dos = split_heads(DO[at, cols])
                s = dot_nt(qs, K[:keys]) * 0.125
                s = (s.reshape(2, rows, keys) + bias[...][None]).reshape(2 * rows, keys)
                lse = jnp.concatenate([LSE[at, 2 * j:2 * j + 1], LSE[at, 2 * j + 1:2 * j + 2]], axis=0)
                prob = jnp.exp(s - lse)
                dp = dot_nt(dos, V[:keys])
                row_dot = jnp.sum(prob * dp, axis=1, keepdims=True)
                ds = (prob * (dp - row_dot) * 0.125).astype(BF)
                dv = dot_tn(prob.astype(BF), dos)
                dk = dot_tn(ds, qs)
                if j == 0 and keys == 512:
                    DV[256:] = dv[256:]
                    DK[256:] = dk[256:]
                    DV[:256] += dv[:256]
                    DK[:256] += dk[:256]
                elif j == 0:
                    DV[:keys] = dv
                    DK[:keys] = dk
                else:
                    DV[:keys] += dv
                    DK[:keys] += dk
                kl = jnp.where(left[:keys], K[:keys], zero[:keys])
                kr = jnp.where(left[:keys], zero[:keys], K[:keys])
                dq = dot(ds[:rows], kl) + dot(ds[rows:], kr)
                DQ[at, cols] = (dq * COS[at] - turned(dq) * SIN[at]).astype(BF)

        for j in range(4):
            heads(j)
        dk = DK[...] + pltpu.roll(DK[...], 64, 1)
        dv = DV[...] + pltpu.roll(DV[...], 64, 1)
        DKV[...] = jnp.where(left, dk * COS[...] - turned(dk) * SIN[...], dv).astype(BF)
        l_wq.wait()
        l_wk.wait()
        l_wv.wait()
        scatter2.drain()
        for i in range(4):
            at = pl.ds(512 * i, 512)
            da = dot_nt(DQ[...], Wq[at]) + dot(DKV[...], Wkv[:, at])
            X0[:, :, at] = da.astype(BF).reshape(4, 128, 512)
        for i in range(2):
            scatter1.cross(i)
        for i in range(2):
            scatter1.own(i)
        second(1, 1)
        pairs[2][0].middle(1)
        for i in range(2):
            scatter1.combine(i)
        pairs[0][0].middle(2)
        for i in range(2):
            rows = scatter_out.rowsof(i)
            lo_o[rows] = lo_o[rows] + scatter_out.total(i)
        pairs[2][1].middle(1)

        def first_rows(i):
            rows = scatter1.rowsof(i)
            back, gain = norm_back(scatter1.total(i), X[rows].astype(F32), gain1[...])
            GA[0, 0, 0:1] += gain
            gt_o[rows] = X2[rows] + back

        first_rows(0)
        second(1, 0)
        cross(0, 1)
        cross(0, 0)
        reuse(1, 0)
        grad_begin(pairs[3][0], A1, DQ, 512, 0)
        reuse(1, 1)
        grad_z = pairs[3][1].grad
        grad_panel(grad_z.at[:, :, :, :, pl.ds(0, 128)], A1, DKV, 128, 0)
        grad_panel(grad_z.at[:, :, :, :, pl.ds(128, 512)], DX2F.reshape(512, 2048), O, 512, 0)
        pairs[3][1].begin(1)
        first_rows(1)
        gain_send(0)
        pairs[0][1].finish()
        pairs[1][1].middle(2)
        pairs[0][0].finish()

    vm, dma = pltpu.VMEM, pltpu.SemaphoreType.DMA
    pl.run_scoped(early, vm((512, 2048), BF), vm((512, 1408), BF), vm((512, 1408), BF), vm((512, 1408), BF),
                  vm((2, 256, 1408), BF), vm((2, 256, 1408), BF), vm((2, 1408, 256), BF), dma((6,)))
    pl.run_scoped(late, vm((512, 2048), BF), vm((512, 2048), BF), vm((2048, 512), BF), vm((128, 2048), BF),
                  vm((512, 512), BF), vm((512, 512), BF), vm((512, 512), BF), vm((512, 512), BF),
                  vm((512, 128), BF), vm((512, 128), BF), vm((512, 128), BF), vm((512, 128), F32),
                  vm((512, 128), F32), vm((512, 128), F32), vm((256, 256), F32), vm((256, 512), F32),
                  vm((512, 128), F32), vm((512, 128), F32))
    second(2, 1)
    pairs[1][0].middle(2)
    second(2, 0)
    gain_next(0)
    pairs[3][1].middle(1)
    pairs[3][0].middle(1)
    gain_next(1)
    cross(1, 1)
    cross(1, 0)
    pairs[2][1].middle(2)
    pairs[2][0].middle(2)
    gain_next(2)
    pairs[1][1].finish()
    pairs[1][0].finish()
    second(3, 0)
    cross(2, 1)
    second(3, 1)
    cross(2, 0)
    pairs[2][1].finish()
    pairs[3][0].middle(2)
    gains_o[...] = pltpu.roll(gain_sum(3), lax.rem(2048 - (p.dp * 64 + tp * 16), 2048), 1)[:, :16]
    pairs[3][1].middle(2)
    pairs[2][0].finish()
    cross(3, 0)
    cross(3, 1)
    pairs[3][0].finish()
    pairs[3][1].finish()
    for stage in range(4):
        for i in range(len(stages[stage])):
            gain_copy(stage, i).wait_send()
    for pair in pairs:
        for panel in pair:
            panel.drain()
    for what in (scatter_out, scatter1, gather):
        what.drain()


def backward(kept, tokens, norm_attn, norm_mlp, cotangent, w_query, w_key, w_value, w_out, w_down, w_gate, w_up):
    (a1, a2, dy, hidden, d_gate, d_up, q, k, v, o, lse, x2, cos, sin, cnt) = kept
    vm, dma = pltpu.VMEM, pltpu.SemaphoreType.DMA
    scratch = []
    for wy, wz in MLP_PANELS[:2]:
        for w in (wy, wz):
            scratch += [vm((4, 2, 4, 64, w), BF), vm((6, 4, 64, w), BF)]
    for w in [w for pair in MLP_PANELS for w in pair]:
        scratch += [vm((4, 2, 64, w), BF), vm((6, 64, w), BF), vm((2, 64, w), BF), vm((64, w), BF), dma((13,)), dma((13,))]
    scratch += [vm((4, 128, 2048), BF)] * 4 + [vm((128, 2048), BF)] * 9
    scratch += [vm((128, 2048), F32)] + [vm((128, 2048), BF)] * 2 + [vm((4, 4, 8, 2048), F32)]
    scratch += [dma((23,))] + [dma((6,))] * 8 + [dma((12,))] * 2 + [pltpu.SemaphoreType.REGULAR((4,))]
    shapes = ((128, 2048), (128, 2048), (64, 512), (64, 64), (64, 64), (64, 512), (64, 1408), (64, 1408), (64, 1408),
              (8, 16))
    return pl.pallas_call(
        backward_kernel,
        name="backward",
        out_shape=[jax.ShapeDtypeStruct(shape, F32) for shape in shapes],
        in_specs=[pl.BlockSpec(memory_space=pltpu.VMEM)] * 3 + [pl.BlockSpec(memory_space=pl.ANY)] * 23,
        out_specs=[pl.BlockSpec(memory_space=pltpu.VMEM)] * 10,
        scratch_shapes=scratch,
        compiler_params=pltpu.CompilerParams(
            collective_id=3, has_side_effects=True, vmem_limit_bytes=63 * 2**20
        ),
    )(norm_attn.reshape(1, 2048), norm_mlp.reshape(1, 2048), cnt,
      a1.reshape(512, 2048), a2, dy.reshape(512, 2048), hidden, d_gate, d_up, q, k, v, o, lse, x2, cos, sin,
      tokens, cotangent, w_query, w_key.T, w_value.T, w_out, w_down, w_gate, w_up)


def deliver_kernel(gains, *refs):
    ins, outs, (one, two), held, sems = refs[:9], refs[9:18], refs[18:20], refs[20:29], refs[29:]
    come = [pltpu.make_async_copy(i, h, sems[0].at[n]) for n, (i, h) in enumerate(zip(ins, held))]
    leave = [pltpu.make_async_copy(h, o, sems[1].at[n]) for n, (h, o) in enumerate(zip(held, outs))]
    for copy in come:
        copy.start()
    one[...] = gains[0:1]
    two[...] = gains[1:2]
    for before, after in zip(come, leave):
        before.wait()
        after.start()
    for copy in leave:
        copy.wait()


def deliver(parts):
    *arrays, gains = parts
    shapes = [jax.ShapeDtypeStruct(a.shape, F32) for a in arrays] + [jax.ShapeDtypeStruct((1, 16), F32)] * 2
    return pl.pallas_call(
        deliver_kernel,
        name="deliver",
        out_shape=shapes,
        in_specs=[pl.BlockSpec(memory_space=pltpu.VMEM)] + [pl.BlockSpec(memory_space=pl.ANY)] * 9,
        out_specs=[pl.BlockSpec(memory_space=pl.ANY)] * 9 + [pl.BlockSpec(memory_space=pltpu.VMEM)] * 2,
        scratch_shapes=[pltpu.VMEM(a.shape, F32) for a in arrays] + [pltpu.SemaphoreType.DMA((9,))] * 2,
    )(gains, *arrays)


def per_device(
    tokens,
    norm_attn,
    w_query,
    w_key,
    w_value,
    w_out,
    norm_mlp,
    w_gate,
    w_up,
    w_down,
    segment_ids,
    cotangent,
):
    weights = (w_query, w_key, w_value, w_out, w_down, w_gate, w_up)
    kept = forward(tokens, norm_attn, norm_mlp, segment_ids, cotangent, *weights)
    (layer_out, grad_tokens, g_query, g_key, g_value, g_out, g_gate, g_up, g_down, gain1, gain2) = deliver(backward(
        kept, tokens, norm_attn, norm_mlp, cotangent, *weights))
    return (layer_out, grad_tokens, gain1.reshape(16), g_query, g_key, g_value, g_out.T, gain2.reshape(16), g_gate, g_up,
            g_down.T)


def solution(mesh):
    placed = (
        P(("dp", "tp"), None),
        P(),
        P(None, "tp"),
        P(None, "tp"),
        P(None, "tp"),
        P("tp", None),
        P(),
        P(None, "tp"),
        P(None, "tp"),
        P("tp", None),
        P(("dp", "tp")),
        P(("dp", "tp"), None),
    )
    return jax.shard_map(
        per_device,
        mesh=mesh,
        in_specs=placed,
        out_specs=(
            P(("dp", "tp"), None),
            P(("dp", "tp"), None),
            P(("dp", "tp")),
            P("dp", "tp"),
            P("dp", "tp"),
            P("dp", "tp"),
            P("tp", "dp"),
            P(("dp", "tp")),
            P("dp", "tp"),
            P("dp", "tp"),
            P("tp", "dp"),
        ),
        check_vma=False,
    )
```

```python
import math

import jax
import jax.numpy as jnp
import numpy as np
from jax import lax
from jax.experimental import pallas as pl
from jax.experimental.pallas import tpu as pltpu
from jax.sharding import PartitionSpec as P

HD = 64
BF = jnp.bfloat16
F32 = jnp.float32
MESH = pl.DeviceIdType.MESH


def place():
    dp = lax.axis_index("dp")
    tp = lax.axis_index("tp")
    return dp // 8, lax.rem(dp // 4, 2), lax.rem(dp, 4), tp


def ring(me, step):
    return lax.rem(me + step + 4, 4)


class Panel:
    def __init__(self, y_first, grad, near, second, far, last, from_x, send, recv, put):
        self.y_first = y_first
        self.grad, self.near, self.second, self.far = grad, near, second, far
        self.last, self.from_x = last, from_x
        self.send, self.recv = send, recv
        self.put = put
        y, xh, z, tp = place()
        self.xh = xh
        one, two = (y, z) if y_first else (z, y)
        steps = lambda me: (me, ring(me, 1), ring(me, 2), ring(me, -1))
        self.at = (None, steps(one), steps(two))
        self.devices = {}
        for step in (1, -1):
            along_y = (ring(y, step) * 8 + xh * 4 + z, tp)
            along_z = (y * 8 + xh * 4 + ring(z, step), tp)
            self.devices[1, step], self.devices[2, step] = (along_y, along_z) if y_first else (along_z, along_y)
        self.other = 1 - xh
        self.across = (y * 8 + self.other * 4 + z, tp)
        self.started = []

    def device(self, stage, step):
        return self.devices[stage, step]

    def part(self, stage, at, half):
        if stage == 1:
            return self.grad.at[at, half] if self.y_first else self.grad.at[:, half, at]
        return self.second.at[at, half]

    def landed(self, stage, k):
        return (self.near if stage == 1 else self.far).at[k]

    def copy(self, stage, k, at, half, step):
        sem = k + (6 if stage == 2 else 0)
        return pltpu.make_async_remote_copy(
            src_ref=self.part(stage, at, half),
            dst_ref=self.landed(stage, k),
            send_sem=self.send.at[sem],
            recv_sem=self.recv.at[sem],
            device_id=self.device(stage, step),
            device_id_type=MESH,
        )

    def go(self, stage, k, at, half, step):
        what = (stage, k, at, half, step)
        self.copy(*what).start()
        self.started.append(what)

    def arrived(self, stage, k):
        self.copy(stage, k, self.at[stage][0], 0, 1).wait_recv()

    def begin(self, stage):
        me, right, over, left = self.at[stage]
        self.go(stage, 0, over, 0, 1)
        self.go(stage, 1, over, 1, -1)
        self.go(stage, 2, right, 1, 1)
        self.go(stage, 3, left, 0, -1)

    def add(self, into, what):
        if len(into.shape) == 3:
            @pl.loop(0, into.shape[0])
            def _(i):
                into[i] = (into[i].astype(F32) + what[i].astype(F32)).astype(BF)
        else:
            into[...] = (into[...].astype(F32) + what[...].astype(F32)).astype(BF)

    def middle(self, stage):
        me, right, over, left = self.at[stage]
        for k, at, half, step in ((0, right, 0, 1), (1, left, 1, -1)):
            self.arrived(stage, k)
            self.add(self.part(stage, at, half), self.landed(stage, k))
            self.go(stage, k + 4, at, half, step)

    def end(self, stage):
        me = self.at[stage][0]
        for half, (a, b) in enumerate(((4, 3), (2, 5))):
            self.arrived(stage, a)
            self.arrived(stage, b)
            own, one, two = self.part(stage, me, half), self.landed(stage, a), self.landed(stage, b)
            if stage == 1:
                @pl.loop(0, 4)
                def _(q):
                    total = own[q].astype(F32) + one[q].astype(F32) + two[q].astype(F32)
                    self.second[q, half] = total.astype(BF)
            else:
                total = own[...].astype(F32) + one[...].astype(F32) + two[...].astype(F32)
                self.last[half] = total.astype(BF)

    def crossing(self):
        return pltpu.make_async_remote_copy(
            src_ref=self.last.at[self.other],
            dst_ref=self.from_x,
            send_sem=self.send.at[12],
            recv_sem=self.recv.at[12],
            device_id=self.across,
            device_id_type=MESH,
        )

    def cross(self):
        self.crossing().start()

    def finish(self):
        self.crossing().wait_recv()
        self.put(self.last[self.xh].astype(F32) + self.from_x[...].astype(F32))

    def sent(self, count):
        for what in self.started[:count]:
            self.copy(*what).wait_send()
        self.started = self.started[count:]

    def drain(self):
        self.sent(len(self.started))
        self.crossing().wait_send()


def dot(a, b):
    return jnp.dot(a, b, preferred_element_type=F32)


def dot_nt(a, b):
    return lax.dot_general(a, b, (((1,), (1,)), ((), ())), preferred_element_type=F32)


def dot_tn(a, b):
    return lax.dot_general(a, b, (((0,), (0,)), ((), ())), preferred_element_type=F32)


class Peers:
    def __init__(self):
        self.dp = lax.axis_index("dp")
        self.me = lax.axis_index("tp")
        self.core = self.me + 1 - 2 * lax.rem(self.me, 2)
        self.next = lax.rem(self.me + 2, 4)
        self.far = lax.rem(self.core + 2, 4)
        self.chip = self.me // 2
        self.to_core = (self.dp, self.core)
        self.to_next = (self.dp, self.next)
        self.to_far = (self.dp, self.far)


class Gather:
    def __init__(self, peers, buf, send, recv, parts):
        self.p, self.buf, self.send, self.recv, self.parts = peers, buf, send, recv, parts
        self.rows = buf.shape[1] // parts
        self.started = []

    def copy(self, kind, owner, i, device):
        at = self.buf.at[owner, pl.ds(i * self.rows, self.rows)]
        sem = kind * self.parts + i
        return pltpu.make_async_remote_copy(
            src_ref=at, dst_ref=at, send_sem=self.send.at[sem], recv_sem=self.recv.at[sem],
            device_id=device, device_id_type=MESH)

    def go(self, *what):
        self.copy(*what).start()
        self.started.append(what)

    def start(self, i):
        self.go(1, self.p.me, i, self.p.to_next)
        self.go(0, self.p.me, i, self.p.to_core)

    def near(self):
        for i in range(self.parts):
            self.copy(0, self.p.core, i, self.p.to_core).wait_recv()

    def forward(self, i):
        self.copy(1, self.p.next, i, self.p.to_next).wait_recv()
        self.go(2, self.p.next, i, self.p.to_core)

    def rest(self, i):
        self.copy(2, self.p.far, i, self.p.to_core).wait_recv()

    def drain(self):
        for what in self.started:
            self.copy(*what).wait_send()
        self.started = []


class Scatter:
    def __init__(self, peers, part, r0, r1, r2, send, recv, parts):
        self.p, self.part, self.r = peers, part, (r0, r1, r2)
        self.send, self.recv, self.parts = send, recv, parts
        self.rows = part.shape[1] // parts
        self.started = []

    def rowsof(self, i):
        return pl.ds(i * self.rows, self.rows)

    def copy(self, kind, owner, i, device):
        sem = kind * self.parts + i
        return pltpu.make_async_remote_copy(
            src_ref=self.part.at[owner, self.rowsof(i)], dst_ref=self.r[kind].at[self.rowsof(i)],
            send_sem=self.send.at[sem], recv_sem=self.recv.at[sem],
            device_id=device, device_id_type=MESH)

    def go(self, *what):
        self.copy(*what).start()
        self.started.append(what)

    def cross(self, i):
        self.go(0, self.p.far, i, self.p.to_core)

    def own(self, i):
        self.go(1, self.p.core, i, self.p.to_core)

    def combine(self, i):
        self.copy(0, self.p.far, i, self.p.to_core).wait_recv()
        at = self.part.at[self.p.next, self.rowsof(i)]
        at[...] = (at[...].astype(F32) + self.r[0][self.rowsof(i)].astype(F32)).astype(BF)
        self.go(2, self.p.next, i, self.p.to_next)

    def total(self, i):
        self.copy(1, self.p.core, i, self.p.to_core).wait_recv()
        self.copy(2, self.p.next, i, self.p.to_next).wait_recv()
        rows = self.rowsof(i)
        return (self.part[self.p.me, rows].astype(F32) + self.r[1][rows].astype(F32)
                + self.r[2][rows].astype(F32))

    def drain(self):
        for what in self.started:
            self.copy(*what).wait_send()
        self.started = []


class Around:
    def __init__(self, peers, buf, out, send, recv):
        self.p, self.buf, self.out, self.send, self.recv = peers, buf, out, send, recv
        y, xh, z, tp = place()
        self.to = [(ring(y, step) * 8 + xh * 4 + z, tp) for step in (1, -1, 2)]
        self.owners = (peers.me, peers.next)
        self.given = (peers.core, peers.far)
        self.started = []

    def copy(self, kind, which, slot):
        sem = 6 * kind + 3 * which + slot
        owner = self.owners[which] if kind < 2 else self.given[which]
        at = self.out.at[slot, owner]
        sem = sem if kind < 2 else sem - 6
        return pltpu.make_async_remote_copy(
            src_ref=self.buf.at[owner] if kind == 0 else at, dst_ref=at,
            send_sem=self.send.at[sem], recv_sem=self.recv.at[sem],
            device_id=self.p.to_core if kind else self.to[slot], device_id_type=MESH)

    def go(self, *what):
        self.copy(*what).start()
        self.started.append(what)

    def spread(self, which):
        for slot in range(3):
            self.go(0, which, slot)

    def hand(self, which, slot):
        self.copy(0, which, slot).wait_recv()
        self.go(1, which, slot)

    def rest(self, which):
        for slot in range(3):
            self.copy(2, which, slot).wait_recv()

    def drain(self):
        for what in self.started:
            self.copy(*what).wait_send()


def rope_tables():
    inverse = np.exp(np.arange(32, dtype=np.float64) * (-2.0 * math.log(10000.0) / 64))
    angles = np.arange(512, dtype=np.float64)[:, None] * np.tile(inverse, 4)[None, :]
    return (np.cos(angles).astype(np.float32), np.sin(angles).astype(np.float32),
            np.tile(inverse, 4)[None, :].astype(np.float32))


def lanes(shape):
    return lax.broadcasted_iota(jnp.int32, shape, len(shape) - 1)


def turned(values):
    low = lax.rem(lanes(values.shape), 64) < 32
    return jnp.where(low, pltpu.roll(values, 96, 1), pltpu.roll(values, 32, 1))


def split_heads(pair):
    left = lanes(pair.shape) < 64
    zero = jnp.zeros_like(pair)
    return jnp.concatenate([jnp.where(left, pair, zero), jnp.where(left, zero, pair)], axis=0)


BLOCKS = ((0, 256, 256), (256, 256, 512))
FF_TILES = ((0, 512), (512, 512), (1024, 384))


def mask_bias(bias, first, start, rows, keys):
    row = lax.broadcasted_iota(jnp.int32, (rows, keys), 0) + start
    key = lax.broadcasted_iota(jnp.int32, (rows, keys), 1)
    allowed = (key <= row) & ((row < first) == (key < first))
    bias[...] = jnp.where(allowed, 0.0, -1e9).astype(F32)


def inverse_rms(rows):
    return lax.rsqrt(jnp.mean(rows * rows, axis=1, keepdims=True) + 1e-5)


def chip_rows(buf, chip):
    return buf[pl.ds(chip * 2, 2)].reshape(256, buf.shape[2])


def forward_kernel(x, gain1, gain2, cos0, sin0, inv, seg, dy_own, *refs):
    hbm_w, refs = refs[:7], refs[7:]
    outs, around_o, refs = refs[:15], refs[15], refs[16:]
    (a1_o, a2_o, dy_o, hid_o, dg_o, du_o, q_o, k_o, v_o, o_o, lse_o, x2_o, cos_o, sin_o, cnt_o) = outs
    (A1, A2, DY, Wq, Wkv, Wo, Wd, Wg, Wu, Q, K, V, O, LSE, PM, R0, R1, R2, DH, HID, DG, DU, X2, COS, SIN,
     CNT, B0, B1, wsem, osem, g1s, g1r, g2s, g2r, g3s, g3r, ss, sr, cs, cr, as_, ar) = refs
    weights = (Wq, Wkv.at[pl.ds(0, 64)], Wkv.at[pl.ds(64, 64)], Wo, Wd, Wg, Wu)
    loads = [pltpu.make_async_copy(h, w, wsem.at[i]) for i, (h, w) in enumerate(zip(hbm_w, weights))]
    p = Peers()
    barrier = pltpu.get_barrier_semaphore()
    around = Around(p, DY, around_o, as_, ar)
    for device in [p.to_core, p.to_next, p.to_far] + around.to:
        pl.semaphore_signal(barrier, inc=1, device_id=device, device_id_type=MESH)
    for load in loads:
        load.start()
    stored = []

    def keep(src, dst):
        copy = pltpu.make_async_copy(src, dst, osem.at[len(stored)])
        copy.start()
        stored.append(copy)

    stream = x[...].astype(F32)
    A1[p.me] = (stream * inverse_rms(stream) * gain1[...]).astype(BF)
    DY[p.me] = dy_own[...]
    CNT[p.me] = jnp.broadcast_to(jnp.sum(seg[...], axis=1, keepdims=True), (8, 128))
    pl.semaphore_wait(barrier, 6)
    first_in = Gather(p, A1, g1s, g1r, 2)
    for i in range(2):
        first_in.start(i)
    counts = [pltpu.make_async_remote_copy(
        src_ref=CNT.at[p.me], dst_ref=CNT.at[p.me], send_sem=cs.at[i], recv_sem=cr.at[i],
        device_id=device, device_id_type=MESH) for i, device in enumerate((p.to_core, p.to_next, p.to_far))]
    for copy in counts:
        copy.start()
    dy_in = Gather(p, DY, g2s, g2r, 2)
    for i in range(2):
        dy_in.start(i)
    around.spread(0)
    for i, owner in enumerate((p.core, p.next, p.far)):
        pltpu.make_async_remote_copy(
            src_ref=CNT.at[owner], dst_ref=CNT.at[owner], send_sem=cs.at[i], recv_sem=cr.at[i],
            device_id=p.to_core, device_id_type=MESH).wait_recv()
    ones = CNT[0] + CNT[1] + CNT[2] + CNT[3]
    first = 512 - ones[0:1, 0:1]
    angle = first.astype(F32) * inv[...]
    cos_n, sin_n = jnp.cos(angle), jnp.sin(angle)
    row = lax.broadcasted_iota(jnp.int32, (512, 128), 0)
    c0, s0 = cos0[...], sin0[...]
    COS[...] = jnp.where(row < first, c0, c0 * cos_n + s0 * sin_n)
    sine = jnp.where(row < first, s0, s0 * cos_n - c0 * sin_n)
    SIN[...] = jnp.where(lax.rem(lanes((512, 128)), 64) < 32, -sine, sine)
    for bias, block in zip((B0, B1), BLOCKS):
        mask_bias(bias, first, *block)
    keep(COS, cos_o)
    keep(SIN, sin_o)
    keep(CNT, cnt_o)

    def project(chip):
        rows = pl.ds(pl.multiple_of(chip * 256, 256), 256)
        a = chip_rows(A1, chip)
        cos, sin = COS[rows], SIN[rows]
        for j in range(2):
            q = dot(a, Wq[:, pl.ds(256 * j, 256)])
            for h in range(2):
                pair = q[:, 128 * h:128 * h + 128]
                Q[rows, pl.ds(256 * j + 128 * h, 128)] = (pair * cos + turned(pair) * sin).astype(BF)
        kv = dot_nt(a, Wkv[...])
        vk = pltpu.roll(kv, 64, 1)
        k_lane = lanes(kv.shape) < 64
        kk = jnp.where(k_lane, kv, vk)
        K[rows] = (kk * cos + turned(kk) * sin).astype(BF)
        V[rows] = jnp.where(k_lane, vk, kv).astype(BF)

    for load in loads[:3]:
        load.wait()
    first_in.near()
    project(p.chip)
    for i in range(2):
        first_in.forward(i)
    for i in range(2):
        first_in.rest(i)
    project(1 - p.chip)
    keep(A1, a1_o)
    keep(Q, q_o)
    keep(K, k_o)
    keep(V, v_o)

    zero = jnp.zeros((512, 128), BF)
    left = lanes((512, 128)) < 64
    for j in range(4):
        for bias, (start, rows, keys) in zip((B0, B1), BLOCKS):
            qs = split_heads(Q[pl.ds(start, rows), pl.ds(128 * j, 128)])
            s = dot_nt(qs, K[:keys]) * 0.125
            s = (s.reshape(2, rows, keys) + bias[...][None]).reshape(2 * rows, keys)
            top = jnp.max(s, axis=1, keepdims=True)
            e = jnp.exp(s - top)
            total = jnp.sum(e, axis=1, keepdims=True)
            lse = top + jnp.log(total)
            eb = (e / total).astype(BF)
            vl = jnp.where(left[:keys], V[:keys], zero[:keys])
            vr = jnp.where(left[:keys], zero[:keys], V[:keys])
            o = dot(eb[:rows], vl) + dot(eb[rows:], vr)
            O[pl.ds(start, rows), pl.ds(128 * j, 128)] = o.astype(BF)
            lane = lanes((rows, 128))
            old = LSE[pl.ds(start, rows)] if j else jnp.zeros((rows, 128), F32)
            LSE[pl.ds(start, rows)] = jnp.where(lane == 2 * j, lse[:rows], jnp.where(lane == 2 * j + 1, lse[rows:], old))
    keep(O, o_o)
    keep(LSE, lse_o)

    def spread(chip):
        rows = pl.ds(pl.multiple_of(chip * 256, 256), 256)
        for j in range(4):
            cols = pl.ds(512 * j, 512)
            PM[pl.ds(chip * 2, 2), :, cols] = dot(O[rows], Wo[:, cols]).astype(BF).reshape(2, 128, 512)

    loads[3].wait()
    scatter = Scatter(p, PM, R0, R1, R2, ss, sr, 2)
    spread(1 - p.chip)
    for i in range(2):
        scatter.cross(i)
    spread(p.chip)
    for i in range(2):
        scatter.own(i)
    for i in range(2):
        scatter.combine(i)
    loads[4].wait()
    dy_in.near()
    for i in range(2):
        dy_in.forward(i)
    around.spread(1)
    for i in range(2):
        dy_in.rest(i)
    keep(DY, dy_o)
    for slot in range(3):
        around.hand(0, slot)
    dy = DY[...].reshape(512, 2048)
    for start, width in FF_TILES:
        DH[:, pl.ds(start, width)] = dot_nt(dy, Wd[pl.ds(start, width)])
    second_in = Gather(p, A2, g3s, g3r, 2)
    for i in range(2):
        rows = scatter.rowsof(i)
        x2 = x[rows].astype(F32) + scatter.total(i)
        X2[rows] = x2
        A2[p.me, rows] = (x2 * inverse_rms(x2) * gain2[...]).astype(BF)
        second_in.start(i)
    keep(X2, x2_o)

    def mlp(chip):
        rows = pl.ds(pl.multiple_of(chip * 256, 256), 256)
        a = chip_rows(A2, chip)
        for start, width in FF_TILES:
            cols = pl.ds(start, width)
            g = dot(a, Wg[:, cols])
            u = dot(a, Wu[:, cols])
            dh = DH[rows, cols]
            sg = jax.nn.sigmoid(g)
            act = g * sg
            HID[rows, cols] = (act * u).astype(BF)
            DU[rows, cols] = (dh * act).astype(BF)
            DG[rows, cols] = (dh * u * (sg + act * (1.0 - sg))).astype(BF)

    loads[5].wait()
    loads[6].wait()
    second_in.near()
    mlp(p.chip)
    for i in range(2):
        second_in.forward(i)
    for i in range(2):
        second_in.rest(i)
    keep(A2, a2_o)
    for slot in range(2):
        around.hand(1, slot)
    mlp(1 - p.chip)
    around.hand(1, 2)
    keep(HID, hid_o)
    keep(DG, dg_o)
    keep(DU, du_o)
    around.rest(0)
    around.rest(1)
    for copy in stored:
        copy.wait()
    for copy in counts:
        copy.wait_send()
    for what in (first_in, dy_in, second_in, scatter, around):
        what.drain()


def forward(tokens, norm_attn, norm_mlp, segment_ids, cotangent, w_query, w_key, w_value, w_out, w_down, w_gate, w_up):
    cos0, sin0, inv = rope_tables()
    rows4 = (4, 128, 2048)
    spec = lambda shape, kind: jax.ShapeDtypeStruct(shape, kind)
    outs = [spec(rows4, BF)] * 3 + [spec((512, 1408), BF)] * 3 + [
        spec((512, 512), BF), spec((512, 128), BF), spec((512, 128), BF), spec((512, 512), BF),
        spec((512, 128), F32), spec((128, 2048), F32), spec((512, 128), F32), spec((512, 128), F32),
        spec((4, 8, 128), jnp.int32), spec((3, 4, 128, 2048), BF)]
    vm = pltpu.VMEM
    dma = pltpu.SemaphoreType.DMA
    scratch = [vm(rows4, BF)] * 3 + [
        vm((2048, 512), BF), vm((128, 2048), BF), vm((512, 2048), BF), vm((1408, 2048), BF),
        vm((2048, 1408), BF), vm((2048, 1408), BF),
        vm((512, 512), BF), vm((512, 128), BF), vm((512, 128), BF), vm((512, 512), BF), vm((512, 128), F32),
        vm(rows4, BF), vm((128, 2048), BF), vm((128, 2048), BF), vm((128, 2048), BF), vm((512, 1408), F32),
        vm((512, 1408), BF), vm((512, 1408), BF), vm((512, 1408), BF), vm((128, 2048), F32),
        vm((512, 128), F32), vm((512, 128), F32), vm((4, 8, 128), jnp.int32), vm((256, 256), F32), vm((256, 512), F32),
        dma((7,)), dma((15,))] + [dma((6,))] * 8 + [dma((3,))] * 2 + [dma((12,))] * 2
    return pl.pallas_call(
        forward_kernel,
        name="forward",
        out_shape=outs,
        in_specs=[pl.BlockSpec(memory_space=pltpu.VMEM)] * 8 + [pl.BlockSpec(memory_space=pl.ANY)] * 7,
        out_specs=[pl.BlockSpec(memory_space=pl.ANY)] * 16,
        scratch_shapes=scratch,
        compiler_params=pltpu.CompilerParams(
            collective_id=2, has_side_effects=True, vmem_limit_bytes=62 * 2**20
        ),
    )(tokens, norm_attn.reshape(1, 2048), norm_mlp.reshape(1, 2048), cos0, sin0, inv, segment_ids.reshape(1, 128),
      cotangent, w_query, w_key.T, w_value.T, w_out, w_down, w_gate, w_up)


PANELS = {
    "gz": (768, False, "gz", 0), "gy": (640, True, "gy", 0), "dy": (256, True, "dy", 0), "dz": (128, False, "dz", 0),
    "uy": (768, True, "uy", 0), "uz": (640, False, "uz", 0), "oz": (384, False, "gz", 0), "oy": (128, True, "gy", 384),
    "ay": (384, True, "gy", 0), "az": (256, False, "gz", 384),
}
SETS = {"gz": 768, "gy": 640, "dy": 256, "dz": 128, "uy": 768, "uz": 640}
WIDE = 256


def grad_panel(grad, left, right, width, start):
    @pl.loop(0, 4)
    def _(at):
        rows = left[:, pl.ds(pl.multiple_of(at * 512, 512), 512)]
        cols = pl.ds(start, width)
        grad[at] = dot_tn(rows, right[:, cols]).astype(BF).reshape(2, 4, 64, width)


def grad_begin(panel, left, right, width, start):
    me, after, over, before = panel.at[1]
    for at, sends in ((over, ((0, over, 0, 1), (1, over, 1, -1))), (after, ((2, after, 1, 1),)),
                      (before, ((3, before, 0, -1),)), (me, ())):
        rows = left[:, pl.ds(pl.multiple_of(at * 512, 512), 512)]
        cols = pl.ds(start, width)
        panel.grad[at] = dot_tn(rows, right[:, cols]).astype(BF).reshape(2, 4, 64, width)
        for what in sends:
            panel.go(1, *what)


def norm_back(dn, rows, gain):
    r = inverse_rms(rows)
    e = dn * gain
    back = r * e - rows * (r * r * r) * jnp.mean(e * rows, axis=1, keepdims=True)
    return back, jnp.sum(dn * rows * r, axis=0, keepdims=True)


def backward_kernel(gain1, gain2, cnt, *refs):
    (a1_h, a2_h, dy_h, hid_h, dg_h, du_h, q_h, k_h, v_h, o_h, lse_h, x2_h, cos_h, sin_h, around_h,
     x_h, wq_h, wk_h, wv_h, wo_h, wd_h, wg_h, wu_h) = refs[:23]
    (lo_o, gt_o, gq_o, gk_o, gv_o, go_o, gg_o, gu_o, gd_o, gains_o) = refs[23:33]
    refs = refs[33:]
    sets, refs = {name: refs[2 * i:2 * i + 2] for i, name in enumerate(SETS)}, refs[2 * len(SETS):]
    slots, refs = {name: refs[6 * i:6 * i + 6] for i, name in enumerate(PANELS)}, refs[6 * len(PANELS):]
    (TG, TN, TS, TX, TT, TF, HS, t_send, t_recv,
     X0, X1, X3, DX2F, Ra0, Ra1, Ra2, Rb0, Rb1, Rb2, GA, GO,
     lsem, s2s, s2r, sls, slr, s1s, s1r, g4s, g4r, gs, gr, credit) = refs
    y, xh, z, tp = place()
    p = Peers()
    peers = [
        (ring(y, 1) * 8 + xh * 4 + z, tp), (ring(y, -1) * 8 + xh * 4 + z, tp),
        (y * 8 + xh * 4 + ring(z, 1), tp), (y * 8 + xh * 4 + ring(z, -1), tp),
        (ring(y, 2) * 8 + xh * 4 + z, tp), (y * 8 + xh * 4 + ring(z, 2), tp),
        (y * 8 + (1 - xh) * 4 + z, tp), p.to_core, p.to_next, p.to_far]
    barrier = pltpu.get_barrier_semaphore()
    for device in peers:
        pl.semaphore_signal(barrier, inc=1, device_id=device, device_id_type=MESH)

    n_loads = [0]

    def load(src, dst):
        copy = pltpu.make_async_copy(src, dst, lsem.at[n_loads[0]])
        n_loads[0] += 1
        copy.start()
        return copy

    def put_cols(ref, start, width):
        def put(v):
            ref[:, pl.ds(start, width)] = v
        return put

    def put_az(v):
        gq_o[:, 384:] = v[:, :128]
        gk_o[...] = v[:, 128:192]
        gv_o[...] = v[:, 192:]

    puts = {"gz": put_cols(gg_o, 640, 768), "gy": put_cols(gg_o, 0, 640), "dy": put_cols(gd_o, 1024, 256),
            "dz": put_cols(gd_o, 1280, 128), "uy": put_cols(gu_o, 0, 768), "uz": put_cols(gu_o, 768, 640),
            "oz": put_cols(go_o, 0, 384), "oy": put_cols(go_o, 384, 128), "ay": put_cols(gq_o, 0, 384), "az": put_az}
    panels = {}
    for name, (width, y_first, at, start) in PANELS.items():
        grad, near = sets[at]
        if SETS[at] != width:
            cols = pl.ds(start, width)
            grad, near = grad.at[:, :, :, :, cols], near.at[:, :, :, cols]
        panels[name] = Panel(y_first, grad, near, *slots[name], puts[name])
    wide = Panel(False, TG, TN, TS, None, None, None, t_send, t_recv, None)
    reused = {"gz": 0, "gy": 1}

    def middle(name, stage):
        panels[name].middle(stage)

    def second(name):
        panel = panels[name]
        panel.end(1)
        if name in reused:
            for step in (1, -1):
                pl.semaphore_signal(credit.at[reused[name]], inc=1, device_id=panel.device(1, step), device_id_type=MESH)
        panel.begin(2)

    def cross(name):
        panels[name].end(2)
        panels[name].cross()

    def finish(name):
        panels[name].finish()

    def reuse(name):
        panels[name].sent(6)
        pl.semaphore_wait(credit.at[reused[name]], 2)

    along_y = ((peers[0], ring(y, 1), ring(y, -1)), (peers[1], ring(y, -1), ring(y, 1)), (peers[4], ring(y, 2), ring(y, 2)))

    def part_cols(at):
        return pl.ds(pl.multiple_of(at * WIDE, WIDE), WIDE)

    def wide_copy(kind, slot, HID=None):
        device, to, _ = along_y[slot]
        if kind == 0:
            src, dst = HS.at[slot] if HID is None else HID.at[:, part_cols(to)], HS.at[slot]
        else:
            src, dst = TT.at[to], TF.at[slot]
        sem = 6 + 3 * kind + slot
        return pltpu.make_async_remote_copy(
            src_ref=src, dst_ref=dst, send_sem=t_send.at[sem], recv_sem=t_recv.at[sem],
            device_id=device, device_id_type=MESH)

    def wide_crossing():
        return pltpu.make_async_remote_copy(
            src_ref=TS.at[:, wide.other], dst_ref=TX, send_sem=t_send.at[12], recv_sem=t_recv.at[12],
            device_id=wide.across, device_id_type=MESH)

    def wide_cross():
        wide.end(1)
        wide_crossing().start()

    def wide_spread():
        wide_crossing().wait_recv()

        @pl.loop(0, 4)
        def _(q):
            TT[q] = (TS[q, xh].astype(F32) + TX[q].astype(F32)).astype(BF)

        gd_o[:, part_cols(y)] = TS[y, xh].astype(F32) + TX[y].astype(F32)
        for slot in range(3):
            wide_copy(1, slot).start()

    def wide_finish():
        for slot in range(3):
            wide_copy(1, slot).wait_recv()
            gd_o[:, part_cols(along_y[slot][2])] = TF[slot].astype(F32)

    stages = ((peers[0], peers[1], peers[4]), (peers[2], peers[3], peers[5]), (peers[6],), (p.to_core, p.to_next, p.to_far))

    def add_gain(row, gain):
        for i in range(4):
            GA[0, 0, row + i:row + i + 1] += gain[:, 512 * i:512 * i + 512]

    def gain_copy(stage, i):
        sem = 3 * stage + i
        return pltpu.make_async_remote_copy(
            src_ref=GA.at[stage, 0], dst_ref=GA.at[stage, i + 1], send_sem=gs.at[sem], recv_sem=gr.at[sem],
            device_id=stages[stage][i], device_id_type=MESH)

    def gain_send(stage):
        for i in range(len(stages[stage])):
            gain_copy(stage, i).start()

    def gain_sum(stage):
        total = GA[stage, 0]
        for i in range(len(stages[stage])):
            gain_copy(stage, i).wait_recv()
            total = total + GA[stage, i + 1]
        return total

    def gain_next(stage):
        GA[stage + 1, 0] = gain_sum(stage)
        gain_send(stage + 1)

    scatter2 = Scatter(p, X0, Ra0, Ra1, Ra2, s2s, s2r, 2)
    scatter_out = Scatter(p, X3, Rb0, Rb1, Rb2, sls, slr, 2)
    scatter1 = Scatter(p, X0, Ra0, Ra1, Ra2, s1s, s1r, 2)
    gather = Gather(p, DX2F, g4s, g4r, 2)

    def early(DY, HID, DG, DU, WG, WU, WD, ST, wsem):
        l_hid, l_a2, l_dg = load(hid_h, HID), load(a2_h, X1), load(dg_h, DG)
        l_dy, l_du = load(dy_h, DY), load(du_h, DU)

        def around_chunk(i):
            return [pltpu.make_async_copy(around_h.at[:, :, pl.ds(256 * i, 256)], ST.at[i % 2], wsem.at[6 + i % 2])]

        def gate_chunk(i):
            at = pl.ds(256 * i, 256)
            return [pltpu.make_async_copy(wg_h.at[at], WG.at[i % 2], wsem.at[i % 2]),
                    pltpu.make_async_copy(wu_h.at[at], WU.at[i % 2], wsem.at[2 + i % 2])]

        def down_chunk(i):
            return [pltpu.make_async_copy(wd_h.at[:, pl.ds(256 * i, 256)], WD.at[i % 2], wsem.at[4 + i % 2])]

        for i in range(2):
            for copy in gate_chunk(i) + down_chunk(i):
                copy.start()
        for i in range(2):
            for copy in around_chunk(i):
                copy.start()
        l_x2 = load(x2_h, lo_o)
        l_hid.wait()
        GA[0, 0] = jnp.zeros((8, 512), F32)
        pl.semaphore_wait(barrier, len(peers))
        for slot in range(3):
            wide_copy(0, slot, HID).start()
        l_a2.wait()
        l_dg.wait()
        a2 = X1.reshape(512, 2048)
        grad_panel(panels["gz"].grad, a2, DG, 768, 640)
        panels["gz"].begin(1)
        grad_begin(panels["gy"], a2, DG, 640, 0)
        l_dy.wait()
        grad_begin(panels["dy"], DY, HID, 256, 1024)
        grad_panel(panels["dz"].grad, DY, HID, 128, 1280)
        panels["dz"].begin(1)
        l_du.wait()
        for i in range(8):
            for copy in gate_chunk(i):
                copy.wait()
            da = dot_nt(DG[...], WG[i % 2]) + dot_nt(DU[...], WU[i % 2])
            X0[:, :, pl.ds(256 * i, 256)] = da.astype(BF).reshape(4, 128, 256)
            if i < 6:
                for copy in gate_chunk(i + 2):
                    copy.start()
        for i in range(2):
            scatter2.cross(i)
        for i in range(2):
            scatter2.own(i)
        middle("gz", 1)
        for slot in range(3):
            wide_copy(0, slot).wait_recv()
        own = HID[:, part_cols(y)]
        for i in range(8):
            for copy in around_chunk(i):
                copy.wait()
            total = dot_tn(DY[:, pl.ds(256 * i, 256)], own)
            for slot in range(3):
                total += dot_tn(ST[i % 2, slot], HS[slot])
            TG[i // 2, i % 2] = total.astype(BF).reshape(4, 64, WIDE)
            if i < 6:
                for copy in around_chunk(i + 2):
                    copy.start()
        wide.begin(1)
        scatter2.combine(0)
        middle("gy", 1)
        scatter2.combine(1)
        for i in range(8):
            for copy in down_chunk(i):
                copy.wait()
            X3[:, :, pl.ds(256 * i, 256)] = dot(HID[...], WD[i % 2]).astype(BF).reshape(4, 128, 256)
            if i < 6:
                for copy in down_chunk(i + 2):
                    copy.start()
        for i in range(2):
            scatter_out.cross(i)
        for i in range(2):
            scatter_out.own(i)
        middle("dz", 1)
        l_x2.wait()

        def middle_rows(i):
            rows = scatter2.rowsof(i)
            back, gain = norm_back(scatter2.total(i), lo_o[rows], gain2[...])
            add_gain(4, gain)
            dx2 = DY[pl.ds(pl.multiple_of(tp * 128 + i * 64, 64), 64)].astype(F32) + back
            gt_o[rows] = dx2
            DX2F[p.me, rows] = dx2.astype(BF)
            gather.start(i)

        middle_rows(0)
        middle("dy", 1)
        second("gz")
        middle_rows(1)
        for i in range(2):
            scatter_out.combine(i)
        wide.middle(1)
        grad_begin(panels["uy"], a2, DU, 768, 0)
        grad_panel(panels["uz"].grad, a2, DU, 640, 768)
        panels["uz"].begin(1)
        second("dz")
        second("gy")
        for slot in range(3):
            wide_copy(0, slot, HID).wait_send()

    def late(X, A1, Wo, Wq, Wkv, Q, O, DO, DQ, K, V, DKV, LSE, COS, SIN, B0, B1, DK, DV):
        l_wo, l_q, l_k, l_v, l_lse, l_cos, l_sin, l_o, l_a1, l_x, l_wq, l_wk, l_wv = [load(*w) for w in (
            (wo_h, Wo), (q_h, Q), (k_h, K), (v_h, V), (lse_h, LSE), (cos_h, COS), (sin_h, SIN), (o_h, O),
            (a1_h, A1), (x_h, X), (wq_h, Wq), (wk_h, Wkv.at[pl.ds(0, 64)]), (wv_h, Wkv.at[pl.ds(64, 64)]))]
        ones = cnt[0] + cnt[1] + cnt[2] + cnt[3]
        first = 512 - ones[0:1, 0:1]
        for bias, block in zip((B0, B1), BLOCKS):
            mask_bias(bias, first, *block)
        second("dy")
        wide_cross()
        gather.near()
        gather.forward(0)
        l_wo.wait()

        def back_out(chip):
            rows = pl.ds(pl.multiple_of(chip * 256, 256), 256)
            DO[rows] = dot_nt(chip_rows(DX2F, chip), Wo[...]).astype(BF)

        back_out(p.chip)
        gather.forward(1)
        middle("gz", 2)
        for i in range(2):
            gather.rest(i)
        back_out(1 - p.chip)
        for copy in (l_q, l_k, l_v, l_lse, l_cos, l_sin, l_o, l_a1):
            copy.wait()
        zero = jnp.zeros((512, 128), BF)
        left = lanes((512, 128)) < 64

        def heads(j):
            cols = pl.ds(128 * j, 128)
            for bias, (start, rows, keys) in zip((B0, B1), BLOCKS):
                at = pl.ds(start, rows)
                qs = split_heads(Q[at, cols])
                dos = split_heads(DO[at, cols])
                s = dot_nt(qs, K[:keys]) * 0.125
                s = (s.reshape(2, rows, keys) + bias[...][None]).reshape(2 * rows, keys)
                lse = jnp.concatenate([LSE[at, 2 * j:2 * j + 1], LSE[at, 2 * j + 1:2 * j + 2]], axis=0)
                prob = jnp.exp(s - lse)
                dp = dot_nt(dos, V[:keys])
                row_dot = jnp.sum(prob * dp, axis=1, keepdims=True)
                ds = (prob * (dp - row_dot) * 0.125).astype(BF)
                dv = dot_tn(prob.astype(BF), dos)
                dk = dot_tn(ds, qs)
                if j == 0 and keys == 512:
                    DV[256:] = dv[256:]
                    DK[256:] = dk[256:]
                    DV[:256] += dv[:256]
                    DK[:256] += dk[:256]
                elif j == 0:
                    DV[:keys] = dv
                    DK[:keys] = dk
                else:
                    DV[:keys] += dv
                    DK[:keys] += dk
                kl = jnp.where(left[:keys], K[:keys], zero[:keys])
                kr = jnp.where(left[:keys], zero[:keys], K[:keys])
                dq = dot(ds[:rows], kl) + dot(ds[rows:], kr)
                DQ[at, cols] = (dq * COS[at] - turned(dq) * SIN[at]).astype(BF)

        middle("uz", 1)
        reuse("gz")
        grad_panel(panels["oz"].grad, DX2F.reshape(512, 2048), O, 384, 0)
        panels["oz"].begin(1)
        reuse("gy")
        grad_begin(panels["oy"], DX2F.reshape(512, 2048), O, 128, 384)
        heads(0)
        heads(1)
        middle("uy", 1)
        heads(2)
        heads(3)
        dk = DK[...] + pltpu.roll(DK[...], 64, 1)
        dv = DV[...] + pltpu.roll(DV[...], 64, 1)
        DKV[...] = jnp.where(left, dk * COS[...] - turned(dk) * SIN[...], dv).astype(BF)
        l_wq.wait()
        l_wk.wait()
        l_wv.wait()
        scatter2.drain()
        for i in range(4):
            at = pl.ds(512 * i, 512)
            da = dot_nt(DQ[...], Wq[at]) + dot(DKV[...], Wkv[:, at])
            X0[:, :, at] = da.astype(BF).reshape(4, 128, 512)
        for i in range(2):
            scatter1.cross(i)
        for i in range(2):
            scatter1.own(i)
        grad_begin(panels["ay"], A1, DQ, 384, 0)
        for i in range(2):
            scatter1.combine(i)
        grad_z = panels["az"].grad
        grad_panel(grad_z.at[:, :, :, :, pl.ds(0, 128)], A1, DQ, 128, 384)
        grad_panel(grad_z.at[:, :, :, :, pl.ds(128, 128)], A1, DKV, 128, 0)
        panels["az"].begin(1)
        middle("dy", 2)
        middle("dz", 2)
        wide_spread()
        middle("gy", 2)
        cross("gz")
        for i in range(2):
            rows = scatter_out.rowsof(i)
            lo_o[rows] = lo_o[rows] + scatter_out.total(i)
        middle("oy", 1)
        second("uz")
        finish("gz")
        middle("oz", 1)
        l_x.wait()

        def first_rows(i):
            rows = scatter1.rowsof(i)
            back, gain = norm_back(scatter1.total(i), X[rows].astype(F32), gain1[...])
            add_gain(0, gain)
            gt_o[rows] = gt_o[rows] + back

        first_rows(0)
        second("uy")
        first_rows(1)
        gain_send(0)
        middle("az", 1)
        middle("ay", 1)

    vm, dma = pltpu.VMEM, pltpu.SemaphoreType.DMA
    pl.run_scoped(early, vm((512, 2048), BF), vm((512, 1408), BF), vm((512, 1408), BF), vm((512, 1408), BF),
                  vm((2, 256, 1408), BF), vm((2, 256, 1408), BF), vm((2, 1408, 256), BF), vm((2, 3, 512, 256), BF), dma((8,)))
    pl.run_scoped(late, vm((128, 2048), BF), vm((512, 2048), BF), vm((512, 2048), BF), vm((2048, 512), BF),
                  vm((128, 2048), BF), vm((512, 512), BF), vm((512, 512), BF), vm((512, 512), BF), vm((512, 512), BF),
                  vm((512, 128), BF), vm((512, 128), BF), vm((512, 128), BF), vm((512, 128), F32),
                  vm((512, 128), F32), vm((512, 128), F32), vm((256, 256), F32), vm((256, 512), F32),
                  vm((512, 128), F32), vm((512, 128), F32))
    cross("dy")
    gain_next(0)
    cross("gy")
    cross("dz")
    finish("dy")
    wide_finish()
    second("oy")
    gain_next(1)
    second("oz")
    finish("gy")
    middle("uz", 2)
    finish("dz")
    middle("uy", 2)
    gain_next(2)
    second("ay")
    second("az")
    middle("oy", 2)
    middle("oz", 2)
    GO[...] = pltpu.roll(gain_sum(3), lax.rem(512 - lax.rem(p.dp * 64 + tp * 16, 512), 512), 1)[:, :128]
    for i in range(2):
        gains_o[i:i + 1] = GO[pl.ds(4 * i + y, 1), :16]
    cross("uy")
    cross("uz")
    middle("ay", 2)
    middle("az", 2)
    cross("oy")
    cross("oz")
    finish("uy")
    cross("az")
    cross("ay")
    for name in ("uz", "oy", "oz", "az", "ay"):
        finish(name)
    for stage in range(4):
        for i in range(len(stages[stage])):
            gain_copy(stage, i).wait_send()
    for panel in panels.values():
        panel.drain()
    wide.sent(6)
    wide_crossing().wait_send()
    for slot in range(3):
        wide_copy(1, slot).wait_send()
    for what in (scatter_out, scatter1, gather):
        what.drain()


def backward(kept, tokens, norm_attn, norm_mlp, w_query, w_key, w_value, w_out, w_down, w_gate, w_up):
    (a1, a2, dy, hidden, d_gate, d_up, q, k, v, o, lse, x2, cos, sin, cnt, around) = kept
    vm, dma = pltpu.VMEM, pltpu.SemaphoreType.DMA
    scratch = []
    for w in SETS.values():
        scratch += [vm((4, 2, 4, 64, w), BF), vm((6, 4, 64, w), BF)]
    for w, *_ in PANELS.values():
        scratch += [vm((4, 2, 64, w), BF), vm((6, 64, w), BF), vm((2, 64, w), BF), vm((64, w), BF), dma((13,)), dma((13,))]
    scratch += [vm((4, 2, 4, 64, WIDE), BF), vm((6, 4, 64, WIDE), BF), vm((4, 2, 64, WIDE), BF), vm((4, 64, WIDE), BF),
                vm((4, 64, WIDE), BF), vm((3, 64, WIDE), BF), vm((3, 512, WIDE), BF), dma((13,)), dma((13,))]
    scratch += [vm((4, 128, 2048), BF)] * 4 + [vm((128, 2048), BF)] * 6
    scratch += [vm((4, 4, 8, 512), F32), vm((8, 128), F32)]
    scratch += [dma((23,))] + [dma((6,))] * 8 + [dma((12,))] * 2 + [pltpu.SemaphoreType.REGULAR((2,))]
    shapes = ((128, 2048), (128, 2048), (64, 512), (64, 64), (64, 64), (64, 512), (64, 1408), (64, 1408), (64, 1408),
              (2, 16))
    return pl.pallas_call(
        backward_kernel,
        name="backward",
        out_shape=[jax.ShapeDtypeStruct(shape, F32) for shape in shapes],
        in_specs=[pl.BlockSpec(memory_space=pltpu.VMEM)] * 3 + [pl.BlockSpec(memory_space=pl.ANY)] * 23,
        out_specs=[pl.BlockSpec(memory_space=pltpu.VMEM)] * 10,
        scratch_shapes=scratch,
        compiler_params=pltpu.CompilerParams(
            collective_id=3, has_side_effects=True, vmem_limit_bytes=63 * 2**20
        ),
    )(norm_attn.reshape(1, 2048), norm_mlp.reshape(1, 2048), cnt,
      a1.reshape(512, 2048), a2, dy.reshape(512, 2048), hidden, d_gate, d_up, q, k, v, o, lse, x2, cos, sin,
      around.reshape(3, 512, 2048), tokens, w_query, w_key.T, w_value.T, w_out, w_down, w_gate, w_up)


def deliver_kernel(gains, *refs):
    ins, outs, (one, two), held, sems = refs[:9], refs[9:18], refs[18:20], refs[20:29], refs[29:]
    come = [pltpu.make_async_copy(i, h, sems[0].at[n]) for n, (i, h) in enumerate(zip(ins, held))]
    leave = [pltpu.make_async_copy(h, o, sems[1].at[n]) for n, (h, o) in enumerate(zip(held, outs))]
    for copy in come:
        copy.start()
    one[...] = gains[0:1]
    two[...] = gains[1:2]
    for before, after in zip(come, leave):
        before.wait()
        after.start()
    for copy in leave:
        copy.wait()


def deliver(parts):
    *arrays, gains = parts
    shapes = [jax.ShapeDtypeStruct(a.shape, F32) for a in arrays] + [jax.ShapeDtypeStruct((1, 16), F32)] * 2
    return pl.pallas_call(
        deliver_kernel,
        name="deliver",
        out_shape=shapes,
        in_specs=[pl.BlockSpec(memory_space=pltpu.VMEM)] + [pl.BlockSpec(memory_space=pl.ANY)] * 9,
        out_specs=[pl.BlockSpec(memory_space=pl.ANY)] * 9 + [pl.BlockSpec(memory_space=pltpu.VMEM)] * 2,
        scratch_shapes=[pltpu.VMEM(a.shape, F32) for a in arrays] + [pltpu.SemaphoreType.DMA((9,))] * 2,
    )(gains, *arrays)


def per_device(
    tokens,
    norm_attn,
    w_query,
    w_key,
    w_value,
    w_out,
    norm_mlp,
    w_gate,
    w_up,
    w_down,
    segment_ids,
    cotangent,
):
    weights = (w_query, w_key, w_value, w_out, w_down, w_gate, w_up)
    kept = forward(tokens, norm_attn, norm_mlp, segment_ids, cotangent, *weights)
    (layer_out, grad_tokens, g_query, g_key, g_value, g_out, g_gate, g_up, g_down, gain1, gain2) = deliver(backward(
        kept, tokens, norm_attn, norm_mlp, *weights))
    return (layer_out, grad_tokens, gain1.reshape(16), g_query, g_key, g_value, g_out.T, gain2.reshape(16), g_gate, g_up,
            g_down.T)


def solution(mesh):
    placed = (
        P(("dp", "tp"), None),
        P(),
        P(None, "tp"),
        P(None, "tp"),
        P(None, "tp"),
        P("tp", None),
        P(),
        P(None, "tp"),
        P(None, "tp"),
        P("tp", None),
        P(("dp", "tp")),
        P(("dp", "tp"), None),
    )
    return jax.shard_map(
        per_device,
        mesh=mesh,
        in_specs=placed,
        out_specs=(
            P(("dp", "tp"), None),
            P(("dp", "tp"), None),
            P(("dp", "tp")),
            P("dp", "tp"),
            P("dp", "tp"),
            P("dp", "tp"),
            P("tp", "dp"),
            P(("dp", "tp")),
            P("dp", "tp"),
            P("dp", "tp"),
            P("tp", "dp"),
        ),
        check_vma=False,
    )
```

```python
import functools
import math

import jax
import jax.numpy as jnp
import numpy as np
from jax import lax
from jax.experimental import pallas as pl
from jax.experimental.pallas import tpu as pltpu
from jax.sharding import PartitionSpec as P

HD = 64
BF = jnp.bfloat16
F32 = jnp.float32
MESH = pl.DeviceIdType.MESH


def place():
    dp = lax.axis_index("dp")
    tp = lax.axis_index("tp")
    return dp // 8, lax.rem(dp // 4, 2), lax.rem(dp, 4), tp


def ring(me, step):
    return lax.rem(me + step + 4, 4)


class Panel:
    def __init__(self, y_first, grad, near, second, far, last, from_x, send, recv, put, direct=False):
        self.y_first = y_first
        self.grad, self.near, self.second, self.far = grad, near, second, far
        self.last, self.from_x = last, from_x
        self.send, self.recv = send, recv
        self.put = put
        self.direct = direct
        y, xh, z, tp = place()
        self.xh = xh
        one, two = (y, z) if y_first else (z, y)
        steps = lambda me: (me, ring(me, 1), ring(me, 2), ring(me, -1))
        self.at = (None, steps(one), steps(two))
        self.devices = {}
        for step in (1, -1, 2):
            along_y = (ring(y, step) * 8 + xh * 4 + z, tp)
            along_z = (y * 8 + xh * 4 + ring(z, step), tp)
            self.devices[1, step], self.devices[2, step] = (along_y, along_z) if y_first else (along_z, along_y)
        self.other = 1 - xh
        self.across = (y * 8 + self.other * 4 + z, tp)
        self.started = []

    def device(self, stage, step):
        return self.devices[stage, step]

    def part(self, stage, at, half):
        if half is None:
            return self.second.at[at]
        if stage == 1:
            return self.grad.at[at, half] if self.y_first else self.grad.at[:, half, at]
        return self.second.at[at, half]

    def landed(self, stage, k):
        return (self.near if stage == 1 else self.far).at[k]

    def copy(self, stage, k, at, half, step):
        sem = k + (6 if stage == 2 else 0)
        return pltpu.make_async_remote_copy(
            src_ref=self.part(stage, at, half),
            dst_ref=self.landed(stage, k),
            send_sem=self.send.at[sem],
            recv_sem=self.recv.at[sem],
            device_id=self.device(stage, step),
            device_id_type=MESH,
        )

    def go(self, stage, k, at, half, step):
        what = (stage, k, at, half, step)
        self.copy(*what).start()
        self.started.append(what)

    def arrived(self, stage, k):
        half = None if stage == 2 and self.direct else 0
        self.copy(stage, k, self.at[stage][0], half, 1).wait_recv()

    def begin(self, stage):
        me, right, over, left = self.at[stage]
        if stage == 2 and self.direct:
            for k, (at, step) in enumerate(((right, 1), (left, -1), (over, 2))):
                self.go(2, k, at, None, step)
            return
        self.go(stage, 0, over, 0, 1)
        self.go(stage, 1, over, 1, -1)
        self.go(stage, 2, right, 1, 1)
        self.go(stage, 3, left, 0, -1)

    def add(self, into, what):
        if len(into.shape) == 3:
            @pl.loop(0, into.shape[0])
            def _(i):
                into[i] = (into[i].astype(F32) + what[i].astype(F32)).astype(BF)
        else:
            into[...] = (into[...].astype(F32) + what[...].astype(F32)).astype(BF)

    def middle(self, stage):
        me, right, over, left = self.at[stage]
        for k, at, half, step in ((0, right, 0, 1), (1, left, 1, -1)):
            self.arrived(stage, k)
            self.add(self.part(stage, at, half), self.landed(stage, k))
            self.go(stage, k + 4, at, half, step)

    def end(self, stage):
        me = self.at[stage][0]
        if stage == 2 and self.direct:
            for k in range(3):
                self.arrived(2, k)
            total = self.second[me].astype(F32)
            for k in range(3):
                total += self.far[k].astype(F32)
            self.last[...] = total.astype(BF)
            return
        for half, (a, b) in enumerate(((4, 3), (2, 5))):
            self.arrived(stage, a)
            self.arrived(stage, b)
            own, one, two = self.part(stage, me, half), self.landed(stage, a), self.landed(stage, b)
            if stage == 1:
                @pl.loop(0, 4)
                def _(q):
                    total = own[q].astype(F32) + one[q].astype(F32) + two[q].astype(F32)
                    self.second[q, half] = total.astype(BF)
            else:
                total = own[...].astype(F32) + one[...].astype(F32) + two[...].astype(F32)
                self.last[half] = total.astype(BF)

    def crossing(self):
        return pltpu.make_async_remote_copy(
            src_ref=self.last.at[self.other],
            dst_ref=self.from_x,
            send_sem=self.send.at[12],
            recv_sem=self.recv.at[12],
            device_id=self.across,
            device_id_type=MESH,
        )

    def cross(self):
        self.crossing().start()

    def finish(self):
        self.crossing().wait_recv()
        self.put(self.last[self.xh].astype(F32) + self.from_x[...].astype(F32))

    def sent(self, count):
        for what in self.started[:count]:
            self.copy(*what).wait_send()
        self.started = self.started[count:]

    def drain(self):
        self.sent(len(self.started))
        self.crossing().wait_send()


def dot(a, b):
    return jnp.dot(a, b, preferred_element_type=F32)


def dot_nt(a, b):
    return lax.dot_general(a, b, (((1,), (1,)), ((), ())), preferred_element_type=F32)


def dot_tn(a, b):
    return lax.dot_general(a, b, (((0,), (0,)), ((), ())), preferred_element_type=F32)


class Peers:
    def __init__(self):
        self.dp = lax.axis_index("dp")
        self.me = lax.axis_index("tp")
        self.core = self.me + 1 - 2 * lax.rem(self.me, 2)
        self.next = lax.rem(self.me + 2, 4)
        self.far = lax.rem(self.core + 2, 4)
        self.chip = self.me // 2
        self.to_core = (self.dp, self.core)
        self.to_next = (self.dp, self.next)
        self.to_far = (self.dp, self.far)


class Gather:
    def __init__(self, peers, buf, send, recv, parts):
        self.p, self.buf, self.send, self.recv, self.parts = peers, buf, send, recv, parts
        self.rows = buf.shape[1] // parts
        self.started = []

    def copy(self, kind, owner, i, device):
        at = self.buf.at[owner, pl.ds(i * self.rows, self.rows)]
        sem = kind * self.parts + i
        return pltpu.make_async_remote_copy(
            src_ref=at, dst_ref=at, send_sem=self.send.at[sem], recv_sem=self.recv.at[sem],
            device_id=device, device_id_type=MESH)

    def go(self, *what):
        self.copy(*what).start()
        self.started.append(what)

    def start(self, i):
        self.go(1, self.p.me, i, self.p.to_next)
        self.go(0, self.p.me, i, self.p.to_core)

    def near(self):
        for i in range(self.parts):
            self.copy(0, self.p.core, i, self.p.to_core).wait_recv()

    def forward(self, i):
        self.copy(1, self.p.next, i, self.p.to_next).wait_recv()
        self.go(2, self.p.next, i, self.p.to_core)

    def rest(self, i):
        self.copy(2, self.p.far, i, self.p.to_core).wait_recv()

    def drain(self):
        for what in self.started:
            self.copy(*what).wait_send()
        self.started = []


class Scatter:
    def __init__(self, peers, part, r0, r1, r2, send, recv, parts):
        self.p, self.part, self.r = peers, part, (r0, r1, r2)
        self.send, self.recv, self.parts = send, recv, parts
        self.rows = part.shape[1] // parts
        self.started = []

    def rowsof(self, i):
        return pl.ds(i * self.rows, self.rows)

    def copy(self, kind, owner, i, device):
        sem = kind * self.parts + i
        return pltpu.make_async_remote_copy(
            src_ref=self.part.at[owner, self.rowsof(i)], dst_ref=self.r[kind].at[self.rowsof(i)],
            send_sem=self.send.at[sem], recv_sem=self.recv.at[sem],
            device_id=device, device_id_type=MESH)

    def go(self, *what):
        self.copy(*what).start()
        self.started.append(what)

    def cross(self, i):
        self.go(0, self.p.far, i, self.p.to_core)

    def own(self, i):
        self.go(1, self.p.core, i, self.p.to_core)

    def combine(self, i):
        self.copy(0, self.p.far, i, self.p.to_core).wait_recv()
        at = self.part.at[self.p.next, self.rowsof(i)]
        at[...] = (at[...].astype(F32) + self.r[0][self.rowsof(i)].astype(F32)).astype(BF)
        self.go(2, self.p.next, i, self.p.to_next)

    def total(self, i):
        self.copy(1, self.p.core, i, self.p.to_core).wait_recv()
        self.copy(2, self.p.next, i, self.p.to_next).wait_recv()
        rows = self.rowsof(i)
        return (self.part[self.p.me, rows].astype(F32) + self.r[1][rows].astype(F32)
                + self.r[2][rows].astype(F32))

    def drain(self):
        for what in self.started:
            self.copy(*what).wait_send()
        self.started = []


class Around:
    def __init__(self, peers, buf, out, send, recv):
        self.p, self.buf, self.out, self.send, self.recv = peers, buf, out, send, recv
        y, xh, z, tp = place()
        self.to = [(ring(y, step) * 8 + xh * 4 + z, tp) for step in (1, -1, 2)]
        self.owners = (peers.me, peers.next)
        self.given = (peers.core, peers.far)
        self.started = []

    def copy(self, kind, which, slot):
        sem = 6 * kind + 3 * which + slot
        owner = self.owners[which] if kind < 2 else self.given[which]
        at = self.out.at[slot, owner]
        sem = sem if kind < 2 else sem - 6
        return pltpu.make_async_remote_copy(
            src_ref=self.buf.at[owner] if kind == 0 else at, dst_ref=at,
            send_sem=self.send.at[sem], recv_sem=self.recv.at[sem],
            device_id=self.p.to_core if kind else self.to[slot], device_id_type=MESH)

    def go(self, *what):
        self.copy(*what).start()
        self.started.append(what)

    def spread(self, which):
        for slot in range(3):
            self.go(0, which, slot)

    def hand(self, which, slot):
        self.copy(0, which, slot).wait_recv()
        self.go(1, which, slot)

    def rest(self, which):
        for slot in range(3):
            self.copy(2, which, slot).wait_recv()

    def drain(self):
        for what in self.started:
            self.copy(*what).wait_send()


def rope_tables():
    inverse = np.exp(np.arange(32, dtype=np.float64) * (-2.0 * math.log(10000.0) / 64))
    angles = np.arange(512, dtype=np.float64)[:, None] * np.tile(inverse, 4)[None, :]
    return (np.cos(angles).astype(np.float32), np.sin(angles).astype(np.float32),
            np.tile(inverse, 4)[None, :].astype(np.float32))


def lanes(shape):
    return lax.broadcasted_iota(jnp.int32, shape, len(shape) - 1)


def turned(values):
    low = lax.rem(lanes(values.shape), 64) < 32
    return jnp.where(low, pltpu.roll(values, 96, 1), pltpu.roll(values, 32, 1))


def split_heads(pair):
    left = lanes(pair.shape) < 64
    zero = jnp.zeros_like(pair)
    return jnp.concatenate([jnp.where(left, pair, zero), jnp.where(left, zero, pair)], axis=0)


BLOCKS = ((0, 256, 256), (256, 256, 512))
FF_TILES = ((0, 512), (512, 512), (1024, 384))


def mask_bias(bias, first, start, rows, keys):
    row = lax.broadcasted_iota(jnp.int32, (rows, keys), 0) + start
    key = lax.broadcasted_iota(jnp.int32, (rows, keys), 1)
    allowed = (key <= row) & ((row < first) == (key < first))
    bias[...] = jnp.where(allowed, 0.0, -1e9).astype(F32)


def inverse_rms(rows):
    return lax.rsqrt(jnp.mean(rows * rows, axis=1, keepdims=True) + 1e-5)


def chip_rows(buf, chip):
    return buf[pl.ds(chip * 2, 2)].reshape(256, buf.shape[2])


def forward_kernel(x, gain1, gain2, cos0, sin0, inv, seg, dy_own, *refs):
    hbm_w, refs = refs[:7], refs[7:]
    outs, around_o, refs = refs[:15], refs[15], refs[16:]
    (a1_o, a2_o, dy_o, hid_o, dg_o, du_o, q_o, k_o, v_o, o_o, lse_o, x2_o, cos_o, sin_o, cnt_o) = outs
    (A1, A2, DY, Wq, Wkv, Wo, Wd, Wg, Wu, Q, K, V, O, LSE, PM, R0, R1, R2, DH, HID, DG, DU, X2, COS, SIN,
     CNT, B0, B1, wsem, osem, g1s, g1r, g2s, g2r, g3s, g3r, ss, sr, cs, cr, as_, ar) = refs
    weights = (Wq, Wkv.at[pl.ds(0, 64)], Wkv.at[pl.ds(64, 64)], Wo, Wd, Wg, Wu)
    loads = [pltpu.make_async_copy(h, w, wsem.at[i]) for i, (h, w) in enumerate(zip(hbm_w, weights))]
    p = Peers()
    barrier = pltpu.get_barrier_semaphore()
    around = Around(p, DY, around_o, as_, ar)
    for device in [p.to_core, p.to_next, p.to_far] + around.to:
        pl.semaphore_signal(barrier, inc=1, device_id=device, device_id_type=MESH)
    for load in loads:
        load.start()
    stored = []

    def keep(src, dst):
        copy = pltpu.make_async_copy(src, dst, osem.at[len(stored)])
        copy.start()
        stored.append(copy)

    stream = x[...].astype(F32)
    A1[p.me] = (stream * inverse_rms(stream) * gain1[...]).astype(BF)
    DY[p.me] = dy_own[...]
    CNT[p.me] = jnp.broadcast_to(jnp.sum(seg[...], axis=1, keepdims=True), (8, 128))
    pl.semaphore_wait(barrier, 6)
    first_in = Gather(p, A1, g1s, g1r, 2)
    for i in range(2):
        first_in.start(i)
    counts = [pltpu.make_async_remote_copy(
        src_ref=CNT.at[p.me], dst_ref=CNT.at[p.me], send_sem=cs.at[i], recv_sem=cr.at[i],
        device_id=device, device_id_type=MESH) for i, device in enumerate((p.to_core, p.to_next, p.to_far))]
    for copy in counts:
        copy.start()
    dy_in = Gather(p, DY, g2s, g2r, 2)
    for i in range(2):
        dy_in.start(i)
    around.spread(0)
    for i, owner in enumerate((p.core, p.next, p.far)):
        pltpu.make_async_remote_copy(
            src_ref=CNT.at[owner], dst_ref=CNT.at[owner], send_sem=cs.at[i], recv_sem=cr.at[i],
            device_id=p.to_core, device_id_type=MESH).wait_recv()
    ones = CNT[0] + CNT[1] + CNT[2] + CNT[3]
    first = 512 - ones[0:1, 0:1]
    angle = first.astype(F32) * inv[...]
    cos_n, sin_n = jnp.cos(angle), jnp.sin(angle)
    row = lax.broadcasted_iota(jnp.int32, (512, 128), 0)
    c0, s0 = cos0[...], sin0[...]
    COS[...] = jnp.where(row < first, c0, c0 * cos_n + s0 * sin_n)
    sine = jnp.where(row < first, s0, s0 * cos_n - c0 * sin_n)
    SIN[...] = jnp.where(lax.rem(lanes((512, 128)), 64) < 32, -sine, sine)
    for bias, block in zip((B0, B1), BLOCKS):
        mask_bias(bias, first, *block)
    keep(COS, cos_o)
    keep(SIN, sin_o)
    keep(CNT, cnt_o)

    def project(chip):
        rows = pl.ds(pl.multiple_of(chip * 256, 256), 256)
        a = chip_rows(A1, chip)
        cos, sin = COS[rows], SIN[rows]
        for j in range(2):
            q = dot(a, Wq[:, pl.ds(256 * j, 256)])
            for h in range(2):
                pair = q[:, 128 * h:128 * h + 128]
                Q[rows, pl.ds(256 * j + 128 * h, 128)] = (pair * cos + turned(pair) * sin).astype(BF)
        kv = dot_nt(a, Wkv[...])
        vk = pltpu.roll(kv, 64, 1)
        k_lane = lanes(kv.shape) < 64
        kk = jnp.where(k_lane, kv, vk)
        K[rows] = (kk * cos + turned(kk) * sin).astype(BF)
        V[rows] = jnp.where(k_lane, vk, kv).astype(BF)

    for load in loads[:3]:
        load.wait()
    first_in.near()
    project(p.chip)
    for i in range(2):
        first_in.forward(i)
    for i in range(2):
        first_in.rest(i)
    project(1 - p.chip)
    keep(A1, a1_o)
    keep(Q, q_o)
    keep(K, k_o)
    keep(V, v_o)

    zero = jnp.zeros((512, 128), BF)
    left = lanes((512, 128)) < 64
    def attend(block, pairs):
        bias = (B0, B1)[block]
        start, rows, keys = BLOCKS[block]
        for j in pairs:
            qs = split_heads(Q[pl.ds(start, rows), pl.ds(128 * j, 128)])
            s = dot_nt(qs, K[:keys]) * 0.125
            s = (s.reshape(2, rows, keys) + bias[...][None]).reshape(2 * rows, keys)
            top = jnp.max(s, axis=1, keepdims=True)
            e = jnp.exp(s - top)
            total = jnp.sum(e, axis=1, keepdims=True)
            lse = top + jnp.log(total)
            eb = (e / total).astype(BF)
            vl = jnp.where(left[:keys], V[:keys], zero[:keys])
            vr = jnp.where(left[:keys], zero[:keys], V[:keys])
            o = dot(eb[:rows], vl) + dot(eb[rows:], vr)
            O[pl.ds(start, rows), pl.ds(128 * j, 128)] = o.astype(BF)
            lane = lanes((rows, 128))
            old = LSE[pl.ds(start, rows)] if j else jnp.zeros((rows, 128), F32)
            LSE[pl.ds(start, rows)] = jnp.where(lane == 2 * j, lse[:rows], jnp.where(lane == 2 * j + 1, lse[rows:], old))

    def attend_rows(other, pairs):
        for chip in range(2):
            @pl.when(p.chip == chip)
            def _():
                attend(1 - chip if other else chip, pairs)

    def spread(chip):
        rows = pl.ds(pl.multiple_of(chip * 256, 256), 256)
        for j in range(4):
            cols = pl.ds(512 * j, 512)
            PM[pl.ds(chip * 2, 2), :, cols] = dot(O[rows], Wo[:, cols]).astype(BF).reshape(2, 128, 512)

    scatter = Scatter(p, PM, R0, R1, R2, ss, sr, 2)
    attend_rows(True, range(4))
    loads[3].wait()
    spread(1 - p.chip)
    for i in range(2):
        scatter.cross(i)
    attend_rows(False, range(2))
    for i in range(2):
        scatter.combine(i)
    attend_rows(False, range(2, 4))
    keep(O, o_o)
    keep(LSE, lse_o)
    spread(p.chip)
    for i in range(2):
        scatter.own(i)
    loads[4].wait()
    dy_in.near()
    for i in range(2):
        dy_in.forward(i)
    around.spread(1)
    for i in range(2):
        dy_in.rest(i)
    keep(DY, dy_o)
    for slot in range(3):
        around.hand(0, slot)
    dy = DY[...].reshape(512, 2048)
    for start, width in FF_TILES:
        DH[:, pl.ds(start, width)] = dot_nt(dy, Wd[pl.ds(start, width)])
    second_in = Gather(p, A2, g3s, g3r, 2)
    for i in range(2):
        rows = scatter.rowsof(i)
        x2 = x[rows].astype(F32) + scatter.total(i)
        X2[rows] = x2
        A2[p.me, rows] = (x2 * inverse_rms(x2) * gain2[...]).astype(BF)
        second_in.start(i)
    keep(X2, x2_o)

    def mlp(chip):
        rows = pl.ds(pl.multiple_of(chip * 256, 256), 256)
        a = chip_rows(A2, chip)
        for start, width in FF_TILES:
            cols = pl.ds(start, width)
            g = dot(a, Wg[:, cols])
            u = dot(a, Wu[:, cols])
            dh = DH[rows, cols]
            sg = jax.nn.sigmoid(g)
            act = g * sg
            HID[rows, cols] = (act * u).astype(BF)
            DU[rows, cols] = (dh * act).astype(BF)
            DG[rows, cols] = (dh * u * (sg + act * (1.0 - sg))).astype(BF)

    loads[5].wait()
    loads[6].wait()
    second_in.near()
    mlp(p.chip)
    for i in range(2):
        second_in.forward(i)
    for i in range(2):
        second_in.rest(i)
    keep(A2, a2_o)
    for slot in range(2):
        around.hand(1, slot)
    mlp(1 - p.chip)
    around.hand(1, 2)
    keep(HID, hid_o)
    keep(DG, dg_o)
    keep(DU, du_o)
    around.rest(0)
    around.rest(1)
    for copy in stored:
        copy.wait()
    for copy in counts:
        copy.wait_send()
    for what in (first_in, dy_in, second_in, scatter, around):
        what.drain()


def forward(tokens, norm_attn, norm_mlp, segment_ids, cotangent, w_query, w_key, w_value, w_out, w_down, w_gate, w_up):
    cos0, sin0, inv = rope_tables()
    rows4 = (4, 128, 2048)
    spec = lambda shape, kind: jax.ShapeDtypeStruct(shape, kind)
    outs = [spec(rows4, BF)] * 3 + [spec((512, 1408), BF)] * 3 + [
        spec((512, 512), BF), spec((512, 128), BF), spec((512, 128), BF), spec((512, 512), BF),
        spec((512, 128), F32), spec((128, 2048), F32), spec((512, 128), F32), spec((512, 128), F32),
        spec((4, 8, 128), jnp.int32), spec((3, 4, 128, 2048), BF)]
    vm = pltpu.VMEM
    dma = pltpu.SemaphoreType.DMA
    scratch = [vm(rows4, BF)] * 3 + [
        vm((2048, 512), BF), vm((128, 2048), BF), vm((512, 2048), BF), vm((1408, 2048), BF),
        vm((2048, 1408), BF), vm((2048, 1408), BF),
        vm((512, 512), BF), vm((512, 128), BF), vm((512, 128), BF), vm((512, 512), BF), vm((512, 128), F32),
        vm(rows4, BF), vm((128, 2048), BF), vm((128, 2048), BF), vm((128, 2048), BF), vm((512, 1408), F32),
        vm((512, 1408), BF), vm((512, 1408), BF), vm((512, 1408), BF), vm((128, 2048), F32),
        vm((512, 128), F32), vm((512, 128), F32), vm((4, 8, 128), jnp.int32), vm((256, 256), F32), vm((256, 512), F32),
        dma((7,)), dma((15,))] + [dma((6,))] * 8 + [dma((3,))] * 2 + [dma((12,))] * 2
    return pl.pallas_call(
        forward_kernel,
        name="forward",
        out_shape=outs,
        in_specs=[pl.BlockSpec(memory_space=pltpu.VMEM)] * 8 + [pl.BlockSpec(memory_space=pl.ANY)] * 7,
        out_specs=[pl.BlockSpec(memory_space=pl.ANY)] * 16,
        scratch_shapes=scratch,
        compiler_params=pltpu.CompilerParams(
            collective_id=2, has_side_effects=True, vmem_limit_bytes=62 * 2**20
        ),
    )(tokens, norm_attn.reshape(1, 2048), norm_mlp.reshape(1, 2048), cos0, sin0, inv, segment_ids.reshape(1, 128),
      cotangent, w_query, w_key.T, w_value.T, w_out, w_down, w_gate, w_up)


PANELS = {
    "gz": (768, False, "gz", 0), "gy": (640, True, "gy", 0), "dy": (256, True, "dy", 0), "dz": (128, False, "dz", 0),
    "uy": (768, True, "uy", 0), "uz": (640, False, "uz", 0), "oz": (384, False, "gz", 0), "oy": (128, True, "gy", 384),
    "ay": (384, True, "gy", 0), "az": (256, False, "gz", 384),
}
SETS = {"gz": 768, "gy": 640, "dy": 256, "dz": 128, "uy": 768, "uz": 640}
DIRECT = ('ay', 'az')
EARLY = (
    "dz", "uz", "gz", "gy", "da2a", "da2b", "s2send", "mid.gy", "loa", "s2c0", "dy", "s2c1", "uy", "mid.gz", "mid.dz",
    "rows0", "lob", "sec.gy", "mid.uz", "rows1", "gt",
)
LATE = (
    "mid.uy", "fwd0", "do1", "fwd1", "sec.gz", "sec.dz", "mid.dy", "do2", "oz", "oy", "h0", "h1", "mid.t", "h2",
    "mid2.gy", "h3", "losend", "da1", "da1b", "s1send", "mid2.gz", "mid.oz", "s1c0", "mid2.dz", "ay", "sec.uy",
    "cro.gz", "sec.dy", "mid.oy", "s1c1", "loc0", "az", "mid.ay", "cro.t", "mid2.dy", "sec.uz", "mid2.uy", "cro.dz",
    "r0", "r1", "cro.gy", "mid.az", "sec.oz", "sec.oy", "sec.ay", "loc1", "gn0", "mid2.uz", "mid2.oz", "cro.dy",
    "cro.uy", "sec.az", "gn1", "spr.t", "mid2.oy", "cro.uz", "cro.oz", "fin.gy", "fin.dy", "gn2", "cro.ay", "cro.oy",
    "fin.uy", "cro.az", "fin.gz", "gfin", "lot", "fin.dz", "fin.oz", "fin.oy", "fin.ay", "fin.uz", "fin.t", "fin.az",
)
WIDE = 256


def grad_panel(grad, left, right, width, start):
    @pl.loop(0, 4)
    def _(at):
        rows = left[:, pl.ds(pl.multiple_of(at * 512, 512), 512)]
        cols = pl.ds(start, width)
        grad[at] = dot_tn(rows, right[:, cols]).astype(BF).reshape(2, 4, 64, width)


def grad_begin(panel, left, right, width, start):
    me, after, over, before = panel.at[1]
    for at, sends in ((over, ((0, over, 0, 1), (1, over, 1, -1))), (after, ((2, after, 1, 1),)),
                      (before, ((3, before, 0, -1),)), (me, ())):
        rows = left[:, pl.ds(pl.multiple_of(at * 512, 512), 512)]
        cols = pl.ds(start, width)
        panel.grad[at] = dot_tn(rows, right[:, cols]).astype(BF).reshape(2, 4, 64, width)
        for what in sends:
            panel.go(1, *what)


def norm_back(dn, rows, gain):
    r = inverse_rms(rows)
    e = dn * gain
    back = r * e - rows * (r * r * r) * jnp.mean(e * rows, axis=1, keepdims=True)
    return back, jnp.sum(dn * rows * r, axis=0, keepdims=True)


def backward_kernel(gain1, gain2, cnt, *refs):
    (a1_h, a2_h, dy_h, hid_h, dg_h, du_h, q_h, k_h, v_h, o_h, lse_h, x2_h, cos_h, sin_h, around_h,
     x_h, wq_h, wk_h, wv_h, wo_h, wd_h, wg_h, wu_h) = refs[:23]
    results, gains_o, refs = refs[23:32], refs[32], refs[33:]
    (lo_o, gt_o, gq_o, gk_o, gv_o, go_o, gg_o, gu_o, gd_o, osem), refs = refs[:10], refs[10:]
    sets, refs = {name: refs[2 * i:2 * i + 2] for i, name in enumerate(SETS)}, refs[2 * len(SETS):]
    slots, refs = {name: refs[6 * i:6 * i + 6] for i, name in enumerate(PANELS)}, refs[6 * len(PANELS):]
    (TG, TN, TS, TX, TT, TF, HS, t_send, t_recv,
     X0, X1, X3, DX2F, Ra0, Ra1, Ra2, Rb0, Rb1, Rb2, GA, GO,
     lsem, s2s, s2r, sls, slr, s1s, s1r, g4s, g4r, gs, gr, credit) = refs
    y, xh, z, tp = place()
    p = Peers()
    peers = [
        (ring(y, 1) * 8 + xh * 4 + z, tp), (ring(y, -1) * 8 + xh * 4 + z, tp),
        (y * 8 + xh * 4 + ring(z, 1), tp), (y * 8 + xh * 4 + ring(z, -1), tp),
        (ring(y, 2) * 8 + xh * 4 + z, tp), (y * 8 + xh * 4 + ring(z, 2), tp),
        (y * 8 + (1 - xh) * 4 + z, tp), p.to_core, p.to_next, p.to_far]
    barrier = pltpu.get_barrier_semaphore()
    for device in peers:
        pl.semaphore_signal(barrier, inc=1, device_id=device, device_id_type=MESH)

    def give(*which):
        for i in which:
            pltpu.make_async_copy((lo_o, gt_o, gq_o, gk_o, gv_o, go_o, gg_o, gu_o, gd_o)[i], results[i], osem.at[i]).start()

    n_loads, waited, chunks_of = [0], {}, {}

    def load(src, dst):
        copy = pltpu.make_async_copy(src, dst, lsem.at[n_loads[0]])
        n_loads[0] += 1
        copy.start()
        return copy

    def put_cols(ref, start, width):
        def put(v):
            ref[:, pl.ds(start, width)] = v
        return put

    def put_az(v):
        gq_o[:, 384:] = v[:, :128]
        gk_o[...] = v[:, 128:192]
        gv_o[...] = v[:, 192:]

    puts = {"gz": put_cols(gg_o, 640, 768), "gy": put_cols(gg_o, 0, 640), "dy": put_cols(gd_o, 1024, 256),
            "dz": put_cols(gd_o, 1280, 128), "uy": put_cols(gu_o, 0, 768), "uz": put_cols(gu_o, 768, 640),
            "oz": put_cols(go_o, 0, 384), "oy": put_cols(go_o, 384, 128), "ay": put_cols(gq_o, 0, 384), "az": put_az}
    panels = {}
    for name, (width, y_first, at, start) in PANELS.items():
        grad, near = sets[at]
        if SETS[at] != width:
            cols = pl.ds(start, width)
            grad, near = grad.at[:, :, :, :, cols], near.at[:, :, :, cols]
        panels[name] = Panel(y_first, grad, near, *slots[name], puts[name], name in DIRECT)
    wide = Panel(False, TG, TN, TS, None, None, None, t_send, t_recv, None)
    reused = {"gz": 0, "gy": 1}
    steps = {}
    outs = {"gz": (6,), "gy": (6,), "uy": (7,), "uz": (7,), "dy": (8,), "dz": (8,), "t": (8,), "oz": (5,), "oy": (5,),
            "ay": (2, 3, 4), "az": (2, 3, 4)}

    def middle(name, stage):
        panels[name].middle(stage)

    def second(name):
        panel = panels[name]
        panel.end(1)
        if name in reused:
            for step in (1, -1):
                pl.semaphore_signal(credit.at[reused[name]], inc=1, device_id=panel.device(1, step), device_id_type=MESH)
        panel.begin(2)

    def cross(name):
        panels[name].end(2)
        panels[name].cross()

    def finished(name):
        which = outs.pop(name)
        if which not in outs.values():
            give(*which)

    def finish(name):
        panels[name].finish()
        finished(name)

    def reuse(name):
        panels[name].sent(6)
        pl.semaphore_wait(credit.at[reused[name]], 2)

    along_y = ((peers[0], ring(y, 1), ring(y, -1)), (peers[1], ring(y, -1), ring(y, 1)), (peers[4], ring(y, 2), ring(y, 2)))

    def part_cols(at):
        return pl.ds(pl.multiple_of(at * WIDE, WIDE), WIDE)

    def wide_copy(kind, slot, HID=None):
        device, to, _ = along_y[slot]
        if kind == 0:
            src, dst = HS.at[slot] if HID is None else HID.at[:, part_cols(to)], HS.at[slot]
        else:
            src, dst = TT.at[to], TF.at[slot]
        sem = 6 + 3 * kind + slot
        return pltpu.make_async_remote_copy(
            src_ref=src, dst_ref=dst, send_sem=t_send.at[sem], recv_sem=t_recv.at[sem],
            device_id=device, device_id_type=MESH)

    def wide_crossing():
        return pltpu.make_async_remote_copy(
            src_ref=TS.at[:, wide.other], dst_ref=TX, send_sem=t_send.at[12], recv_sem=t_recv.at[12],
            device_id=wide.across, device_id_type=MESH)

    def wide_cross():
        wide.end(1)
        wide_crossing().start()

    def wide_spread():
        wide_crossing().wait_recv()

        @pl.loop(0, 4)
        def _(q):
            TT[q] = (TS[q, xh].astype(F32) + TX[q].astype(F32)).astype(BF)

        gd_o[:, part_cols(y)] = TS[y, xh].astype(F32) + TX[y].astype(F32)
        for slot in range(3):
            wide_copy(1, slot).start()

    def wide_finish():
        for slot in range(3):
            wide_copy(1, slot).wait_recv()
            gd_o[:, part_cols(along_y[slot][2])] = TF[slot].astype(F32)
        finished("t")

    stages = ((peers[0], peers[1], peers[4]), (peers[2], peers[3], peers[5]), (peers[6],), (p.to_core, p.to_next, p.to_far))

    def add_gain(row, gain):
        for i in range(4):
            GA[0, 0, row + i:row + i + 1] += gain[:, 512 * i:512 * i + 512]

    def gain_copy(stage, i):
        sem = 3 * stage + i
        return pltpu.make_async_remote_copy(
            src_ref=GA.at[stage, 0], dst_ref=GA.at[stage, i + 1], send_sem=gs.at[sem], recv_sem=gr.at[sem],
            device_id=stages[stage][i], device_id_type=MESH)

    def gain_send(stage):
        for i in range(len(stages[stage])):
            gain_copy(stage, i).start()

    def gain_sum(stage):
        total = GA[stage, 0]
        for i in range(len(stages[stage])):
            gain_copy(stage, i).wait_recv()
            total = total + GA[stage, i + 1]
        return total

    def gain_next(stage):
        GA[stage + 1, 0] = gain_sum(stage)
        gain_send(stage + 1)

    scatter2 = Scatter(p, X0, Ra0, Ra1, Ra2, s2s, s2r, 2)
    scatter_out = Scatter(p, X3, Rb0, Rb1, Rb2, sls, slr, 2)
    scatter1 = Scatter(p, X0, Ra0, Ra1, Ra2, s1s, s1r, 2)
    gather = Gather(p, DX2F, g4s, g4r, 2)

    def need(*loads):
        for one in loads:
            if id(one) not in waited:
                waited[id(one)] = one
                one.wait()

    def twice(run):
        return lambda: [run(i) for i in range(2)]

    for name in panels:
        steps["mid." + name] = functools.partial(middle, name, 1)
        steps["sec." + name] = functools.partial(second, name)
        steps["mid2." + name] = functools.partial(middle, name, 2)
        steps["cro." + name] = functools.partial(cross, name)
        steps["fin." + name] = functools.partial(finish, name)
    steps["mid.t"], steps["cro.t"], steps["spr.t"], steps["fin.t"] = functools.partial(wide.middle, 1), wide_cross, wide_spread, wide_finish
    for i in range(2):
        steps["s2c%d" % i] = functools.partial(scatter2.combine, i)
        steps["loc%d" % i] = functools.partial(scatter_out.combine, i)
        steps["s1c%d" % i] = functools.partial(scatter1.combine, i)
    for i in range(3):
        steps["gn%d" % i] = functools.partial(gain_next, i)

    def sender(scatter):
        def run():
            twice(scatter.cross)()
            twice(scatter.own)()
        return run

    steps["s2send"], steps["losend"], steps["s1send"] = sender(scatter2), sender(scatter_out), sender(scatter1)

    def layer_total():
        for i in range(2):
            rows = scatter_out.rowsof(i)
            lo_o[rows] = lo_o[rows] + scatter_out.total(i)
        give(0)

    def gain_last():
        GO[...] = pltpu.roll(gain_sum(3), lax.rem(512 - lax.rem(p.dp * 64 + tp * 16, 512), 512), 1)[:, :128]
        for i in range(2):
            gains_o[i:i + 1] = GO[pl.ds(4 * i + y, 1), :16]

    steps["lot"], steps["gfin"] = layer_total, gain_last

    def early(DY, HID, DG, DU, WG, WU, WD, ST, wsem):
        l_dy, l_hid, l_a2, l_du = load(dy_h, DY), load(hid_h, HID), load(a2_h, X1), load(du_h, DU)

        def around_chunk(i):
            return [pltpu.make_async_copy(around_h.at[:, :, pl.ds(256 * i, 256)], ST.at[i % 2], wsem.at[6 + i % 2])]

        def gate_chunk(i):
            at = pl.ds(256 * i, 256)
            return [pltpu.make_async_copy(wg_h.at[at], WG.at[i % 2], wsem.at[i % 2]),
                    pltpu.make_async_copy(wu_h.at[at], WU.at[i % 2], wsem.at[2 + i % 2])]

        def down_chunk(i):
            return [pltpu.make_async_copy(wd_h.at[:, pl.ds(256 * i, 256)], WD.at[i % 2], wsem.at[4 + i % 2])]

        def stream(chunk, use):
            for i in chunks_of[chunk]:
                for copy in chunk(i):
                    copy.wait()
                use(i)
                if i < 6:
                    for copy in chunk(i + 2):
                        copy.start()

        GA[0, 0] = jnp.zeros((8, 512), F32)
        pl.semaphore_wait(barrier, len(peers))
        for slot in range(3):
            wide_copy(0, slot, hid_h).start()
        l_dg = load(dg_h, DG)
        for i in range(2):
            for copy in gate_chunk(i):
                copy.start()
        l_x2 = load(x2_h, lo_o)
        for i in range(2):
            for copy in down_chunk(i) + around_chunk(i):
                copy.start()
        a2 = X1.reshape(512, 2048)

        def grads(name, left, right, width, start, *loads):
            def run():
                need(*loads)
                panel = panels[name]
                if panel.y_first:
                    grad_begin(panel, left, right, width, start)
                else:
                    grad_panel(panel.grad, left, right, width, start)
                    panel.begin(1)
            steps[name] = run

        grads("gz", a2, DG, 768, 640, l_a2, l_dg)
        grads("gy", a2, DG, 640, 0, l_a2, l_dg)
        grads("uy", a2, DU, 768, 0, l_a2, l_du)
        grads("uz", a2, DU, 640, 768, l_a2, l_du)
        grads("dy", DY, HID, 256, 1024, l_dy, l_hid)
        grads("dz", DY, HID, 128, 1280, l_dy, l_hid)

        def normed(i):
            da = dot_nt(DG[...], WG[i % 2]) + dot_nt(DU[...], WU[i % 2])
            X0[:, :, pl.ds(256 * i, 256)] = da.astype(BF).reshape(4, 128, 256)

        def part_of_out(i):
            X3[:, :, pl.ds(256 * i, 256)] = dot(HID[...], WD[i % 2]).astype(BF).reshape(4, 128, 256)

        def from_four(i):
            total = dot_tn(DY[:, pl.ds(256 * i, 256)], HID[:, part_cols(y)])
            for slot in range(3):
                total += dot_tn(ST[i % 2, slot], HS[slot])
            TG[i // 2, i % 2] = total.astype(BF).reshape(4, 64, WIDE)

        def half(chunk, use, which, *loads):
            def run():
                need(*loads)
                chunks_of[chunk] = range(4 * which, 4 * which + 4)
                stream(chunk, use)
            return run

        for which in range(2):
            steps["da2" + "ab"[which]] = half(gate_chunk, normed, which, l_dg, l_du)
            steps["lo" + "ab"[which]] = half(down_chunk, part_of_out, which, l_hid)

        def four():
            need(l_dy, l_hid)
            for slot in range(3):
                wide_copy(0, slot).wait_recv()
            chunks_of[around_chunk] = range(8)
            stream(around_chunk, from_four)
            wide.begin(1)

        def middle_rows(i):
            need(l_x2)
            rows = scatter2.rowsof(i)
            back, gain = norm_back(scatter2.total(i), lo_o[rows], gain2[...])
            add_gain(4, gain)
            dx2 = DY[pl.ds(pl.multiple_of(tp * 128 + i * 64, 64), 64)].astype(F32) + back
            gt_o[rows] = dx2
            DX2F[p.me, rows] = dx2.astype(BF)
            gather.start(i)

        steps["gt"] = four
        for i in range(2):
            steps["rows%d" % i] = functools.partial(middle_rows, i)
        for name in EARLY:
            steps[name]()
        need(l_dy, l_hid, l_a2, l_du, l_dg, l_x2)
        for slot in range(3):
            wide_copy(0, slot, hid_h).wait_send()

    def late(X, A1, Wo, Wq, Wkv, Q, O, DO, DQ, K, V, DKV, LSE, COS, SIN, B0, B1, DK, DV):
        l_wo, l_o, l_q, l_k, l_v, l_lse, l_cos, l_sin, l_a1, l_wq, l_wk, l_wv, l_x = late_loads = [load(*w) for w in (
            (wo_h, Wo), (o_h, O), (q_h, Q), (k_h, K), (v_h, V), (lse_h, LSE), (cos_h, COS), (sin_h, SIN),
            (a1_h, A1), (wq_h, Wq), (wk_h, Wkv.at[pl.ds(0, 64)]), (wv_h, Wkv.at[pl.ds(64, 64)]), (x_h, X))]
        ones = cnt[0] + cnt[1] + cnt[2] + cnt[3]
        first = 512 - ones[0:1, 0:1]
        for bias, block in zip((B0, B1), BLOCKS):
            mask_bias(bias, first, *block)

        def back_out(chip):
            need(l_wo)
            rows = pl.ds(pl.multiple_of(chip * 256, 256), 256)
            DO[rows] = dot_nt(chip_rows(DX2F, chip), Wo[...]).astype(BF)

        def forward_first():
            gather.near()
            gather.forward(0)

        def back_rest():
            twice(gather.rest)()
            back_out(1 - p.chip)

        steps["fwd0"], steps["fwd1"] = forward_first, functools.partial(gather.forward, 1)
        steps["do1"], steps["do2"] = functools.partial(back_out, p.chip), back_rest
        zero = jnp.zeros((512, 128), BF)
        left = lanes((512, 128)) < 64

        def heads(j):
            cols = pl.ds(128 * j, 128)
            for bias, (start, rows, keys) in zip((B0, B1), BLOCKS):
                at = pl.ds(start, rows)
                qs = split_heads(Q[at, cols])
                dos = split_heads(DO[at, cols])
                s = dot_nt(qs, K[:keys]) * 0.125
                s = (s.reshape(2, rows, keys) + bias[...][None]).reshape(2 * rows, keys)
                lse = jnp.concatenate([LSE[at, 2 * j:2 * j + 1], LSE[at, 2 * j + 1:2 * j + 2]], axis=0)
                prob = jnp.exp(s - lse)
                dp = dot_nt(dos, V[:keys])
                row_dot = jnp.sum(prob * dp, axis=1, keepdims=True)
                ds = (prob * (dp - row_dot) * 0.125).astype(BF)
                dv = dot_tn(prob.astype(BF), dos)
                dk = dot_tn(ds, qs)
                if j == 0 and keys == 512:
                    DV[256:] = dv[256:]
                    DK[256:] = dk[256:]
                    DV[:256] += dv[:256]
                    DK[:256] += dk[:256]
                elif j == 0:
                    DV[:keys] = dv
                    DK[:keys] = dk
                else:
                    DV[:keys] += dv
                    DK[:keys] += dk
                kl = jnp.where(left[:keys], K[:keys], zero[:keys])
                kr = jnp.where(left[:keys], zero[:keys], K[:keys])
                dq = dot(ds[:rows], kl) + dot(ds[rows:], kr)
                DQ[at, cols] = (dq * COS[at] - turned(dq) * SIN[at]).astype(BF)

        def head_step(j):
            need(l_q, l_k, l_v, l_lse, l_cos, l_sin)
            heads(j)
            if j == 3:
                dk = DK[...] + pltpu.roll(DK[...], 64, 1)
                dv = DV[...] + pltpu.roll(DV[...], 64, 1)
                DKV[...] = jnp.where(left, dk * COS[...] - turned(dk) * SIN[...], dv).astype(BF)

        for j in range(4):
            steps["h%d" % j] = functools.partial(head_step, j)

        def normed(which):
            need(l_wq, l_wk, l_wv)
            if not which:
                scatter2.drain()
            for i in range(2 * which, 2 * which + 2):
                at = pl.ds(512 * i, 512)
                da = dot_nt(DQ[...], Wq[at]) + dot(DKV[...], Wkv[:, at])
                X0[:, :, at] = da.astype(BF).reshape(4, 128, 512)

        steps["da1"], steps["da1b"] = functools.partial(normed, 0), functools.partial(normed, 1)

        def reuse_once(name):
            if name in reused:
                reuse(name)
                del reused[name]

        def out_z():
            need(l_o)
            reuse_once("gz")
            grad_panel(panels["oz"].grad, DX2F.reshape(512, 2048), O, 384, 0)
            panels["oz"].begin(1)

        def out_y():
            need(l_o)
            reuse_once("gy")
            grad_begin(panels["oy"], DX2F.reshape(512, 2048), O, 128, 384)

        def attn_y():
            need(l_a1)
            reuse_once("gy")
            grad_begin(panels["ay"], A1, DQ, 384, 0)

        def attn_z():
            need(l_a1)
            reuse_once("gz")
            grad_z = panels["az"].grad
            grad_panel(grad_z.at[:, :, :, :, pl.ds(0, 128)], A1, DQ, 128, 384)
            grad_panel(grad_z.at[:, :, :, :, pl.ds(128, 128)], A1, DKV, 128, 0)
            panels["az"].begin(1)

        steps["oz"], steps["oy"], steps["ay"], steps["az"] = out_z, out_y, attn_y, attn_z

        def first_rows(i):
            need(l_x)
            rows = scatter1.rowsof(i)
            back, gain = norm_back(scatter1.total(i), X[rows].astype(F32), gain1[...])
            add_gain(0, gain)
            gt_o[rows] = gt_o[rows] + back
            if i:
                give(1)
                gain_send(0)

        for i in range(2):
            steps["r%d" % i] = functools.partial(first_rows, i)
        for name in LATE:
            steps[name]()
        need(*late_loads)

    vm, dma = pltpu.VMEM, pltpu.SemaphoreType.DMA
    pl.run_scoped(early, vm((512, 2048), BF), vm((512, 1408), BF), vm((512, 1408), BF), vm((512, 1408), BF),
                  vm((2, 256, 1408), BF), vm((2, 256, 1408), BF), vm((2, 1408, 256), BF), vm((2, 3, 512, 256), BF), dma((8,)))
    pl.run_scoped(late, vm((128, 2048), BF), vm((512, 2048), BF), vm((512, 2048), BF), vm((2048, 512), BF),
                  vm((128, 2048), BF), vm((512, 512), BF), vm((512, 512), BF), vm((512, 512), BF), vm((512, 512), BF),
                  vm((512, 128), BF), vm((512, 128), BF), vm((512, 128), BF), vm((512, 128), F32),
                  vm((512, 128), F32), vm((512, 128), F32), vm((256, 256), F32), vm((256, 512), F32),
                  vm((512, 128), F32), vm((512, 128), F32))
    for i in range(9):
        pltpu.make_async_copy((lo_o, gt_o, gq_o, gk_o, gv_o, go_o, gg_o, gu_o, gd_o)[i], results[i], osem.at[i]).wait()
    for stage in range(4):
        for i in range(len(stages[stage])):
            gain_copy(stage, i).wait_send()
    for panel in panels.values():
        panel.drain()
    wide.sent(6)
    wide_crossing().wait_send()
    for slot in range(3):
        wide_copy(1, slot).wait_send()
    for what in (scatter_out, scatter1, gather):
        what.drain()


def backward(kept, tokens, norm_attn, norm_mlp, w_query, w_key, w_value, w_out, w_down, w_gate, w_up):
    (a1, a2, dy, hidden, d_gate, d_up, q, k, v, o, lse, x2, cos, sin, cnt, around) = kept
    vm, dma = pltpu.VMEM, pltpu.SemaphoreType.DMA
    shapes = ((128, 2048), (128, 2048), (64, 512), (64, 64), (64, 64), (64, 512), (64, 1408), (64, 1408), (64, 1408),
              (2, 16))
    scratch = [vm(shape, F32) for shape in shapes[:9]] + [dma((9,))]
    for w in SETS.values():
        scratch += [vm((4, 2, 4, 64, w), BF), vm((6, 4, 64, w), BF)]
    for name, (w, *_) in PANELS.items():
        far = (3, 2, 64, w) if name in DIRECT else (6, 64, w)
        scratch += [vm((4, 2, 64, w), BF), vm(far, BF), vm((2, 64, w), BF), vm((64, w), BF), dma((13,)), dma((13,))]
    scratch += [vm((4, 2, 4, 64, WIDE), BF), vm((6, 4, 64, WIDE), BF), vm((4, 2, 64, WIDE), BF), vm((4, 64, WIDE), BF),
                vm((4, 64, WIDE), BF), vm((3, 64, WIDE), BF), vm((3, 512, WIDE), BF), dma((13,)), dma((13,))]
    scratch += [vm((4, 128, 2048), BF)] * 4 + [vm((128, 2048), BF)] * 6
    scratch += [vm((4, 4, 8, 512), F32), vm((8, 128), F32)]
    scratch += [dma((23,))] + [dma((6,))] * 8 + [dma((12,))] * 2 + [pltpu.SemaphoreType.REGULAR((2,))]
    return pl.pallas_call(
        backward_kernel,
        name="backward",
        out_shape=[jax.ShapeDtypeStruct(shape, F32) for shape in shapes],
        in_specs=[pl.BlockSpec(memory_space=pltpu.VMEM)] * 3 + [pl.BlockSpec(memory_space=pl.ANY)] * 23,
        out_specs=[pl.BlockSpec(memory_space=pl.ANY)] * 9 + [pl.BlockSpec(memory_space=pltpu.VMEM)],
        scratch_shapes=scratch,
        compiler_params=pltpu.CompilerParams(
            collective_id=3, has_side_effects=True, vmem_limit_bytes=63 * 2**20
        ),
    )(norm_attn.reshape(1, 2048), norm_mlp.reshape(1, 2048), cnt,
      a1.reshape(512, 2048), a2, dy.reshape(512, 2048), hidden, d_gate, d_up, q, k, v, o, lse, x2, cos, sin,
      around.reshape(3, 512, 2048), tokens, w_query, w_key.T, w_value.T, w_out, w_down, w_gate, w_up)


def deliver_kernel(*refs):
    ins, outs, held, (one, two), sems = refs[:10], refs[10:21], refs[21:31], refs[31:33], refs[33:]
    come = [pltpu.make_async_copy(i, h, sems[0].at[n]) for n, (i, h) in enumerate(zip(ins, held))]
    leave = [pltpu.make_async_copy(h, o, sems[1].at[n]) for n, (h, o) in enumerate(zip(held[:9] + (one, two), outs))]
    for copy in come:
        copy.start()
    for before, after in zip(come[:9], leave):
        before.wait()
        after.start()
    come[9].wait()
    one[...] = held[9][0:1]
    two[...] = held[9][1:2]
    for copy in leave[9:]:
        copy.start()
    for copy in leave:
        copy.wait()


def deliver(parts):
    shapes = [jax.ShapeDtypeStruct(a.shape, F32) for a in parts[:9]] + [jax.ShapeDtypeStruct((1, 16), F32)] * 2
    return pl.pallas_call(
        deliver_kernel,
        name="deliver",
        out_shape=shapes,
        in_specs=[pl.BlockSpec(memory_space=pl.ANY)] * 10,
        out_specs=[pl.BlockSpec(memory_space=pl.ANY)] * 11,
        scratch_shapes=[pltpu.VMEM(a.shape, F32) for a in parts] + [pltpu.VMEM((1, 16), F32)] * 2
        + [pltpu.SemaphoreType.DMA((10,)), pltpu.SemaphoreType.DMA((11,))],
    )(*parts)


def per_device(
    tokens,
    norm_attn,
    w_query,
    w_key,
    w_value,
    w_out,
    norm_mlp,
    w_gate,
    w_up,
    w_down,
    segment_ids,
    cotangent,
):
    weights = (w_query, w_key, w_value, w_out, w_down, w_gate, w_up)
    kept = forward(tokens, norm_attn, norm_mlp, segment_ids, cotangent, *weights)
    (layer_out, grad_tokens, g_query, g_key, g_value, g_out, g_gate, g_up, g_down, gain1, gain2) = deliver(backward(
        kept, tokens, norm_attn, norm_mlp, *weights))
    return (layer_out, grad_tokens, gain1.reshape(16), g_query, g_key, g_value, g_out.T, gain2.reshape(16), g_gate, g_up,
            g_down.T)


def solution(mesh):
    placed = (
        P(("dp", "tp"), None),
        P(),
        P(None, "tp"),
        P(None, "tp"),
        P(None, "tp"),
        P("tp", None),
        P(),
        P(None, "tp"),
        P(None, "tp"),
        P("tp", None),
        P(("dp", "tp")),
        P(("dp", "tp"), None),
    )
    return jax.shard_map(
        per_device,
        mesh=mesh,
        in_specs=placed,
        out_specs=(
            P(("dp", "tp"), None),
            P(("dp", "tp"), None),
            P(("dp", "tp")),
            P("dp", "tp"),
            P("dp", "tp"),
            P("dp", "tp"),
            P("tp", "dp"),
            P(("dp", "tp")),
            P("dp", "tp"),
            P("dp", "tp"),
            P("tp", "dp"),
        ),
        check_vma=False,
    )
```

```python
import functools
import math

import jax
import jax.numpy as jnp
import numpy as np
from jax import lax
from jax.experimental import pallas as pl
from jax.experimental.pallas import tpu as pltpu
from jax.sharding import PartitionSpec as P

HD = 64
BF = jnp.bfloat16
F32 = jnp.float32
MESH = pl.DeviceIdType.MESH


def place():
    dp = lax.axis_index("dp")
    tp = lax.axis_index("tp")
    return dp // 8, lax.rem(dp // 4, 2), lax.rem(dp, 4), tp


def ring(me, step):
    return lax.rem(me + step + 4, 4)


class Panel:
    def __init__(self, y_first, grad, near, second, far, last, from_x, send, recv, put, direct=False):
        self.y_first = y_first
        self.grad, self.near, self.second, self.far = grad, near, second, far
        self.last, self.from_x = last, from_x
        self.send, self.recv = send, recv
        self.put = put
        self.direct = direct
        y, xh, z, tp = place()
        self.xh = xh
        one, two = (y, z) if y_first else (z, y)
        steps = lambda me: (me, ring(me, 1), ring(me, 2), ring(me, -1))
        self.at = (None, steps(one), steps(two))
        self.devices = {}
        for step in (1, -1, 2):
            along_y = (ring(y, step) * 8 + xh * 4 + z, tp)
            along_z = (y * 8 + xh * 4 + ring(z, step), tp)
            self.devices[1, step], self.devices[2, step] = (along_y, along_z) if y_first else (along_z, along_y)
        self.other = 1 - xh
        self.across = (y * 8 + self.other * 4 + z, tp)
        self.started = []

    def device(self, stage, step):
        return self.devices[stage, step]

    def part(self, stage, at, half):
        if half is None:
            return self.second.at[at]
        if stage == 1:
            return self.grad.at[at, half] if self.y_first else self.grad.at[:, half, at]
        return self.second.at[at, half]

    def landed(self, stage, k):
        return (self.near if stage == 1 else self.far).at[k]

    def copy(self, stage, k, at, half, step):
        sem = k + (6 if stage == 2 else 0)
        return pltpu.make_async_remote_copy(
            src_ref=self.part(stage, at, half),
            dst_ref=self.landed(stage, k),
            send_sem=self.send.at[sem],
            recv_sem=self.recv.at[sem],
            device_id=self.device(stage, step),
            device_id_type=MESH,
        )

    def go(self, stage, k, at, half, step):
        what = (stage, k, at, half, step)
        self.copy(*what).start()
        self.started.append(what)

    def arrived(self, stage, k):
        half = None if stage == 2 and self.direct else 0
        self.copy(stage, k, self.at[stage][0], half, 1).wait_recv()

    def begin(self, stage):
        me, right, over, left = self.at[stage]
        if stage == 2 and self.direct:
            for k, (at, step) in enumerate(((right, 1), (left, -1), (over, 2))):
                self.go(2, k, at, None, step)
            return
        self.go(stage, 0, over, 0, 1)
        self.go(stage, 1, over, 1, -1)
        self.go(stage, 2, right, 1, 1)
        self.go(stage, 3, left, 0, -1)

    def add(self, into, what):
        if len(into.shape) == 3:
            @pl.loop(0, into.shape[0])
            def _(i):
                into[i] = (into[i].astype(F32) + what[i].astype(F32)).astype(BF)
        else:
            into[...] = (into[...].astype(F32) + what[...].astype(F32)).astype(BF)

    def middle(self, stage):
        me, right, over, left = self.at[stage]
        for k, at, half, step in ((0, right, 0, 1), (1, left, 1, -1)):
            self.arrived(stage, k)
            self.add(self.part(stage, at, half), self.landed(stage, k))
            self.go(stage, k + 4, at, half, step)

    def end(self, stage):
        me = self.at[stage][0]
        if stage == 2 and self.direct:
            for k in range(3):
                self.arrived(2, k)
            total = self.second[me].astype(F32)
            for k in range(3):
                total += self.far[k].astype(F32)
            self.last[...] = total.astype(BF)
            return
        for half, (a, b) in enumerate(((4, 3), (2, 5))):
            self.arrived(stage, a)
            self.arrived(stage, b)
            own, one, two = self.part(stage, me, half), self.landed(stage, a), self.landed(stage, b)
            if stage == 1:
                @pl.loop(0, 4)
                def _(q):
                    total = own[q].astype(F32) + one[q].astype(F32) + two[q].astype(F32)
                    self.second[q, half] = total.astype(BF)
            else:
                total = own[...].astype(F32) + one[...].astype(F32) + two[...].astype(F32)
                self.last[half] = total.astype(BF)

    def crossing(self):
        return pltpu.make_async_remote_copy(
            src_ref=self.last.at[self.other],
            dst_ref=self.from_x,
            send_sem=self.send.at[12],
            recv_sem=self.recv.at[12],
            device_id=self.across,
            device_id_type=MESH,
        )

    def cross(self):
        self.crossing().start()

    def finish(self):
        self.crossing().wait_recv()
        self.put(self.last[self.xh].astype(F32) + self.from_x[...].astype(F32))

    def sent(self, count):
        for what in self.started[:count]:
            self.copy(*what).wait_send()
        self.started = self.started[count:]

    def drain(self):
        self.sent(len(self.started))
        self.crossing().wait_send()


def dot(a, b):
    return jnp.dot(a, b, preferred_element_type=F32)


def dot_nt(a, b):
    return lax.dot_general(a, b, (((1,), (1,)), ((), ())), preferred_element_type=F32)


def dot_tn(a, b):
    return lax.dot_general(a, b, (((0,), (0,)), ((), ())), preferred_element_type=F32)


class Peers:
    def __init__(self):
        self.dp = lax.axis_index("dp")
        self.me = lax.axis_index("tp")
        self.core = self.me + 1 - 2 * lax.rem(self.me, 2)
        self.next = lax.rem(self.me + 2, 4)
        self.far = lax.rem(self.core + 2, 4)
        self.chip = self.me // 2
        self.to_core = (self.dp, self.core)
        self.to_next = (self.dp, self.next)
        self.to_far = (self.dp, self.far)


class Gather:
    def __init__(self, peers, buf, send, recv, parts):
        self.p, self.buf, self.send, self.recv, self.parts = peers, buf, send, recv, parts
        self.rows = buf.shape[1] // parts
        self.started = []

    def copy(self, kind, owner, i, device):
        at = self.buf.at[owner, pl.ds(i * self.rows, self.rows)]
        sem = kind * self.parts + i
        return pltpu.make_async_remote_copy(
            src_ref=at, dst_ref=at, send_sem=self.send.at[sem], recv_sem=self.recv.at[sem],
            device_id=device, device_id_type=MESH)

    def go(self, *what):
        self.copy(*what).start()
        self.started.append(what)

    def start(self, i):
        self.go(1, self.p.me, i, self.p.to_next)
        self.go(0, self.p.me, i, self.p.to_core)

    def near(self):
        for i in range(self.parts):
            self.copy(0, self.p.core, i, self.p.to_core).wait_recv()

    def forward(self, i):
        self.copy(1, self.p.next, i, self.p.to_next).wait_recv()
        self.go(2, self.p.next, i, self.p.to_core)

    def rest(self, i):
        self.copy(2, self.p.far, i, self.p.to_core).wait_recv()

    def drain(self):
        for what in self.started:
            self.copy(*what).wait_send()
        self.started = []


class Scatter:
    def __init__(self, peers, part, r0, r1, r2, send, recv, parts):
        self.p, self.part, self.r = peers, part, (r0, r1, r2)
        self.send, self.recv, self.parts = send, recv, parts
        self.rows = part.shape[1] // parts
        self.started = []

    def rowsof(self, i):
        return pl.ds(i * self.rows, self.rows)

    def copy(self, kind, owner, i, device):
        sem = kind * self.parts + i
        return pltpu.make_async_remote_copy(
            src_ref=self.part.at[owner, self.rowsof(i)], dst_ref=self.r[kind].at[self.rowsof(i)],
            send_sem=self.send.at[sem], recv_sem=self.recv.at[sem],
            device_id=device, device_id_type=MESH)

    def go(self, *what):
        self.copy(*what).start()
        self.started.append(what)

    def cross(self, i):
        self.go(0, self.p.far, i, self.p.to_core)

    def own(self, i):
        self.go(1, self.p.core, i, self.p.to_core)

    def combine(self, i):
        self.copy(0, self.p.far, i, self.p.to_core).wait_recv()
        at = self.part.at[self.p.next, self.rowsof(i)]
        at[...] = (at[...].astype(F32) + self.r[0][self.rowsof(i)].astype(F32)).astype(BF)
        self.go(2, self.p.next, i, self.p.to_next)

    def total(self, i):
        self.copy(1, self.p.core, i, self.p.to_core).wait_recv()
        self.copy(2, self.p.next, i, self.p.to_next).wait_recv()
        rows = self.rowsof(i)
        return (self.part[self.p.me, rows].astype(F32) + self.r[1][rows].astype(F32)
                + self.r[2][rows].astype(F32))

    def drain(self):
        for what in self.started:
            self.copy(*what).wait_send()
        self.started = []


class Around:
    def __init__(self, peers, buf, out, send, recv):
        self.p, self.buf, self.out, self.send, self.recv = peers, buf, out, send, recv
        y, xh, z, tp = place()
        self.to = [(ring(y, step) * 8 + xh * 4 + z, tp) for step in (1, -1, 2)]
        self.owners = (peers.me, peers.next)
        self.given = (peers.core, peers.far)
        self.started = []

    def copy(self, kind, which, slot):
        sem = 6 * kind + 3 * which + slot
        owner = self.owners[which] if kind < 2 else self.given[which]
        at = self.out.at[slot, owner]
        sem = sem if kind < 2 else sem - 6
        return pltpu.make_async_remote_copy(
            src_ref=self.buf.at[owner] if kind == 0 else at, dst_ref=at,
            send_sem=self.send.at[sem], recv_sem=self.recv.at[sem],
            device_id=self.p.to_core if kind else self.to[slot], device_id_type=MESH)

    def go(self, *what):
        self.copy(*what).start()
        self.started.append(what)

    def spread(self, which):
        for slot in range(3):
            self.go(0, which, slot)

    def hand(self, which, slot):
        self.copy(0, which, slot).wait_recv()
        self.go(1, which, slot)

    def rest(self, which):
        for slot in range(3):
            self.copy(2, which, slot).wait_recv()

    def drain(self):
        for what in self.started:
            self.copy(*what).wait_send()


def rope_tables():
    inverse = np.exp(np.arange(32, dtype=np.float64) * (-2.0 * math.log(10000.0) / 64))
    angles = np.arange(512, dtype=np.float64)[:, None] * np.tile(inverse, 4)[None, :]
    return (np.cos(angles).astype(np.float32), np.sin(angles).astype(np.float32),
            np.tile(inverse, 4)[None, :].astype(np.float32))


def lanes(shape):
    return lax.broadcasted_iota(jnp.int32, shape, len(shape) - 1)


def turned(values):
    low = lax.rem(lanes(values.shape), 64) < 32
    return jnp.where(low, pltpu.roll(values, 96, 1), pltpu.roll(values, 32, 1))


def split_heads(pair):
    left = lanes(pair.shape) < 64
    zero = jnp.zeros_like(pair)
    return jnp.concatenate([jnp.where(left, pair, zero), jnp.where(left, zero, pair)], axis=0)


BLOCKS = ((0, 256, 256), (256, 256, 512))
FF_TILES = ((0, 512), (512, 512), (1024, 384))


def mask_bias(bias, first, start, rows, keys):
    row = lax.broadcasted_iota(jnp.int32, (rows, keys), 0) + start
    key = lax.broadcasted_iota(jnp.int32, (rows, keys), 1)
    allowed = (key <= row) & ((row < first) == (key < first))
    bias[...] = jnp.where(allowed, 0.0, -1e9).astype(F32)


def inverse_rms(rows):
    return lax.rsqrt(jnp.mean(rows * rows, axis=1, keepdims=True) + 1e-5)


def chip_rows(buf, chip):
    return buf[pl.ds(chip * 2, 2)].reshape(256, buf.shape[2])


def forward_kernel(gain1, gain2, inv, seg, x_h, cos_h, sin_h, dy_h, *refs):
    hbm_w, refs = refs[:7], refs[7:]
    outs, around_o, refs = refs[:15], refs[15], refs[16:]
    (a1_o, a2_o, dy_o, hid_o, dg_o, du_o, q_o, k_o, v_o, o_o, lse_o, x2_o, cos_o, sin_o, cnt_o) = outs
    (A1, A2, DY, Wq, Wkv, Wo, Wd, Wg, Wu, Q, K, V, O, LSE, PM, R0, R1, R2, DH, HID, DG, DU, X2, COS, SIN,
     CNT, B0, B1, wsem, osem, g1s, g1r, g2s, g2r, g3s, g3r, ss, sr, cs, cr, as_, ar, x, cos0, sin0, isem) = refs
    weights = (Wq, Wkv.at[pl.ds(0, 64)], Wkv.at[pl.ds(64, 64)], Wo, Wd, Wg, Wu)
    loads = [pltpu.make_async_copy(h, w, wsem.at[i]) for i, (h, w) in enumerate(zip(hbm_w, weights))]
    p = Peers()
    barrier = pltpu.get_barrier_semaphore()
    around = Around(p, DY, around_o, as_, ar)
    for device in [p.to_core, p.to_next, p.to_far] + around.to:
        pl.semaphore_signal(barrier, inc=1, device_id=device, device_id_type=MESH)
    firsts = [pltpu.make_async_copy(h, v, isem.at[i]) for i, (h, v) in enumerate(
        ((x_h, x), (dy_h, DY.at[p.me]), (cos_h, cos0), (sin_h, sin0)))]
    for load in firsts + loads:
        load.start()
    stored = []

    def keep(src, dst):
        copy = pltpu.make_async_copy(src, dst, osem.at[len(stored)])
        copy.start()
        stored.append(copy)

    firsts[0].wait()
    stream = x[...].astype(F32)
    A1[p.me] = (stream * inverse_rms(stream) * gain1[...]).astype(BF)
    firsts[1].wait()
    CNT[p.me] = jnp.broadcast_to(jnp.sum(seg[...], axis=1, keepdims=True), (8, 128))
    pl.semaphore_wait(barrier, 6)
    first_in = Gather(p, A1, g1s, g1r, 2)
    for i in range(2):
        first_in.start(i)
    counts = [pltpu.make_async_remote_copy(
        src_ref=CNT.at[p.me], dst_ref=CNT.at[p.me], send_sem=cs.at[i], recv_sem=cr.at[i],
        device_id=device, device_id_type=MESH) for i, device in enumerate((p.to_core, p.to_next, p.to_far))]
    for copy in counts:
        copy.start()
    dy_in = Gather(p, DY, g2s, g2r, 2)
    for i in range(2):
        dy_in.start(i)
    around.spread(0)
    for i, owner in enumerate((p.core, p.next, p.far)):
        pltpu.make_async_remote_copy(
            src_ref=CNT.at[owner], dst_ref=CNT.at[owner], send_sem=cs.at[i], recv_sem=cr.at[i],
            device_id=p.to_core, device_id_type=MESH).wait_recv()
    ones = CNT[0] + CNT[1] + CNT[2] + CNT[3]
    first = 512 - ones[0:1, 0:1]
    firsts[2].wait()
    firsts[3].wait()
    angle = first.astype(F32) * inv[...]
    cos_n, sin_n = jnp.cos(angle), jnp.sin(angle)
    row = lax.broadcasted_iota(jnp.int32, (512, 128), 0)
    c0, s0 = cos0[...], sin0[...]
    COS[...] = jnp.where(row < first, c0, c0 * cos_n + s0 * sin_n)
    sine = jnp.where(row < first, s0, s0 * cos_n - c0 * sin_n)
    SIN[...] = jnp.where(lax.rem(lanes((512, 128)), 64) < 32, -sine, sine)
    for bias, block in zip((B0, B1), BLOCKS):
        mask_bias(bias, first, *block)
    keep(COS, cos_o)
    keep(SIN, sin_o)
    keep(CNT, cnt_o)

    def project(chip):
        rows = pl.ds(pl.multiple_of(chip * 256, 256), 256)
        a = chip_rows(A1, chip)
        cos, sin = COS[rows], SIN[rows]
        for j in range(2):
            q = dot(a, Wq[:, pl.ds(256 * j, 256)])
            for h in range(2):
                pair = q[:, 128 * h:128 * h + 128]
                Q[rows, pl.ds(256 * j + 128 * h, 128)] = (pair * cos + turned(pair) * sin).astype(BF)
        kv = dot_nt(a, Wkv[...])
        vk = pltpu.roll(kv, 64, 1)
        k_lane = lanes(kv.shape) < 64
        kk = jnp.where(k_lane, kv, vk)
        K[rows] = (kk * cos + turned(kk) * sin).astype(BF)
        V[rows] = jnp.where(k_lane, vk, kv).astype(BF)

    for load in loads[:3]:
        load.wait()
    first_in.near()
    project(p.chip)
    for i in range(2):
        first_in.forward(i)
    for i in range(2):
        first_in.rest(i)
    project(1 - p.chip)
    keep(A1, a1_o)
    keep(Q, q_o)
    keep(K, k_o)
    keep(V, v_o)

    zero = jnp.zeros((512, 128), BF)
    left = lanes((512, 128)) < 64
    def attend(block, pairs):
        bias = (B0, B1)[block]
        start, rows, keys = BLOCKS[block]
        for j in pairs:
            qs = split_heads(Q[pl.ds(start, rows), pl.ds(128 * j, 128)])
            s = dot_nt(qs, K[:keys]) * 0.125
            s = (s.reshape(2, rows, keys) + bias[...][None]).reshape(2 * rows, keys)
            top = jnp.max(s, axis=1, keepdims=True)
            e = jnp.exp(s - top)
            total = jnp.sum(e, axis=1, keepdims=True)
            lse = top + jnp.log(total)
            eb = (e / total).astype(BF)
            vl = jnp.where(left[:keys], V[:keys], zero[:keys])
            vr = jnp.where(left[:keys], zero[:keys], V[:keys])
            o = dot(eb[:rows], vl) + dot(eb[rows:], vr)
            O[pl.ds(start, rows), pl.ds(128 * j, 128)] = o.astype(BF)
            lane = lanes((rows, 128))
            old = LSE[pl.ds(start, rows)] if j else jnp.zeros((rows, 128), F32)
            LSE[pl.ds(start, rows)] = jnp.where(lane == 2 * j, lse[:rows], jnp.where(lane == 2 * j + 1, lse[rows:], old))

    def attend_rows(other, pairs):
        for chip in range(2):
            @pl.when(p.chip == chip)
            def _():
                attend(1 - chip if other else chip, pairs)

    def spread(chip):
        rows = pl.ds(pl.multiple_of(chip * 256, 256), 256)
        for j in range(4):
            cols = pl.ds(512 * j, 512)
            PM[pl.ds(chip * 2, 2), :, cols] = dot(O[rows], Wo[:, cols]).astype(BF).reshape(2, 128, 512)

    scatter = Scatter(p, PM, R0, R1, R2, ss, sr, 2)
    attend_rows(True, range(4))
    loads[3].wait()
    spread(1 - p.chip)
    for i in range(2):
        scatter.cross(i)
    attend_rows(False, range(2))
    for i in range(2):
        scatter.combine(i)
    attend_rows(False, range(2, 4))
    dy_in.near()
    for i in range(2):
        dy_in.forward(i)
    around.spread(1)
    keep(O, o_o)
    keep(LSE, lse_o)
    spread(p.chip)
    for i in range(2):
        scatter.own(i)
    loads[4].wait()
    for i in range(2):
        dy_in.rest(i)
    keep(DY, dy_o)
    for slot in range(3):
        around.hand(0, slot)
    dy = DY[...].reshape(512, 2048)
    for start, width in FF_TILES:
        DH[:, pl.ds(start, width)] = dot_nt(dy, Wd[pl.ds(start, width)])
    second_in = Gather(p, A2, g3s, g3r, 2)
    for i in range(2):
        rows = scatter.rowsof(i)
        x2 = x[rows].astype(F32) + scatter.total(i)
        X2[rows] = x2
        A2[p.me, rows] = (x2 * inverse_rms(x2) * gain2[...]).astype(BF)
        second_in.start(i)
    keep(X2, x2_o)

    def mlp(chip, start, count):
        a = A2[pl.ds(chip * 2, 2), pl.ds(start, count)].reshape(2 * count, 2048)
        rows = [pl.ds(pl.multiple_of(chip * 256 + 128 * i + start, 64), count) for i in range(2)]
        for first_col, width in FF_TILES:
            cols = pl.ds(first_col, width)
            g = dot(a, Wg[:, cols])
            u = dot(a, Wu[:, cols])
            dh = jnp.concatenate([DH[r, cols] for r in rows], axis=0)
            sg = jax.nn.sigmoid(g)
            act = g * sg
            values = ((HID, act * u), (DU, dh * act), (DG, dh * u * (sg + act * (1.0 - sg))))
            for ref, value in values:
                for i, r in enumerate(rows):
                    ref[r, cols] = value[i * count:(i + 1) * count].astype(BF)

    def keep_rows(chip):
        rows = pl.ds(pl.multiple_of(chip * 256, 256), 256)
        for ref, out in ((HID, hid_o), (DG, dg_o), (DU, du_o)):
            keep(ref.at[rows], out.at[rows])

    loads[5].wait()
    loads[6].wait()
    second_in.near()
    mlp(p.chip, 0, 128)
    keep_rows(p.chip)
    second_in.forward(0)
    for slot in range(2):
        around.hand(1, slot)
    second_in.rest(0)
    mlp(1 - p.chip, 0, 64)
    second_in.forward(1)
    second_in.rest(1)
    keep(A2, a2_o)
    around.hand(1, 2)
    mlp(1 - p.chip, 64, 64)
    keep_rows(1 - p.chip)
    around.rest(0)
    around.rest(1)
    for copy in stored:
        copy.wait()
    for copy in counts:
        copy.wait_send()
    for what in (first_in, dy_in, second_in, scatter, around):
        what.drain()


def forward(tokens, norm_attn, norm_mlp, segment_ids, cotangent, w_query, w_key, w_value, w_out, w_down, w_gate, w_up):
    cos0, sin0, inv = rope_tables()
    rows4 = (4, 128, 2048)
    spec = lambda shape, kind: jax.ShapeDtypeStruct(shape, kind)
    outs = [spec(rows4, BF)] * 3 + [spec((512, 1408), BF)] * 3 + [
        spec((512, 512), BF), spec((512, 128), BF), spec((512, 128), BF), spec((512, 512), BF),
        spec((512, 128), F32), spec((128, 2048), F32), spec((512, 128), F32), spec((512, 128), F32),
        spec((4, 8, 128), jnp.int32), spec((3, 4, 128, 2048), BF)]
    vm = pltpu.VMEM
    dma = pltpu.SemaphoreType.DMA
    scratch = [vm(rows4, BF)] * 3 + [
        vm((2048, 512), BF), vm((128, 2048), BF), vm((512, 2048), BF), vm((1408, 2048), BF),
        vm((2048, 1408), BF), vm((2048, 1408), BF),
        vm((512, 512), BF), vm((512, 128), BF), vm((512, 128), BF), vm((512, 512), BF), vm((512, 128), F32),
        vm(rows4, BF), vm((128, 2048), BF), vm((128, 2048), BF), vm((128, 2048), BF), vm((512, 1408), F32),
        vm((512, 1408), BF), vm((512, 1408), BF), vm((512, 1408), BF), vm((128, 2048), F32),
        vm((512, 128), F32), vm((512, 128), F32), vm((4, 8, 128), jnp.int32), vm((256, 256), F32), vm((256, 512), F32),
        dma((7,)), dma((18,))] + [dma((6,))] * 8 + [dma((3,))] * 2 + [dma((12,))] * 2 + [
        vm((128, 2048), BF), vm((512, 128), F32), vm((512, 128), F32), dma((4,))]
    return pl.pallas_call(
        forward_kernel,
        name="forward",
        out_shape=outs,
        in_specs=[pl.BlockSpec(memory_space=pltpu.VMEM)] * 4 + [pl.BlockSpec(memory_space=pl.ANY)] * 11,
        out_specs=[pl.BlockSpec(memory_space=pl.ANY)] * 16,
        scratch_shapes=scratch,
        compiler_params=pltpu.CompilerParams(
            collective_id=2, has_side_effects=True, vmem_limit_bytes=62 * 2**20
        ),
    )(norm_attn.reshape(1, 2048), norm_mlp.reshape(1, 2048), inv, segment_ids.reshape(1, 128),
      tokens, cos0, sin0, cotangent, w_query, w_key.T, w_value.T, w_out, w_down, w_gate, w_up)


PANELS = {
    "gz": (768, False, "gz", 0), "gy": (640, True, "gy", 0), "dy": (256, True, "dy", 0), "dz": (128, False, "dz", 0),
    "uy": (768, True, "uy", 0), "uz": (640, False, "uz", 0), "oz": (384, False, "gz", 0), "oy": (128, True, "gy", 384),
    "ay": (384, True, "gy", 0), "az": (256, False, "gz", 384),
}
SETS = {"gz": 768, "gy": 640, "dy": 256, "dz": 128, "uy": 768, "uz": 640}
DIRECT = ('ay', 'az')
EARLY = (
    "dz", "uz", "gz", "gy", "da2a", "da2b", "s2send", "mid.gy", "loa", "s2c0", "dy", "s2c1", "uy", "mid.gz", "mid.dz",
    "rows0", "lob", "sec.gy", "mid.uz", "rows1", "gt",
)
LATE = (
    "mid.uy", "fwd0", "do1", "fwd1", "sec.gz", "sec.dz", "mid.dy", "do2", "oz", "oy", "h0", "h1", "mid.t", "h2",
    "mid2.gy", "h3", "losend", "da1", "da1b", "s1send", "mid2.gz", "mid.oz", "s1c0", "mid2.dz", "ay", "sec.uy",
    "cro.gz", "sec.dy", "mid.oy", "s1c1", "loc0", "az", "mid.ay", "cro.t", "mid2.dy", "sec.uz", "mid2.uy", "cro.dz",
    "r0", "r1", "cro.gy", "mid.az", "sec.oz", "sec.oy", "sec.ay", "loc1", "gn0", "mid2.uz", "mid2.oz", "cro.dy",
    "cro.uy", "sec.az", "gn1", "spr.t", "mid2.oy", "cro.uz", "cro.oz", "fin.gy", "fin.dy", "gn2", "cro.ay", "cro.oy",
    "fin.uy", "cro.az", "fin.gz", "gfin", "lot", "fin.dz", "fin.oz", "fin.oy", "fin.ay", "fin.uz", "fin.t", "fin.az",
)
WIDE = 256


def grad_panel(grad, left, right, width, start):
    @pl.loop(0, 4)
    def _(at):
        rows = left[:, pl.ds(pl.multiple_of(at * 512, 512), 512)]
        cols = pl.ds(start, width)
        grad[at] = dot_tn(rows, right[:, cols]).astype(BF).reshape(2, 4, 64, width)


def grad_begin(panel, left, right, width, start):
    me, after, over, before = panel.at[1]
    for at, sends in ((over, ((0, over, 0, 1), (1, over, 1, -1))), (after, ((2, after, 1, 1),)),
                      (before, ((3, before, 0, -1),)), (me, ())):
        rows = left[:, pl.ds(pl.multiple_of(at * 512, 512), 512)]
        cols = pl.ds(start, width)
        panel.grad[at] = dot_tn(rows, right[:, cols]).astype(BF).reshape(2, 4, 64, width)
        for what in sends:
            panel.go(1, *what)


def norm_back(dn, rows, gain):
    r = inverse_rms(rows)
    e = dn * gain
    back = r * e - rows * (r * r * r) * jnp.mean(e * rows, axis=1, keepdims=True)
    return back, jnp.sum(dn * rows * r, axis=0, keepdims=True)


def backward_kernel(gain1, gain2, cnt, *refs):
    (a1_h, a2_h, dy_h, hid_h, dg_h, du_h, q_h, k_h, v_h, o_h, lse_h, x2_h, cos_h, sin_h, around_h,
     x_h, wq_h, wk_h, wv_h, wo_h, wd_h, wg_h, wu_h) = refs[:23]
    results, gains_o, refs = refs[23:32], refs[32], refs[33:]
    (lo_o, gt_o, gq_o, gk_o, gv_o, go_o, gg_o, gu_o, gd_o, osem), refs = refs[:10], refs[10:]
    sets, refs = {name: refs[2 * i:2 * i + 2] for i, name in enumerate(SETS)}, refs[2 * len(SETS):]
    slots, refs = {name: refs[6 * i:6 * i + 6] for i, name in enumerate(PANELS)}, refs[6 * len(PANELS):]
    (TG, TN, TS, TX, TT, TF, HS, t_send, t_recv,
     X0, X1, X3, DX2F, Ra0, Ra1, Ra2, Rb0, Rb1, Rb2, GA, GO,
     lsem, s2s, s2r, sls, slr, s1s, s1r, g4s, g4r, gs, gr, credit) = refs
    y, xh, z, tp = place()
    p = Peers()
    peers = [
        (ring(y, 1) * 8 + xh * 4 + z, tp), (ring(y, -1) * 8 + xh * 4 + z, tp),
        (y * 8 + xh * 4 + ring(z, 1), tp), (y * 8 + xh * 4 + ring(z, -1), tp),
        (ring(y, 2) * 8 + xh * 4 + z, tp), (y * 8 + xh * 4 + ring(z, 2), tp),
        (y * 8 + (1 - xh) * 4 + z, tp), p.to_core, p.to_next, p.to_far]
    barrier = pltpu.get_barrier_semaphore()
    for device in peers:
        pl.semaphore_signal(barrier, inc=1, device_id=device, device_id_type=MESH)

    def give(*which):
        for i in which:
            pltpu.make_async_copy((lo_o, gt_o, gq_o, gk_o, gv_o, go_o, gg_o, gu_o, gd_o)[i], results[i], osem.at[i]).start()

    n_loads, waited, chunks_of = [0], {}, {}

    def load(src, dst):
        copy = pltpu.make_async_copy(src, dst, lsem.at[n_loads[0]])
        n_loads[0] += 1
        copy.start()
        return copy

    def put_cols(ref, start, width):
        def put(v):
            ref[:, pl.ds(start, width)] = v
        return put

    def put_az(v):
        gq_o[:, 384:] = v[:, :128]
        gk_o[...] = v[:, 128:192]
        gv_o[...] = v[:, 192:]

    puts = {"gz": put_cols(gg_o, 640, 768), "gy": put_cols(gg_o, 0, 640), "dy": put_cols(gd_o, 1024, 256),
            "dz": put_cols(gd_o, 1280, 128), "uy": put_cols(gu_o, 0, 768), "uz": put_cols(gu_o, 768, 640),
            "oz": put_cols(go_o, 0, 384), "oy": put_cols(go_o, 384, 128), "ay": put_cols(gq_o, 0, 384), "az": put_az}
    panels = {}
    for name, (width, y_first, at, start) in PANELS.items():
        grad, near = sets[at]
        if SETS[at] != width:
            cols = pl.ds(start, width)
            grad, near = grad.at[:, :, :, :, cols], near.at[:, :, :, cols]
        panels[name] = Panel(y_first, grad, near, *slots[name], puts[name], name in DIRECT)
    wide = Panel(False, TG, TN, TS, None, None, None, t_send, t_recv, None)
    reused = {"gz": 0, "gy": 1}
    steps = {}
    outs = {"gz": (6,), "gy": (6,), "uy": (7,), "uz": (7,), "dy": (8,), "dz": (8,), "t": (8,), "oz": (5,), "oy": (5,),
            "ay": (2, 3, 4), "az": (2, 3, 4)}

    def middle(name, stage):
        panels[name].middle(stage)

    def second(name):
        panel = panels[name]
        panel.end(1)
        if name in reused:
            for step in (1, -1):
                pl.semaphore_signal(credit.at[reused[name]], inc=1, device_id=panel.device(1, step), device_id_type=MESH)
        panel.begin(2)

    def cross(name):
        panels[name].end(2)
        panels[name].cross()

    def finished(name):
        which = outs.pop(name)
        if which not in outs.values():
            give(*which)

    def finish(name):
        panels[name].finish()
        finished(name)

    def reuse(name):
        panels[name].sent(6)
        pl.semaphore_wait(credit.at[reused[name]], 2)

    along_y = ((peers[0], ring(y, 1), ring(y, -1)), (peers[1], ring(y, -1), ring(y, 1)), (peers[4], ring(y, 2), ring(y, 2)))

    def part_cols(at):
        return pl.ds(pl.multiple_of(at * WIDE, WIDE), WIDE)

    def wide_copy(kind, slot, HID=None):
        device, to, _ = along_y[slot]
        if kind == 0:
            src, dst = HS.at[slot] if HID is None else HID.at[:, part_cols(to)], HS.at[slot]
        else:
            src, dst = TT.at[to], TF.at[slot]
        sem = 6 + 3 * kind + slot
        return pltpu.make_async_remote_copy(
            src_ref=src, dst_ref=dst, send_sem=t_send.at[sem], recv_sem=t_recv.at[sem],
            device_id=device, device_id_type=MESH)

    def wide_crossing():
        return pltpu.make_async_remote_copy(
            src_ref=TS.at[:, wide.other], dst_ref=TX, send_sem=t_send.at[12], recv_sem=t_recv.at[12],
            device_id=wide.across, device_id_type=MESH)

    def wide_cross():
        wide.end(1)
        wide_crossing().start()

    def wide_spread():
        wide_crossing().wait_recv()

        @pl.loop(0, 4)
        def _(q):
            TT[q] = (TS[q, xh].astype(F32) + TX[q].astype(F32)).astype(BF)

        gd_o[:, part_cols(y)] = TS[y, xh].astype(F32) + TX[y].astype(F32)
        for slot in range(3):
            wide_copy(1, slot).start()

    def wide_finish():
        for slot in range(3):
            wide_copy(1, slot).wait_recv()
            gd_o[:, part_cols(along_y[slot][2])] = TF[slot].astype(F32)
        finished("t")

    stages = ((peers[0], peers[1], peers[4]), (peers[2], peers[3], peers[5]), (peers[6],), (p.to_core, p.to_next, p.to_far))

    def add_gain(row, gain):
        for i in range(4):
            GA[0, 0, row + i:row + i + 1] += gain[:, 512 * i:512 * i + 512]

    def gain_copy(stage, i):
        sem = 3 * stage + i
        return pltpu.make_async_remote_copy(
            src_ref=GA.at[stage, 0], dst_ref=GA.at[stage, i + 1], send_sem=gs.at[sem], recv_sem=gr.at[sem],
            device_id=stages[stage][i], device_id_type=MESH)

    def gain_send(stage):
        for i in range(len(stages[stage])):
            gain_copy(stage, i).start()

    def gain_sum(stage):
        total = GA[stage, 0]
        for i in range(len(stages[stage])):
            gain_copy(stage, i).wait_recv()
            total = total + GA[stage, i + 1]
        return total

    def gain_next(stage):
        GA[stage + 1, 0] = gain_sum(stage)
        gain_send(stage + 1)

    scatter2 = Scatter(p, X0, Ra0, Ra1, Ra2, s2s, s2r, 2)
    scatter_out = Scatter(p, X3, Rb0, Rb1, Rb2, sls, slr, 2)
    scatter1 = Scatter(p, X0, Ra0, Ra1, Ra2, s1s, s1r, 2)
    gather = Gather(p, DX2F, g4s, g4r, 2)

    def need(*loads):
        for one in loads:
            if id(one) not in waited:
                waited[id(one)] = one
                one.wait()

    def twice(run):
        return lambda: [run(i) for i in range(2)]

    for name in panels:
        steps["mid." + name] = functools.partial(middle, name, 1)
        steps["sec." + name] = functools.partial(second, name)
        steps["mid2." + name] = functools.partial(middle, name, 2)
        steps["cro." + name] = functools.partial(cross, name)
        steps["fin." + name] = functools.partial(finish, name)
    steps["mid.t"], steps["cro.t"], steps["spr.t"], steps["fin.t"] = functools.partial(wide.middle, 1), wide_cross, wide_spread, wide_finish
    for i in range(2):
        steps["s2c%d" % i] = functools.partial(scatter2.combine, i)
        steps["loc%d" % i] = functools.partial(scatter_out.combine, i)
        steps["s1c%d" % i] = functools.partial(scatter1.combine, i)
    for i in range(3):
        steps["gn%d" % i] = functools.partial(gain_next, i)

    def sender(scatter):
        def run():
            twice(scatter.cross)()
            twice(scatter.own)()
        return run

    steps["s2send"], steps["losend"], steps["s1send"] = sender(scatter2), sender(scatter_out), sender(scatter1)

    def layer_total():
        for i in range(2):
            rows = scatter_out.rowsof(i)
            lo_o[rows] = lo_o[rows] + scatter_out.total(i)
        give(0)

    def gain_last():
        GO[...] = pltpu.roll(gain_sum(3), lax.rem(512 - lax.rem(p.dp * 64 + tp * 16, 512), 512), 1)[:, :128]
        for i in range(2):
            gains_o[i:i + 1] = GO[pl.ds(4 * i + y, 1), :16]

    steps["lot"], steps["gfin"] = layer_total, gain_last

    def early(DY, HID, DG, DU, WG, WU, WD, ST, wsem):
        l_dy, l_hid, l_a2, l_du = load(dy_h, DY), load(hid_h, HID), load(a2_h, X1), load(du_h, DU)

        def around_chunk(i):
            return [pltpu.make_async_copy(around_h.at[:, :, pl.ds(256 * i, 256)], ST.at[i % 2], wsem.at[6 + i % 2])]

        def gate_chunk(i):
            at = pl.ds(256 * i, 256)
            return [pltpu.make_async_copy(wg_h.at[at], WG.at[i % 2], wsem.at[i % 2]),
                    pltpu.make_async_copy(wu_h.at[at], WU.at[i % 2], wsem.at[2 + i % 2])]

        def down_chunk(i):
            return [pltpu.make_async_copy(wd_h.at[:, pl.ds(256 * i, 256)], WD.at[i % 2], wsem.at[4 + i % 2])]

        def stream(chunk, use):
            for i in chunks_of[chunk]:
                for copy in chunk(i):
                    copy.wait()
                use(i)
                if i < 6:
                    for copy in chunk(i + 2):
                        copy.start()

        GA[0, 0] = jnp.zeros((8, 512), F32)
        pl.semaphore_wait(barrier, len(peers))
        for slot in range(3):
            wide_copy(0, slot, hid_h).start()
        l_dg = load(dg_h, DG)
        for i in range(2):
            for copy in gate_chunk(i):
                copy.start()
        l_x2 = load(x2_h, lo_o)
        for i in range(2):
            for copy in down_chunk(i) + around_chunk(i):
                copy.start()
        a2 = X1.reshape(512, 2048)

        def grads(name, left, right, width, start, *loads):
            def run():
                need(*loads)
                panel = panels[name]
                if panel.y_first:
                    grad_begin(panel, left, right, width, start)
                else:
                    grad_panel(panel.grad, left, right, width, start)
                    panel.begin(1)
            steps[name] = run

        grads("gz", a2, DG, 768, 640, l_a2, l_dg)
        grads("gy", a2, DG, 640, 0, l_a2, l_dg)
        grads("uy", a2, DU, 768, 0, l_a2, l_du)
        grads("uz", a2, DU, 640, 768, l_a2, l_du)
        grads("dy", DY, HID, 256, 1024, l_dy, l_hid)
        grads("dz", DY, HID, 128, 1280, l_dy, l_hid)

        def normed(i):
            da = dot_nt(DG[...], WG[i % 2]) + dot_nt(DU[...], WU[i % 2])
            X0[:, :, pl.ds(256 * i, 256)] = da.astype(BF).reshape(4, 128, 256)

        def part_of_out(i):
            X3[:, :, pl.ds(256 * i, 256)] = dot(HID[...], WD[i % 2]).astype(BF).reshape(4, 128, 256)

        def from_four(i):
            total = dot_tn(DY[:, pl.ds(256 * i, 256)], HID[:, part_cols(y)])
            for slot in range(3):
                total += dot_tn(ST[i % 2, slot], HS[slot])
            TG[i // 2, i % 2] = total.astype(BF).reshape(4, 64, WIDE)

        def half(chunk, use, which, *loads):
            def run():
                need(*loads)
                chunks_of[chunk] = range(4 * which, 4 * which + 4)
                stream(chunk, use)
            return run

        for which in range(2):
            steps["da2" + "ab"[which]] = half(gate_chunk, normed, which, l_dg, l_du)
            steps["lo" + "ab"[which]] = half(down_chunk, part_of_out, which, l_hid)

        def four():
            need(l_dy, l_hid)
            for slot in range(3):
                wide_copy(0, slot).wait_recv()
            chunks_of[around_chunk] = range(8)
            stream(around_chunk, from_four)
            wide.begin(1)

        def middle_rows(i):
            need(l_x2)
            rows = scatter2.rowsof(i)
            back, gain = norm_back(scatter2.total(i), lo_o[rows], gain2[...])
            add_gain(4, gain)
            dx2 = DY[pl.ds(pl.multiple_of(tp * 128 + i * 64, 64), 64)].astype(F32) + back
            gt_o[rows] = dx2
            DX2F[p.me, rows] = dx2.astype(BF)
            gather.start(i)

        steps["gt"] = four
        for i in range(2):
            steps["rows%d" % i] = functools.partial(middle_rows, i)
        for name in EARLY:
            steps[name]()
        need(l_dy, l_hid, l_a2, l_du, l_dg, l_x2)
        for slot in range(3):
            wide_copy(0, slot, hid_h).wait_send()

    def late(X, A1, Wo, Wq, Wkv, Q, O, DO, DQ, K, V, DKV, LSE, COS, SIN, B0, B1, DK, DV):
        l_wo, l_o, l_q, l_k, l_v, l_lse, l_cos, l_sin, l_a1, l_wq, l_wk, l_wv, l_x = late_loads = [load(*w) for w in (
            (wo_h, Wo), (o_h, O), (q_h, Q), (k_h, K), (v_h, V), (lse_h, LSE), (cos_h, COS), (sin_h, SIN),
            (a1_h, A1), (wq_h, Wq), (wk_h, Wkv.at[pl.ds(0, 64)]), (wv_h, Wkv.at[pl.ds(64, 64)]), (x_h, X))]
        ones = cnt[0] + cnt[1] + cnt[2] + cnt[3]
        first = 512 - ones[0:1, 0:1]
        for bias, block in zip((B0, B1), BLOCKS):
            mask_bias(bias, first, *block)

        def back_out(chip):
            need(l_wo)
            rows = pl.ds(pl.multiple_of(chip * 256, 256), 256)
            DO[rows] = dot_nt(chip_rows(DX2F, chip), Wo[...]).astype(BF)

        def forward_first():
            gather.near()
            gather.forward(0)

        def back_rest():
            twice(gather.rest)()
            back_out(1 - p.chip)

        steps["fwd0"], steps["fwd1"] = forward_first, functools.partial(gather.forward, 1)
        steps["do1"], steps["do2"] = functools.partial(back_out, p.chip), back_rest
        zero = jnp.zeros((512, 128), BF)
        left = lanes((512, 128)) < 64

        def heads(j):
            cols = pl.ds(128 * j, 128)
            for bias, (start, rows, keys) in zip((B0, B1), BLOCKS):
                at = pl.ds(start, rows)
                qs = split_heads(Q[at, cols])
                dos = split_heads(DO[at, cols])
                s = dot_nt(qs, K[:keys]) * 0.125
                s = (s.reshape(2, rows, keys) + bias[...][None]).reshape(2 * rows, keys)
                lse = jnp.concatenate([LSE[at, 2 * j:2 * j + 1], LSE[at, 2 * j + 1:2 * j + 2]], axis=0)
                prob = jnp.exp(s - lse)
                dp = dot_nt(dos, V[:keys])
                row_dot = jnp.sum(prob * dp, axis=1, keepdims=True)
                ds = (prob * (dp - row_dot) * 0.125).astype(BF)
                dv = dot_tn(prob.astype(BF), dos)
                dk = dot_tn(ds, qs)
                if j == 0 and keys == 512:
                    DV[256:] = dv[256:]
                    DK[256:] = dk[256:]
                    DV[:256] += dv[:256]
                    DK[:256] += dk[:256]
                elif j == 0:
                    DV[:keys] = dv
                    DK[:keys] = dk
                else:
                    DV[:keys] += dv
                    DK[:keys] += dk
                kl = jnp.where(left[:keys], K[:keys], zero[:keys])
                kr = jnp.where(left[:keys], zero[:keys], K[:keys])
                dq = dot(ds[:rows], kl) + dot(ds[rows:], kr)
                DQ[at, cols] = (dq * COS[at] - turned(dq) * SIN[at]).astype(BF)

        def head_step(j):
            need(l_q, l_k, l_v, l_lse, l_cos, l_sin)
            heads(j)
            if j == 3:
                dk = DK[...] + pltpu.roll(DK[...], 64, 1)
                dv = DV[...] + pltpu.roll(DV[...], 64, 1)
                DKV[...] = jnp.where(left, dk * COS[...] - turned(dk) * SIN[...], dv).astype(BF)

        for j in range(4):
            steps["h%d" % j] = functools.partial(head_step, j)

        def normed(which):
            need(l_wq, l_wk, l_wv)
            if not which:
                scatter2.drain()
            for i in range(2 * which, 2 * which + 2):
                at = pl.ds(512 * i, 512)
                da = dot_nt(DQ[...], Wq[at]) + dot(DKV[...], Wkv[:, at])
                X0[:, :, at] = da.astype(BF).reshape(4, 128, 512)

        steps["da1"], steps["da1b"] = functools.partial(normed, 0), functools.partial(normed, 1)

        def reuse_once(name):
            if name in reused:
                reuse(name)
                del reused[name]

        def out_z():
            need(l_o)
            reuse_once("gz")
            grad_panel(panels["oz"].grad, DX2F.reshape(512, 2048), O, 384, 0)
            panels["oz"].begin(1)

        def out_y():
            need(l_o)
            reuse_once("gy")
            grad_begin(panels["oy"], DX2F.reshape(512, 2048), O, 128, 384)

        def attn_y():
            need(l_a1)
            reuse_once("gy")
            grad_begin(panels["ay"], A1, DQ, 384, 0)

        def attn_z():
            need(l_a1)
            reuse_once("gz")
            grad_z = panels["az"].grad
            grad_panel(grad_z.at[:, :, :, :, pl.ds(0, 128)], A1, DQ, 128, 384)
            grad_panel(grad_z.at[:, :, :, :, pl.ds(128, 128)], A1, DKV, 128, 0)
            panels["az"].begin(1)

        steps["oz"], steps["oy"], steps["ay"], steps["az"] = out_z, out_y, attn_y, attn_z

        def first_rows(i):
            need(l_x)
            rows = scatter1.rowsof(i)
            back, gain = norm_back(scatter1.total(i), X[rows].astype(F32), gain1[...])
            add_gain(0, gain)
            gt_o[rows] = gt_o[rows] + back
            if i:
                give(1)
                gain_send(0)

        for i in range(2):
            steps["r%d" % i] = functools.partial(first_rows, i)
        for name in LATE:
            steps[name]()
        need(*late_loads)

    vm, dma = pltpu.VMEM, pltpu.SemaphoreType.DMA
    pl.run_scoped(early, vm((512, 2048), BF), vm((512, 1408), BF), vm((512, 1408), BF), vm((512, 1408), BF),
                  vm((2, 256, 1408), BF), vm((2, 256, 1408), BF), vm((2, 1408, 256), BF), vm((2, 3, 512, 256), BF), dma((8,)))
    pl.run_scoped(late, vm((128, 2048), BF), vm((512, 2048), BF), vm((512, 2048), BF), vm((2048, 512), BF),
                  vm((128, 2048), BF), vm((512, 512), BF), vm((512, 512), BF), vm((512, 512), BF), vm((512, 512), BF),
                  vm((512, 128), BF), vm((512, 128), BF), vm((512, 128), BF), vm((512, 128), F32),
                  vm((512, 128), F32), vm((512, 128), F32), vm((256, 256), F32), vm((256, 512), F32),
                  vm((512, 128), F32), vm((512, 128), F32))
    for i in range(9):
        pltpu.make_async_copy((lo_o, gt_o, gq_o, gk_o, gv_o, go_o, gg_o, gu_o, gd_o)[i], results[i], osem.at[i]).wait()
    for stage in range(4):
        for i in range(len(stages[stage])):
            gain_copy(stage, i).wait_send()
    for panel in panels.values():
        panel.drain()
    wide.sent(6)
    wide_crossing().wait_send()
    for slot in range(3):
        wide_copy(1, slot).wait_send()
    for what in (scatter_out, scatter1, gather):
        what.drain()


def backward(kept, tokens, norm_attn, norm_mlp, w_query, w_key, w_value, w_out, w_down, w_gate, w_up):
    (a1, a2, dy, hidden, d_gate, d_up, q, k, v, o, lse, x2, cos, sin, cnt, around) = kept
    vm, dma = pltpu.VMEM, pltpu.SemaphoreType.DMA
    shapes = ((128, 2048), (128, 2048), (64, 512), (64, 64), (64, 64), (64, 512), (64, 1408), (64, 1408), (64, 1408),
              (2, 16))
    scratch = [vm(shape, F32) for shape in shapes[:9]] + [dma((9,))]
    for w in SETS.values():
        scratch += [vm((4, 2, 4, 64, w), BF), vm((6, 4, 64, w), BF)]
    for name, (w, *_) in PANELS.items():
        far = (3, 2, 64, w) if name in DIRECT else (6, 64, w)
        scratch += [vm((4, 2, 64, w), BF), vm(far, BF), vm((2, 64, w), BF), vm((64, w), BF), dma((13,)), dma((13,))]
    scratch += [vm((4, 2, 4, 64, WIDE), BF), vm((6, 4, 64, WIDE), BF), vm((4, 2, 64, WIDE), BF), vm((4, 64, WIDE), BF),
                vm((4, 64, WIDE), BF), vm((3, 64, WIDE), BF), vm((3, 512, WIDE), BF), dma((13,)), dma((13,))]
    scratch += [vm((4, 128, 2048), BF)] * 4 + [vm((128, 2048), BF)] * 6
    scratch += [vm((4, 4, 8, 512), F32), vm((8, 128), F32)]
    scratch += [dma((23,))] + [dma((6,))] * 8 + [dma((12,))] * 2 + [pltpu.SemaphoreType.REGULAR((2,))]
    return pl.pallas_call(
        backward_kernel,
        name="backward",
        out_shape=[jax.ShapeDtypeStruct(shape, F32) for shape in shapes],
        in_specs=[pl.BlockSpec(memory_space=pltpu.VMEM)] * 3 + [pl.BlockSpec(memory_space=pl.ANY)] * 23,
        out_specs=[pl.BlockSpec(memory_space=pl.ANY)] * 9 + [pl.BlockSpec(memory_space=pltpu.VMEM)],
        scratch_shapes=scratch,
        compiler_params=pltpu.CompilerParams(
            collective_id=3, has_side_effects=True, vmem_limit_bytes=63 * 2**20
        ),
    )(norm_attn.reshape(1, 2048), norm_mlp.reshape(1, 2048), cnt,
      a1.reshape(512, 2048), a2, dy.reshape(512, 2048), hidden, d_gate, d_up, q, k, v, o, lse, x2, cos, sin,
      around.reshape(3, 512, 2048), tokens, w_query, w_key.T, w_value.T, w_out, w_down, w_gate, w_up)


def deliver_kernel(*refs):
    ins, outs, held, (one, two), sems = refs[:10], refs[10:21], refs[21:31], refs[31:33], refs[33:]
    come = [pltpu.make_async_copy(i, h, sems[0].at[n]) for n, (i, h) in enumerate(zip(ins, held))]
    leave = [pltpu.make_async_copy(h, o, sems[1].at[n]) for n, (h, o) in enumerate(zip(held[:9] + (one, two), outs))]
    for copy in come:
        copy.start()
    for before, after in zip(come[:9], leave):
        before.wait()
        after.start()
    come[9].wait()
    one[...] = held[9][0:1]
    two[...] = held[9][1:2]
    for copy in leave[9:]:
        copy.start()
    for copy in leave:
        copy.wait()


def deliver(parts):
    shapes = [jax.ShapeDtypeStruct(a.shape, F32) for a in parts[:9]] + [jax.ShapeDtypeStruct((1, 16), F32)] * 2
    return pl.pallas_call(
        deliver_kernel,
        name="deliver",
        out_shape=shapes,
        in_specs=[pl.BlockSpec(memory_space=pl.ANY)] * 10,
        out_specs=[pl.BlockSpec(memory_space=pl.ANY)] * 11,
        scratch_shapes=[pltpu.VMEM(a.shape, F32) for a in parts] + [pltpu.VMEM((1, 16), F32)] * 2
        + [pltpu.SemaphoreType.DMA((10,)), pltpu.SemaphoreType.DMA((11,))],
    )(*parts)


def per_device(
    tokens,
    norm_attn,
    w_query,
    w_key,
    w_value,
    w_out,
    norm_mlp,
    w_gate,
    w_up,
    w_down,
    segment_ids,
    cotangent,
):
    weights = (w_query, w_key, w_value, w_out, w_down, w_gate, w_up)
    kept = forward(tokens, norm_attn, norm_mlp, segment_ids, cotangent, *weights)
    (layer_out, grad_tokens, g_query, g_key, g_value, g_out, g_gate, g_up, g_down, gain1, gain2) = deliver(backward(
        kept, tokens, norm_attn, norm_mlp, *weights))
    return (layer_out, grad_tokens, gain1.reshape(16), g_query, g_key, g_value, g_out.T, gain2.reshape(16), g_gate, g_up,
            g_down.T)


def solution(mesh):
    placed = (
        P(("dp", "tp"), None),
        P(),
        P(None, "tp"),
        P(None, "tp"),
        P(None, "tp"),
        P("tp", None),
        P(),
        P(None, "tp"),
        P(None, "tp"),
        P("tp", None),
        P(("dp", "tp")),
        P(("dp", "tp"), None),
    )
    return jax.shard_map(
        per_device,
        mesh=mesh,
        in_specs=placed,
        out_specs=(
            P(("dp", "tp"), None),
            P(("dp", "tp"), None),
            P(("dp", "tp")),
            P("dp", "tp"),
            P("dp", "tp"),
            P("dp", "tp"),
            P("tp", "dp"),
            P(("dp", "tp")),
            P("dp", "tp"),
            P("dp", "tp"),
            P("tp", "dp"),
        ),
        check_vma=False,
    )
```

```python
import functools
import math

import jax
import jax.numpy as jnp
import numpy as np
from jax import lax
from jax.experimental import pallas as pl
from jax.experimental.pallas import tpu as pltpu
from jax.sharding import PartitionSpec as P

HD = 64
BF = jnp.bfloat16
F32 = jnp.float32
MESH = pl.DeviceIdType.MESH


def place():
    dp = lax.axis_index("dp")
    tp = lax.axis_index("tp")
    return dp // 8, lax.rem(dp // 4, 2), lax.rem(dp, 4), tp


def ring(me, step):
    return lax.rem(me + step + 4, 4)


class Panel:
    def __init__(self, y_first, grad, near, second, far, last, from_x, send, recv, put, direct=False):
        self.y_first = y_first
        self.grad, self.near, self.second, self.far = grad, near, second, far
        self.last, self.from_x = last, from_x
        self.send, self.recv = send, recv
        self.put = put
        self.direct = direct
        y, xh, z, tp = place()
        self.xh = xh
        one, two = (y, z) if y_first else (z, y)
        steps = lambda me: (me, ring(me, 1), ring(me, 2), ring(me, -1))
        self.at = (None, steps(one), steps(two))
        self.devices = {}
        for step in (1, -1, 2):
            along_y = (ring(y, step) * 8 + xh * 4 + z, tp)
            along_z = (y * 8 + xh * 4 + ring(z, step), tp)
            self.devices[1, step], self.devices[2, step] = (along_y, along_z) if y_first else (along_z, along_y)
        self.other = 1 - xh
        self.across = (y * 8 + self.other * 4 + z, tp)
        self.started = []

    def device(self, stage, step):
        return self.devices[stage, step]

    def part(self, stage, at, half):
        if half is None:
            return self.second.at[at]
        if stage == 1:
            return self.grad.at[at, half] if self.y_first else self.grad.at[:, half, at]
        return self.second.at[at, half]

    def landed(self, stage, k):
        return (self.near if stage == 1 else self.far).at[k]

    def copy(self, stage, k, at, half, step):
        sem = k + (6 if stage == 2 else 0)
        return pltpu.make_async_remote_copy(
            src_ref=self.part(stage, at, half),
            dst_ref=self.landed(stage, k),
            send_sem=self.send.at[sem],
            recv_sem=self.recv.at[sem],
            device_id=self.device(stage, step),
            device_id_type=MESH,
        )

    def go(self, stage, k, at, half, step):
        what = (stage, k, at, half, step)
        self.copy(*what).start()
        self.started.append(what)

    def arrived(self, stage, k):
        half = None if stage == 2 and self.direct else 0
        self.copy(stage, k, self.at[stage][0], half, 1).wait_recv()

    def begin(self, stage):
        me, right, over, left = self.at[stage]
        if stage == 2 and self.direct:
            for k, (at, step) in enumerate(((right, 1), (left, -1), (over, 2))):
                self.go(2, k, at, None, step)
            return
        self.go(stage, 0, over, 0, 1)
        self.go(stage, 1, over, 1, -1)
        self.go(stage, 2, right, 1, 1)
        self.go(stage, 3, left, 0, -1)

    def add(self, into, what):
        if len(into.shape) == 3:
            @pl.loop(0, into.shape[0])
            def _(i):
                into[i] = (into[i].astype(F32) + what[i].astype(F32)).astype(BF)
        else:
            into[...] = (into[...].astype(F32) + what[...].astype(F32)).astype(BF)

    def middle(self, stage):
        me, right, over, left = self.at[stage]
        for k, at, half, step in ((0, right, 0, 1), (1, left, 1, -1)):
            self.arrived(stage, k)
            self.add(self.part(stage, at, half), self.landed(stage, k))
            self.go(stage, k + 4, at, half, step)

    def end(self, stage):
        me = self.at[stage][0]
        if stage == 2 and self.direct:
            for k in range(3):
                self.arrived(2, k)
            total = self.second[me].astype(F32)
            for k in range(3):
                total += self.far[k].astype(F32)
            self.last[...] = total.astype(BF)
            return
        for half, (a, b) in enumerate(((4, 3), (2, 5))):
            self.arrived(stage, a)
            self.arrived(stage, b)
            own, one, two = self.part(stage, me, half), self.landed(stage, a), self.landed(stage, b)
            if stage == 1:
                @pl.loop(0, 4)
                def _(q):
                    total = own[q].astype(F32) + one[q].astype(F32) + two[q].astype(F32)
                    self.second[q, half] = total.astype(BF)
            else:
                total = own[...].astype(F32) + one[...].astype(F32) + two[...].astype(F32)
                self.last[half] = total.astype(BF)

    def crossing(self):
        return pltpu.make_async_remote_copy(
            src_ref=self.last.at[self.other],
            dst_ref=self.from_x,
            send_sem=self.send.at[12],
            recv_sem=self.recv.at[12],
            device_id=self.across,
            device_id_type=MESH,
        )

    def cross(self):
        self.crossing().start()

    def finish(self):
        self.crossing().wait_recv()
        self.put(self.last[self.xh].astype(F32) + self.from_x[...].astype(F32))

    def sent(self, count):
        for what in self.started[:count]:
            self.copy(*what).wait_send()
        self.started = self.started[count:]

    def drain(self):
        self.sent(len(self.started))
        self.crossing().wait_send()


def dot(a, b):
    return jnp.dot(a, b, preferred_element_type=F32)


def dot_nt(a, b):
    return lax.dot_general(a, b, (((1,), (1,)), ((), ())), preferred_element_type=F32)


def dot_tn(a, b):
    return lax.dot_general(a, b, (((0,), (0,)), ((), ())), preferred_element_type=F32)


class Peers:
    def __init__(self):
        self.dp = lax.axis_index("dp")
        self.me = lax.axis_index("tp")
        self.core = self.me + 1 - 2 * lax.rem(self.me, 2)
        self.next = lax.rem(self.me + 2, 4)
        self.far = lax.rem(self.core + 2, 4)
        self.chip = self.me // 2
        self.to_core = (self.dp, self.core)
        self.to_next = (self.dp, self.next)
        self.to_far = (self.dp, self.far)


class Gather:
    def __init__(self, peers, buf, send, recv, parts):
        self.p, self.buf, self.send, self.recv, self.parts = peers, buf, send, recv, parts
        self.rows = buf.shape[1] // parts
        self.started = []

    def copy(self, kind, owner, i, device):
        at = self.buf.at[owner, pl.ds(i * self.rows, self.rows)]
        sem = kind * self.parts + i
        return pltpu.make_async_remote_copy(
            src_ref=at, dst_ref=at, send_sem=self.send.at[sem], recv_sem=self.recv.at[sem],
            device_id=device, device_id_type=MESH)

    def go(self, *what):
        self.copy(*what).start()
        self.started.append(what)

    def start(self, i):
        self.go(1, self.p.me, i, self.p.to_next)
        self.go(0, self.p.me, i, self.p.to_core)

    def near(self):
        for i in range(self.parts):
            self.copy(0, self.p.core, i, self.p.to_core).wait_recv()

    def forward(self, i):
        self.copy(1, self.p.next, i, self.p.to_next).wait_recv()
        self.go(2, self.p.next, i, self.p.to_core)

    def rest(self, i):
        self.copy(2, self.p.far, i, self.p.to_core).wait_recv()

    def drain(self):
        for what in self.started:
            self.copy(*what).wait_send()
        self.started = []


class Scatter:
    def __init__(self, peers, part, r0, r1, r2, send, recv, parts):
        self.p, self.part, self.r = peers, part, (r0, r1, r2)
        self.send, self.recv, self.parts = send, recv, parts
        self.rows = part.shape[1] // parts
        self.started = []

    def rowsof(self, i):
        return pl.ds(i * self.rows, self.rows)

    def copy(self, kind, owner, i, device):
        sem = kind * self.parts + i
        return pltpu.make_async_remote_copy(
            src_ref=self.part.at[owner, self.rowsof(i)], dst_ref=self.r[kind].at[self.rowsof(i)],
            send_sem=self.send.at[sem], recv_sem=self.recv.at[sem],
            device_id=device, device_id_type=MESH)

    def go(self, *what):
        self.copy(*what).start()
        self.started.append(what)

    def cross(self, i):
        self.go(0, self.p.far, i, self.p.to_core)

    def own(self, i):
        self.go(1, self.p.core, i, self.p.to_core)

    def combine(self, i):
        self.copy(0, self.p.far, i, self.p.to_core).wait_recv()
        at = self.part.at[self.p.next, self.rowsof(i)]
        at[...] = (at[...].astype(F32) + self.r[0][self.rowsof(i)].astype(F32)).astype(BF)
        self.go(2, self.p.next, i, self.p.to_next)

    def total(self, i):
        self.copy(1, self.p.core, i, self.p.to_core).wait_recv()
        self.copy(2, self.p.next, i, self.p.to_next).wait_recv()
        rows = self.rowsof(i)
        return (self.part[self.p.me, rows].astype(F32) + self.r[1][rows].astype(F32)
                + self.r[2][rows].astype(F32))

    def drain(self):
        for what in self.started:
            self.copy(*what).wait_send()
        self.started = []


class Around:
    def __init__(self, peers, buf, out, send, recv):
        self.p, self.buf, self.out, self.send, self.recv = peers, buf, out, send, recv
        y, xh, z, tp = place()
        self.to = [(ring(y, step) * 8 + xh * 4 + z, tp) for step in (1, -1, 2)]
        self.owners = (peers.me, peers.next)
        self.given = (peers.core, peers.far)
        self.started = []

    def copy(self, kind, which, slot):
        sem = 6 * kind + 3 * which + slot
        owner = self.owners[which] if kind < 2 else self.given[which]
        at = self.out.at[slot, owner]
        sem = sem if kind < 2 else sem - 6
        return pltpu.make_async_remote_copy(
            src_ref=self.buf.at[owner] if kind == 0 else at, dst_ref=at,
            send_sem=self.send.at[sem], recv_sem=self.recv.at[sem],
            device_id=self.p.to_core if kind else self.to[slot], device_id_type=MESH)

    def go(self, *what):
        self.copy(*what).start()
        self.started.append(what)

    def spread(self, which):
        for slot in range(3):
            self.go(0, which, slot)

    def hand(self, which, slot):
        self.copy(0, which, slot).wait_recv()
        self.go(1, which, slot)

    def rest(self, which):
        for slot in range(3):
            self.copy(2, which, slot).wait_recv()

    def drain(self):
        for what in self.started:
            self.copy(*what).wait_send()


def rope_tables():
    inverse = np.exp(np.arange(32, dtype=np.float64) * (-2.0 * math.log(10000.0) / 64))
    angles = np.arange(512, dtype=np.float64)[:, None] * np.tile(inverse, 4)[None, :]
    return (np.cos(angles).astype(np.float32), np.sin(angles).astype(np.float32),
            np.tile(inverse, 4)[None, :].astype(np.float32))


def lanes(shape):
    return lax.broadcasted_iota(jnp.int32, shape, len(shape) - 1)


def turned(values):
    low = lax.rem(lanes(values.shape), 64) < 32
    return jnp.where(low, pltpu.roll(values, 96, 1), pltpu.roll(values, 32, 1))


def split_heads(pair):
    left = lanes(pair.shape) < 64
    zero = jnp.zeros_like(pair)
    return jnp.concatenate([jnp.where(left, pair, zero), jnp.where(left, zero, pair)], axis=0)


BLOCKS = ((0, 256, 256), (256, 256, 512))
FF_TILES = ((0, 512), (512, 512), (1024, 384))


def mask_bias(bias, first, start, rows, keys):
    row = lax.broadcasted_iota(jnp.int32, (rows, keys), 0) + start
    key = lax.broadcasted_iota(jnp.int32, (rows, keys), 1)
    allowed = (key <= row) & ((row < first) == (key < first))
    bias[...] = jnp.where(allowed, 0.0, -1e9).astype(F32)


def inverse_rms(rows):
    return lax.rsqrt(jnp.mean(rows * rows, axis=1, keepdims=True) + 1e-5)


def chip_rows(buf, chip):
    return buf[pl.ds(chip * 2, 2)].reshape(256, buf.shape[2])


def forward_kernel(gain1, gain2, inv, seg, x_h, cos_h, sin_h, dy_h, *refs):
    hbm_w, refs = refs[:7], refs[7:]
    outs, around_o, refs = refs[:15], refs[15], refs[16:]
    (a1_o, a2_o, dy_o, hid_o, dg_o, du_o, q_o, k_o, v_o, o_o, lse_o, x2_o, cos_o, sin_o, cnt_o) = outs
    (A1, A2, DY, Wq, Wkv, Wo, Wd, Wg, Wu, Q, K, V, O, LSE, PM, R0, R1, R2, DH, HID, DG, DU, X2, COS, SIN,
     CNT, B0, B1, wsem, osem, g1s, g1r, g2s, g2r, g3s, g3r, ss, sr, cs, cr, as_, ar, x, cos0, sin0, isem) = refs
    weights = (Wq, Wkv.at[pl.ds(0, 64)], Wkv.at[pl.ds(64, 64)], Wo, Wd, Wg, Wu)
    loads = [pltpu.make_async_copy(h, w, wsem.at[i]) for i, (h, w) in enumerate(zip(hbm_w, weights))]
    p = Peers()
    barrier = pltpu.get_barrier_semaphore()
    around = Around(p, DY, around_o, as_, ar)
    for device in [p.to_core, p.to_next, p.to_far] + around.to:
        pl.semaphore_signal(barrier, inc=1, device_id=device, device_id_type=MESH)
    firsts = [pltpu.make_async_copy(h, v, isem.at[i]) for i, (h, v) in enumerate(
        ((x_h, x), (dy_h, DY.at[p.me]), (cos_h, cos0), (sin_h, sin0)))]
    for load in firsts + loads:
        load.start()
    stored = []

    def keep(src, dst):
        copy = pltpu.make_async_copy(src, dst, osem.at[len(stored)])
        copy.start()
        stored.append(copy)

    firsts[0].wait()
    stream = x[...].astype(F32)
    A1[p.me] = (stream * inverse_rms(stream) * gain1[...]).astype(BF)
    firsts[1].wait()
    CNT[p.me] = jnp.broadcast_to(jnp.sum(seg[...], axis=1, keepdims=True), (8, 128))
    pl.semaphore_wait(barrier, 6)
    first_in = Gather(p, A1, g1s, g1r, 2)
    for i in range(2):
        first_in.start(i)
    counts = [pltpu.make_async_remote_copy(
        src_ref=CNT.at[p.me], dst_ref=CNT.at[p.me], send_sem=cs.at[i], recv_sem=cr.at[i],
        device_id=device, device_id_type=MESH) for i, device in enumerate((p.to_core, p.to_next, p.to_far))]
    for copy in counts:
        copy.start()
    dy_in = Gather(p, DY, g2s, g2r, 2)
    for i in range(2):
        dy_in.start(i)
    around.spread(0)
    for i, owner in enumerate((p.core, p.next, p.far)):
        pltpu.make_async_remote_copy(
            src_ref=CNT.at[owner], dst_ref=CNT.at[owner], send_sem=cs.at[i], recv_sem=cr.at[i],
            device_id=p.to_core, device_id_type=MESH).wait_recv()
    ones = CNT[0] + CNT[1] + CNT[2] + CNT[3]
    first = 512 - ones[0:1, 0:1]
    firsts[2].wait()
    firsts[3].wait()
    angle = first.astype(F32) * inv[...]
    cos_n, sin_n = jnp.cos(angle), jnp.sin(angle)
    row = lax.broadcasted_iota(jnp.int32, (512, 128), 0)
    c0, s0 = cos0[...], sin0[...]
    COS[...] = jnp.where(row < first, c0, c0 * cos_n + s0 * sin_n)
    sine = jnp.where(row < first, s0, s0 * cos_n - c0 * sin_n)
    SIN[...] = jnp.where(lax.rem(lanes((512, 128)), 64) < 32, -sine, sine)
    for bias, block in zip((B0, B1), BLOCKS):
        mask_bias(bias, first, *block)
    keep(COS, cos_o)
    keep(SIN, sin_o)
    keep(CNT, cnt_o)

    def project(chip):
        rows = pl.ds(pl.multiple_of(chip * 256, 256), 256)
        a = chip_rows(A1, chip)
        cos, sin = COS[rows], SIN[rows]
        for j in range(2):
            q = dot(a, Wq[:, pl.ds(256 * j, 256)])
            for h in range(2):
                pair = q[:, 128 * h:128 * h + 128]
                Q[rows, pl.ds(256 * j + 128 * h, 128)] = (pair * cos + turned(pair) * sin).astype(BF)
        kv = dot_nt(a, Wkv[...])
        vk = pltpu.roll(kv, 64, 1)
        k_lane = lanes(kv.shape) < 64
        kk = jnp.where(k_lane, kv, vk)
        K[rows] = (kk * cos + turned(kk) * sin).astype(BF)
        V[rows] = jnp.where(k_lane, vk, kv).astype(BF)

    for load in loads[:3]:
        load.wait()
    first_in.near()
    project(p.chip)
    for i in range(2):
        first_in.forward(i)
    for i in range(2):
        first_in.rest(i)
    project(1 - p.chip)
    keep(A1, a1_o)
    keep(Q, q_o)
    keep(K, k_o)
    keep(V, v_o)

    zero = jnp.zeros((512, 128), BF)
    left = lanes((512, 128)) < 64
    def attend(block, pairs):
        bias = (B0, B1)[block]
        start, rows, keys = BLOCKS[block]
        for j in pairs:
            qs = split_heads(Q[pl.ds(start, rows), pl.ds(128 * j, 128)])
            s = dot_nt(qs, K[:keys]) * 0.125
            s = (s.reshape(2, rows, keys) + bias[...][None]).reshape(2 * rows, keys)
            top = jnp.max(s, axis=1, keepdims=True)
            e = jnp.exp(s - top)
            total = jnp.sum(e, axis=1, keepdims=True)
            lse = top + jnp.log(total)
            eb = (e / total).astype(BF)
            vl = jnp.where(left[:keys], V[:keys], zero[:keys])
            vr = jnp.where(left[:keys], zero[:keys], V[:keys])
            o = dot(eb[:rows], vl) + dot(eb[rows:], vr)
            O[pl.ds(start, rows), pl.ds(128 * j, 128)] = o.astype(BF)
            lane = lanes((rows, 128))
            old = LSE[pl.ds(start, rows)] if j else jnp.zeros((rows, 128), F32)
            LSE[pl.ds(start, rows)] = jnp.where(lane == 2 * j, lse[:rows], jnp.where(lane == 2 * j + 1, lse[rows:], old))

    def attend_rows(other, pairs):
        for chip in range(2):
            @pl.when(p.chip == chip)
            def _():
                attend(1 - chip if other else chip, pairs)

    def spread(chip):
        rows = pl.ds(pl.multiple_of(chip * 256, 256), 256)
        for j in range(4):
            cols = pl.ds(512 * j, 512)
            PM[pl.ds(chip * 2, 2), :, cols] = dot(O[rows], Wo[:, cols]).astype(BF).reshape(2, 128, 512)

    scatter = Scatter(p, PM, R0, R1, R2, ss, sr, 2)
    attend_rows(True, range(4))
    loads[3].wait()
    spread(1 - p.chip)
    for i in range(2):
        scatter.cross(i)
    attend_rows(False, range(2))
    for i in range(2):
        scatter.combine(i)
    attend_rows(False, range(2, 4))
    dy_in.near()
    for i in range(2):
        dy_in.forward(i)
    around.spread(1)
    keep(O, o_o)
    keep(LSE, lse_o)
    spread(p.chip)
    for i in range(2):
        scatter.own(i)
    loads[4].wait()
    for i in range(2):
        dy_in.rest(i)
    keep(DY, dy_o)
    for slot in range(3):
        around.hand(0, slot)
    dy = DY[...].reshape(512, 2048)
    for start, width in FF_TILES:
        DH[:, pl.ds(start, width)] = dot_nt(dy, Wd[pl.ds(start, width)])
    second_in = Gather(p, A2, g3s, g3r, 2)
    for i in range(2):
        rows = scatter.rowsof(i)
        x2 = x[rows].astype(F32) + scatter.total(i)
        X2[rows] = x2
        A2[p.me, rows] = (x2 * inverse_rms(x2) * gain2[...]).astype(BF)
        second_in.start(i)
    keep(X2, x2_o)

    def mlp(chip, start, count):
        a = A2[pl.ds(chip * 2, 2), pl.ds(start, count)].reshape(2 * count, 2048)
        rows = [pl.ds(pl.multiple_of(chip * 256 + 128 * i + start, 64), count) for i in range(2)]
        for first_col, width in FF_TILES:
            cols = pl.ds(first_col, width)
            g = dot(a, Wg[:, cols])
            u = dot(a, Wu[:, cols])
            dh = jnp.concatenate([DH[r, cols] for r in rows], axis=0)
            sg = jax.nn.sigmoid(g)
            act = g * sg
            values = ((HID, act * u), (DU, dh * act), (DG, dh * u * (sg + act * (1.0 - sg))))
            for ref, value in values:
                for i, r in enumerate(rows):
                    ref[r, cols] = value[i * count:(i + 1) * count].astype(BF)

    def keep_rows(chip):
        rows = pl.ds(pl.multiple_of(chip * 256, 256), 256)
        for ref, out in ((HID, hid_o), (DG, dg_o), (DU, du_o)):
            keep(ref.at[rows], out.at[rows])

    loads[5].wait()
    loads[6].wait()
    second_in.near()
    mlp(p.chip, 0, 128)
    keep_rows(p.chip)
    second_in.forward(0)
    for slot in range(2):
        around.hand(1, slot)
    second_in.rest(0)
    mlp(1 - p.chip, 0, 64)
    second_in.forward(1)
    second_in.rest(1)
    keep(A2, a2_o)
    around.hand(1, 2)
    mlp(1 - p.chip, 64, 64)
    keep_rows(1 - p.chip)
    around.rest(0)
    around.rest(1)
    for copy in stored:
        copy.wait()
    for copy in counts:
        copy.wait_send()
    for what in (first_in, dy_in, second_in, scatter, around):
        what.drain()


def forward(tokens, norm_attn, norm_mlp, segment_ids, cotangent, w_query, w_key, w_value, w_out, w_down, w_gate, w_up):
    cos0, sin0, inv = rope_tables()
    rows4 = (4, 128, 2048)
    spec = lambda shape, kind: jax.ShapeDtypeStruct(shape, kind)
    outs = [spec(rows4, BF)] * 3 + [spec((512, 1408), BF)] * 3 + [
        spec((512, 512), BF), spec((512, 128), BF), spec((512, 128), BF), spec((512, 512), BF),
        spec((512, 128), F32), spec((128, 2048), F32), spec((512, 128), F32), spec((512, 128), F32),
        spec((4, 8, 128), jnp.int32), spec((3, 4, 128, 2048), BF)]
    vm = pltpu.VMEM
    dma = pltpu.SemaphoreType.DMA
    scratch = [vm(rows4, BF)] * 3 + [
        vm((2048, 512), BF), vm((128, 2048), BF), vm((512, 2048), BF), vm((1408, 2048), BF),
        vm((2048, 1408), BF), vm((2048, 1408), BF),
        vm((512, 512), BF), vm((512, 128), BF), vm((512, 128), BF), vm((512, 512), BF), vm((512, 128), F32),
        vm(rows4, BF), vm((128, 2048), BF), vm((128, 2048), BF), vm((128, 2048), BF), vm((512, 1408), F32),
        vm((512, 1408), BF), vm((512, 1408), BF), vm((512, 1408), BF), vm((128, 2048), F32),
        vm((512, 128), F32), vm((512, 128), F32), vm((4, 8, 128), jnp.int32), vm((256, 256), F32), vm((256, 512), F32),
        dma((7,)), dma((18,))] + [dma((6,))] * 8 + [dma((3,))] * 2 + [dma((12,))] * 2 + [
        vm((128, 2048), BF), vm((512, 128), F32), vm((512, 128), F32), dma((4,))]
    return pl.pallas_call(
        forward_kernel,
        name="forward",
        out_shape=outs,
        in_specs=[pl.BlockSpec(memory_space=pltpu.VMEM)] * 4 + [pl.BlockSpec(memory_space=pl.ANY)] * 11,
        out_specs=[pl.BlockSpec(memory_space=pl.ANY)] * 16,
        scratch_shapes=scratch,
        compiler_params=pltpu.CompilerParams(
            collective_id=2, has_side_effects=True, vmem_limit_bytes=62 * 2**20
        ),
    )(norm_attn.reshape(1, 2048), norm_mlp.reshape(1, 2048), inv, segment_ids.reshape(1, 128),
      tokens, cos0, sin0, cotangent, w_query, w_key.T, w_value.T, w_out, w_down, w_gate, w_up)


PANELS = {
    "gz": (768, False, "gz", 0), "gy": (640, True, "gy", 0), "dy": (256, True, "dy", 0), "dz": (128, False, "dz", 0),
    "uy": (768, True, "uy", 0), "uz": (640, False, "uz", 0), "oz": (384, False, "gz", 0), "oy": (128, True, "gy", 384),
    "ay": (384, True, "gy", 0), "az": (256, False, "gz", 384),
}
SETS = {"gz": 768, "gy": 640, "dy": 256, "dz": 128, "uy": 768, "uz": 640}
DIRECT = ('ay', 'az')
EARLY = (
    "dz", "uz", "da2a", "gy", "gz", "mid.dz", "da2b", "s2send", "mid.gy", "s2c0", "s2c1", "uy", "mid.gz", "loa",
    "rows0", "sec.gy", "lob", "rows1", "gt", "dy",
)
LATE = (
    "fwd0", "fwd1", "do1", "mid.uz", "losend", "sec.gz", "loc0", "do2", "loc1", "h0", "mid.uy", "oz", "mid.dy",
    "sec.dz", "h1", "h2", "h3", "mid2.gz", "mid2.gy", "az", "mid.t", "oy", "da1", "da1b", "s1send", "lot", "ay",
    "s1c0", "s1c1", "mid.oz", "sec.uy", "mid.oy", "cro.t", "sec.dy", "mid.ay", "sec.uz", "cro.gy", "sec.oz",
    "mid2.uy", "mid2.dz", "r0", "sec.oy", "mid.az", "r1", "mid2.dy", "mid2.uz", "cro.gz", "mid2.oy", "cro.uy",
    "sec.ay", "gn0", "mid2.oz", "sec.az", "cro.oy", "fin.gy", "cro.dz", "cro.dy", "gn1", "cro.uz", "spr.t", "fin.gz",
    "cro.oz", "fin.uy", "cro.ay", "fin.oy", "fin.dy", "gn2", "cro.az", "fin.uz", "gfin", "fin.ay", "fin.oz", "fin.t",
    "fin.dz", "fin.az",
)
WIDE = 256


def grad_panel(grad, left, right, width, start):
    @pl.loop(0, 4)
    def _(at):
        rows = left[:, pl.ds(pl.multiple_of(at * 512, 512), 512)]
        cols = pl.ds(start, width)
        grad[at] = dot_tn(rows, right[:, cols]).astype(BF).reshape(2, 4, 64, width)


def grad_begin(panel, left, right, width, start):
    me, after, over, before = panel.at[1]
    for at, sends in ((over, ((0, over, 0, 1), (1, over, 1, -1))), (after, ((2, after, 1, 1),)),
                      (before, ((3, before, 0, -1),)), (me, ())):
        rows = left[:, pl.ds(pl.multiple_of(at * 512, 512), 512)]
        cols = pl.ds(start, width)
        panel.grad[at] = dot_tn(rows, right[:, cols]).astype(BF).reshape(2, 4, 64, width)
        for what in sends:
            panel.go(1, *what)


def norm_back(dn, rows, gain):
    r = inverse_rms(rows)
    e = dn * gain
    back = r * e - rows * (r * r * r) * jnp.mean(e * rows, axis=1, keepdims=True)
    return back, jnp.sum(dn * rows * r, axis=0, keepdims=True)


def backward_kernel(gain1, gain2, cnt, *refs):
    (a1_h, a2_h, dy_h, hid_h, dg_h, du_h, q_h, k_h, v_h, o_h, lse_h, x2_h, cos_h, sin_h, around_h,
     x_h, wq_h, wk_h, wv_h, wo_h, wd_h, wg_h, wu_h) = refs[:23]
    results, gains_o, refs = refs[23:32], refs[32], refs[33:]
    (lo_o, gt_o, gq_o, gk_o, gv_o, go_o, gg_o, gu_o, gd_o, osem), refs = refs[:10], refs[10:]
    sets, refs = {name: refs[2 * i:2 * i + 2] for i, name in enumerate(SETS)}, refs[2 * len(SETS):]
    slots, refs = {name: refs[6 * i:6 * i + 6] for i, name in enumerate(PANELS)}, refs[6 * len(PANELS):]
    (TG, TN, TS, TX, TT, TF, HS, t_send, t_recv,
     X0, X1, X3, DX2F, Ra0, Ra1, Ra2, Rb0, Rb1, Rb2, GA, GO,
     lsem, s2s, s2r, sls, slr, s1s, s1r, g4s, g4r, gs, gr, credit) = refs
    y, xh, z, tp = place()
    p = Peers()
    peers = [
        (ring(y, 1) * 8 + xh * 4 + z, tp), (ring(y, -1) * 8 + xh * 4 + z, tp),
        (y * 8 + xh * 4 + ring(z, 1), tp), (y * 8 + xh * 4 + ring(z, -1), tp),
        (ring(y, 2) * 8 + xh * 4 + z, tp), (y * 8 + xh * 4 + ring(z, 2), tp),
        (y * 8 + (1 - xh) * 4 + z, tp), p.to_core, p.to_next, p.to_far]
    barrier = pltpu.get_barrier_semaphore()
    for device in peers:
        pl.semaphore_signal(barrier, inc=1, device_id=device, device_id_type=MESH)

    def give(*which):
        for i in which:
            pltpu.make_async_copy((lo_o, gt_o, gq_o, gk_o, gv_o, go_o, gg_o, gu_o, gd_o)[i], results[i], osem.at[i]).start()

    n_loads, waited, chunks_of = [0], {}, {}

    def load(src, dst):
        copy = pltpu.make_async_copy(src, dst, lsem.at[n_loads[0]])
        n_loads[0] += 1
        copy.start()
        return copy

    def put_cols(ref, start, width):
        def put(v):
            ref[:, pl.ds(start, width)] = v
        return put

    def put_az(v):
        gq_o[:, 384:] = v[:, :128]
        gk_o[...] = v[:, 128:192]
        gv_o[...] = v[:, 192:]

    puts = {"gz": put_cols(gg_o, 640, 768), "gy": put_cols(gg_o, 0, 640), "dy": put_cols(gd_o, 1024, 256),
            "dz": put_cols(gd_o, 1280, 128), "uy": put_cols(gu_o, 0, 768), "uz": put_cols(gu_o, 768, 640),
            "oz": put_cols(go_o, 0, 384), "oy": put_cols(go_o, 384, 128), "ay": put_cols(gq_o, 0, 384), "az": put_az}
    panels = {}
    for name, (width, y_first, at, start) in PANELS.items():
        grad, near = sets[at]
        if SETS[at] != width:
            cols = pl.ds(start, width)
            grad, near = grad.at[:, :, :, :, cols], near.at[:, :, :, cols]
        panels[name] = Panel(y_first, grad, near, *slots[name], puts[name], name in DIRECT)
    wide = Panel(False, TG, TN, TS, None, None, None, t_send, t_recv, None)
    reused = {"gz": 0, "gy": 1}
    steps = {}
    outs = {"gz": (6,), "gy": (6,), "uy": (7,), "uz": (7,), "dy": (8,), "dz": (8,), "t": (8,), "oz": (5,), "oy": (5,),
            "ay": (2, 3, 4), "az": (2, 3, 4)}

    def middle(name, stage):
        panels[name].middle(stage)

    def second(name):
        panel = panels[name]
        panel.end(1)
        if name in reused:
            for step in (1, -1):
                pl.semaphore_signal(credit.at[reused[name]], inc=1, device_id=panel.device(1, step), device_id_type=MESH)
        panel.begin(2)

    def cross(name):
        panels[name].end(2)
        panels[name].cross()

    def finished(name):
        which = outs.pop(name)
        if which not in outs.values():
            give(*which)

    def finish(name):
        panels[name].finish()
        finished(name)

    def reuse(name):
        panels[name].sent(6)
        pl.semaphore_wait(credit.at[reused[name]], 2)

    along_y = ((peers[0], ring(y, 1), ring(y, -1)), (peers[1], ring(y, -1), ring(y, 1)), (peers[4], ring(y, 2), ring(y, 2)))

    def part_cols(at):
        return pl.ds(pl.multiple_of(at * WIDE, WIDE), WIDE)

    def wide_copy(kind, slot, HID=None):
        device, to, _ = along_y[slot]
        if kind == 0:
            src, dst = HS.at[slot] if HID is None else HID.at[:, part_cols(to)], HS.at[slot]
        else:
            src, dst = TT.at[to], TF.at[slot]
        sem = 6 + 3 * kind + slot
        return pltpu.make_async_remote_copy(
            src_ref=src, dst_ref=dst, send_sem=t_send.at[sem], recv_sem=t_recv.at[sem],
            device_id=device, device_id_type=MESH)

    def wide_crossing():
        return pltpu.make_async_remote_copy(
            src_ref=TS.at[:, wide.other], dst_ref=TX, send_sem=t_send.at[12], recv_sem=t_recv.at[12],
            device_id=wide.across, device_id_type=MESH)

    def wide_cross():
        wide.end(1)
        wide_crossing().start()

    def wide_spread():
        wide_crossing().wait_recv()

        @pl.loop(0, 4)
        def _(q):
            TT[q] = (TS[q, xh].astype(F32) + TX[q].astype(F32)).astype(BF)

        gd_o[:, part_cols(y)] = TS[y, xh].astype(F32) + TX[y].astype(F32)
        for slot in range(3):
            wide_copy(1, slot).start()

    def wide_finish():
        for slot in range(3):
            wide_copy(1, slot).wait_recv()
            gd_o[:, part_cols(along_y[slot][2])] = TF[slot].astype(F32)
        finished("t")

    stages = ((peers[0], peers[1], peers[4]), (peers[2], peers[3], peers[5]), (peers[6],), (p.to_core, p.to_next, p.to_far))

    def add_gain(row, gain):
        for i in range(4):
            GA[0, 0, row + i:row + i + 1] += gain[:, 512 * i:512 * i + 512]

    def gain_copy(stage, i):
        sem = 3 * stage + i
        return pltpu.make_async_remote_copy(
            src_ref=GA.at[stage, 0], dst_ref=GA.at[stage, i + 1], send_sem=gs.at[sem], recv_sem=gr.at[sem],
            device_id=stages[stage][i], device_id_type=MESH)

    def gain_send(stage):
        for i in range(len(stages[stage])):
            gain_copy(stage, i).start()

    def gain_sum(stage):
        total = GA[stage, 0]
        for i in range(len(stages[stage])):
            gain_copy(stage, i).wait_recv()
            total = total + GA[stage, i + 1]
        return total

    def gain_next(stage):
        GA[stage + 1, 0] = gain_sum(stage)
        gain_send(stage + 1)

    scatter2 = Scatter(p, X0, Ra0, Ra1, Ra2, s2s, s2r, 2)
    scatter_out = Scatter(p, X3, Rb0, Rb1, Rb2, sls, slr, 2)
    scatter1 = Scatter(p, X0, Ra0, Ra1, Ra2, s1s, s1r, 2)
    gather = Gather(p, DX2F, g4s, g4r, 2)

    def need(*loads):
        for one in loads:
            if id(one) not in waited:
                waited[id(one)] = one
                one.wait()

    def twice(run):
        return lambda: [run(i) for i in range(2)]

    for name in panels:
        steps["mid." + name] = functools.partial(middle, name, 1)
        steps["sec." + name] = functools.partial(second, name)
        steps["mid2." + name] = functools.partial(middle, name, 2)
        steps["cro." + name] = functools.partial(cross, name)
        steps["fin." + name] = functools.partial(finish, name)
    steps["mid.t"], steps["cro.t"], steps["spr.t"], steps["fin.t"] = functools.partial(wide.middle, 1), wide_cross, wide_spread, wide_finish
    for i in range(2):
        steps["s2c%d" % i] = functools.partial(scatter2.combine, i)
        steps["loc%d" % i] = functools.partial(scatter_out.combine, i)
        steps["s1c%d" % i] = functools.partial(scatter1.combine, i)
    for i in range(3):
        steps["gn%d" % i] = functools.partial(gain_next, i)

    def sender(scatter):
        def run():
            twice(scatter.cross)()
            twice(scatter.own)()
        return run

    steps["s2send"], steps["losend"], steps["s1send"] = sender(scatter2), sender(scatter_out), sender(scatter1)

    def layer_total():
        for i in range(2):
            rows = scatter_out.rowsof(i)
            lo_o[rows] = lo_o[rows] + scatter_out.total(i)
        give(0)

    def gain_last():
        GO[...] = pltpu.roll(gain_sum(3), lax.rem(512 - lax.rem(p.dp * 64 + tp * 16, 512), 512), 1)[:, :128]
        for i in range(2):
            gains_o[i:i + 1] = GO[pl.ds(4 * i + y, 1), :16]

    steps["lot"], steps["gfin"] = layer_total, gain_last

    def early(DY, HID, DG, DU, WG, WU, WD, ST, wsem):
        l_dy, l_hid, l_a2, l_du = load(dy_h, DY), load(hid_h, HID), load(a2_h, X1), load(du_h, DU)

        def around_chunk(i):
            return [pltpu.make_async_copy(around_h.at[:, :, pl.ds(256 * i, 256)], ST.at[i % 2], wsem.at[6 + i % 2])]

        def gate_chunk(i):
            at = pl.ds(256 * i, 256)
            return [pltpu.make_async_copy(wg_h.at[at], WG.at[i % 2], wsem.at[i % 2]),
                    pltpu.make_async_copy(wu_h.at[at], WU.at[i % 2], wsem.at[2 + i % 2])]

        def down_chunk(i):
            return [pltpu.make_async_copy(wd_h.at[:, pl.ds(256 * i, 256)], WD.at[i % 2], wsem.at[4 + i % 2])]

        def stream(chunk, use):
            for i in chunks_of[chunk]:
                for copy in chunk(i):
                    copy.wait()
                use(i)
                if i < 6:
                    for copy in chunk(i + 2):
                        copy.start()

        GA[0, 0] = jnp.zeros((8, 512), F32)
        pl.semaphore_wait(barrier, len(peers))
        for slot in range(3):
            wide_copy(0, slot, hid_h).start()
        l_dg = load(dg_h, DG)
        for i in range(2):
            for copy in gate_chunk(i):
                copy.start()
        l_x2 = load(x2_h, lo_o)
        for i in range(2):
            for copy in down_chunk(i) + around_chunk(i):
                copy.start()
        a2 = X1.reshape(512, 2048)

        def grads(name, left, right, width, start, *loads):
            def run():
                need(*loads)
                panel = panels[name]
                if panel.y_first:
                    grad_begin(panel, left, right, width, start)
                else:
                    grad_panel(panel.grad, left, right, width, start)
                    panel.begin(1)
            steps[name] = run

        grads("gz", a2, DG, 768, 640, l_a2, l_dg)
        grads("gy", a2, DG, 640, 0, l_a2, l_dg)
        grads("uy", a2, DU, 768, 0, l_a2, l_du)
        grads("uz", a2, DU, 640, 768, l_a2, l_du)
        grads("dy", DY, HID, 256, 1024, l_dy, l_hid)
        grads("dz", DY, HID, 128, 1280, l_dy, l_hid)

        def normed(i):
            da = dot_nt(DG[...], WG[i % 2]) + dot_nt(DU[...], WU[i % 2])
            X0[:, :, pl.ds(256 * i, 256)] = da.astype(BF).reshape(4, 128, 256)

        def part_of_out(i):
            X3[:, :, pl.ds(256 * i, 256)] = dot(HID[...], WD[i % 2]).astype(BF).reshape(4, 128, 256)

        def from_four(i):
            total = dot_tn(DY[:, pl.ds(256 * i, 256)], HID[:, part_cols(y)])
            for slot in range(3):
                total += dot_tn(ST[i % 2, slot], HS[slot])
            TG[i // 2, i % 2] = total.astype(BF).reshape(4, 64, WIDE)

        def half(chunk, use, which, *loads):
            def run():
                need(*loads)
                chunks_of[chunk] = range(4 * which, 4 * which + 4)
                stream(chunk, use)
            return run

        for which in range(2):
            steps["da2" + "ab"[which]] = half(gate_chunk, normed, which, l_dg, l_du)
            steps["lo" + "ab"[which]] = half(down_chunk, part_of_out, which, l_hid)

        def four():
            need(l_dy, l_hid)
            for slot in range(3):
                wide_copy(0, slot).wait_recv()
            chunks_of[around_chunk] = range(8)
            stream(around_chunk, from_four)
            wide.begin(1)

        def middle_rows(i):
            need(l_x2)
            rows = scatter2.rowsof(i)
            back, gain = norm_back(scatter2.total(i), lo_o[rows], gain2[...])
            add_gain(4, gain)
            dx2 = DY[pl.ds(pl.multiple_of(tp * 128 + i * 64, 64), 64)].astype(F32) + back
            gt_o[rows] = dx2
            DX2F[p.me, rows] = dx2.astype(BF)
            gather.start(i)

        steps["gt"] = four
        for i in range(2):
            steps["rows%d" % i] = functools.partial(middle_rows, i)
        for name in EARLY:
            steps[name]()
        need(l_dy, l_hid, l_a2, l_du, l_dg, l_x2)
        for slot in range(3):
            wide_copy(0, slot, hid_h).wait_send()

    def late(X, A1, Wo, Wq, Wkv, Q, O, DO, DQ, K, V, DKV, LSE, COS, SIN, B0, B1, DK, DV):
        l_wo, l_o, l_q, l_k, l_v, l_lse, l_cos, l_sin, l_a1, l_wq, l_wk, l_wv, l_x = late_loads = [load(*w) for w in (
            (wo_h, Wo), (o_h, O), (q_h, Q), (k_h, K), (v_h, V), (lse_h, LSE), (cos_h, COS), (sin_h, SIN),
            (a1_h, A1), (wq_h, Wq), (wk_h, Wkv.at[pl.ds(0, 64)]), (wv_h, Wkv.at[pl.ds(64, 64)]), (x_h, X))]
        ones = cnt[0] + cnt[1] + cnt[2] + cnt[3]
        first = 512 - ones[0:1, 0:1]
        for bias, block in zip((B0, B1), BLOCKS):
            mask_bias(bias, first, *block)

        def back_out(chip):
            need(l_wo)
            rows = pl.ds(pl.multiple_of(chip * 256, 256), 256)
            DO[rows] = dot_nt(chip_rows(DX2F, chip), Wo[...]).astype(BF)

        def forward_first():
            gather.near()
            gather.forward(0)

        def back_rest():
            twice(gather.rest)()
            back_out(1 - p.chip)

        steps["fwd0"], steps["fwd1"] = forward_first, functools.partial(gather.forward, 1)
        steps["do1"], steps["do2"] = functools.partial(back_out, p.chip), back_rest
        zero = jnp.zeros((512, 128), BF)
        left = lanes((512, 128)) < 64

        def heads(j):
            cols = pl.ds(128 * j, 128)
            for bias, (start, rows, keys) in zip((B0, B1), BLOCKS):
                at = pl.ds(start, rows)
                qs = split_heads(Q[at, cols])
                dos = split_heads(DO[at, cols])
                s = dot_nt(qs, K[:keys]) * 0.125
                s = (s.reshape(2, rows, keys) + bias[...][None]).reshape(2 * rows, keys)
                lse = jnp.concatenate([LSE[at, 2 * j:2 * j + 1], LSE[at, 2 * j + 1:2 * j + 2]], axis=0)
                prob = jnp.exp(s - lse)
                dp = dot_nt(dos, V[:keys])
                row_dot = jnp.sum(prob * dp, axis=1, keepdims=True)
                ds = (prob * (dp - row_dot) * 0.125).astype(BF)
                dv = dot_tn(prob.astype(BF), dos)
                dk = dot_tn(ds, qs)
                if j == 0 and keys == 512:
                    DV[256:] = dv[256:]
                    DK[256:] = dk[256:]
                    DV[:256] += dv[:256]
                    DK[:256] += dk[:256]
                elif j == 0:
                    DV[:keys] = dv
                    DK[:keys] = dk
                else:
                    DV[:keys] += dv
                    DK[:keys] += dk
                kl = jnp.where(left[:keys], K[:keys], zero[:keys])
                kr = jnp.where(left[:keys], zero[:keys], K[:keys])
                dq = dot(ds[:rows], kl) + dot(ds[rows:], kr)
                DQ[at, cols] = (dq * COS[at] - turned(dq) * SIN[at]).astype(BF)

        def head_step(j):
            need(l_q, l_k, l_v, l_lse, l_cos, l_sin)
            heads(j)
            if j == 3:
                dk = DK[...] + pltpu.roll(DK[...], 64, 1)
                dv = DV[...] + pltpu.roll(DV[...], 64, 1)
                DKV[...] = jnp.where(left, dk * COS[...] - turned(dk) * SIN[...], dv).astype(BF)

        for j in range(4):
            steps["h%d" % j] = functools.partial(head_step, j)

        def normed(which):
            need(l_wq, l_wk, l_wv)
            if not which:
                scatter2.drain()
            for i in range(2 * which, 2 * which + 2):
                at = pl.ds(512 * i, 512)
                da = dot_nt(DQ[...], Wq[at]) + dot(DKV[...], Wkv[:, at])
                X0[:, :, at] = da.astype(BF).reshape(4, 128, 512)

        steps["da1"], steps["da1b"] = functools.partial(normed, 0), functools.partial(normed, 1)

        def reuse_once(name):
            if name in reused:
                reuse(name)
                del reused[name]

        def out_z():
            need(l_o)
            reuse_once("gz")
            grad_panel(panels["oz"].grad, DX2F.reshape(512, 2048), O, 384, 0)
            panels["oz"].begin(1)

        def out_y():
            need(l_o)
            reuse_once("gy")
            grad_begin(panels["oy"], DX2F.reshape(512, 2048), O, 128, 384)

        def attn_y():
            need(l_a1)
            reuse_once("gy")
            grad_begin(panels["ay"], A1, DQ, 384, 0)

        def attn_z():
            need(l_a1)
            reuse_once("gz")
            grad_z = panels["az"].grad
            grad_panel(grad_z.at[:, :, :, :, pl.ds(0, 128)], A1, DQ, 128, 384)
            grad_panel(grad_z.at[:, :, :, :, pl.ds(128, 128)], A1, DKV, 128, 0)
            panels["az"].begin(1)

        steps["oz"], steps["oy"], steps["ay"], steps["az"] = out_z, out_y, attn_y, attn_z

        def first_rows(i):
            need(l_x)
            rows = scatter1.rowsof(i)
            back, gain = norm_back(scatter1.total(i), X[rows].astype(F32), gain1[...])
            add_gain(0, gain)
            gt_o[rows] = gt_o[rows] + back
            if i:
                give(1)
                gain_send(0)

        for i in range(2):
            steps["r%d" % i] = functools.partial(first_rows, i)
        for name in LATE:
            steps[name]()
        need(*late_loads)

    vm, dma = pltpu.VMEM, pltpu.SemaphoreType.DMA
    pl.run_scoped(early, vm((512, 2048), BF), vm((512, 1408), BF), vm((512, 1408), BF), vm((512, 1408), BF),
                  vm((2, 256, 1408), BF), vm((2, 256, 1408), BF), vm((2, 1408, 256), BF), vm((2, 3, 512, 256), BF), dma((8,)))
    pl.run_scoped(late, vm((128, 2048), BF), vm((512, 2048), BF), vm((512, 2048), BF), vm((2048, 512), BF),
                  vm((128, 2048), BF), vm((512, 512), BF), vm((512, 512), BF), vm((512, 512), BF), vm((512, 512), BF),
                  vm((512, 128), BF), vm((512, 128), BF), vm((512, 128), BF), vm((512, 128), F32),
                  vm((512, 128), F32), vm((512, 128), F32), vm((256, 256), F32), vm((256, 512), F32),
                  vm((512, 128), F32), vm((512, 128), F32))
    for i in range(9):
        pltpu.make_async_copy((lo_o, gt_o, gq_o, gk_o, gv_o, go_o, gg_o, gu_o, gd_o)[i], results[i], osem.at[i]).wait()
    for stage in range(4):
        for i in range(len(stages[stage])):
            gain_copy(stage, i).wait_send()
    for panel in panels.values():
        panel.drain()
    wide.sent(6)
    wide_crossing().wait_send()
    for slot in range(3):
        wide_copy(1, slot).wait_send()
    for what in (scatter_out, scatter1, gather):
        what.drain()


def backward(kept, tokens, norm_attn, norm_mlp, w_query, w_key, w_value, w_out, w_down, w_gate, w_up):
    (a1, a2, dy, hidden, d_gate, d_up, q, k, v, o, lse, x2, cos, sin, cnt, around) = kept
    vm, dma = pltpu.VMEM, pltpu.SemaphoreType.DMA
    shapes = ((128, 2048), (128, 2048), (64, 512), (64, 64), (64, 64), (64, 512), (64, 1408), (64, 1408), (64, 1408),
              (2, 16))
    scratch = [vm(shape, F32) for shape in shapes[:9]] + [dma((9,))]
    for w in SETS.values():
        scratch += [vm((4, 2, 4, 64, w), BF), vm((6, 4, 64, w), BF)]
    for name, (w, *_) in PANELS.items():
        far = (3, 2, 64, w) if name in DIRECT else (6, 64, w)
        scratch += [vm((4, 2, 64, w), BF), vm(far, BF), vm((2, 64, w), BF), vm((64, w), BF), dma((13,)), dma((13,))]
    scratch += [vm((4, 2, 4, 64, WIDE), BF), vm((6, 4, 64, WIDE), BF), vm((4, 2, 64, WIDE), BF), vm((4, 64, WIDE), BF),
                vm((4, 64, WIDE), BF), vm((3, 64, WIDE), BF), vm((3, 512, WIDE), BF), dma((13,)), dma((13,))]
    scratch += [vm((4, 128, 2048), BF)] * 4 + [vm((128, 2048), BF)] * 6
    scratch += [vm((4, 4, 8, 512), F32), vm((8, 128), F32)]
    scratch += [dma((23,))] + [dma((6,))] * 8 + [dma((12,))] * 2 + [pltpu.SemaphoreType.REGULAR((2,))]
    return pl.pallas_call(
        backward_kernel,
        name="backward",
        out_shape=[jax.ShapeDtypeStruct(shape, F32) for shape in shapes],
        in_specs=[pl.BlockSpec(memory_space=pltpu.VMEM)] * 3 + [pl.BlockSpec(memory_space=pl.ANY)] * 23,
        out_specs=[pl.BlockSpec(memory_space=pl.ANY)] * 9 + [pl.BlockSpec(memory_space=pltpu.VMEM)],
        scratch_shapes=scratch,
        compiler_params=pltpu.CompilerParams(
            collective_id=3, has_side_effects=True, vmem_limit_bytes=63 * 2**20
        ),
    )(norm_attn.reshape(1, 2048), norm_mlp.reshape(1, 2048), cnt,
      a1.reshape(512, 2048), a2, dy.reshape(512, 2048), hidden, d_gate, d_up, q, k, v, o, lse, x2, cos, sin,
      around.reshape(3, 512, 2048), tokens, w_query, w_key.T, w_value.T, w_out, w_down, w_gate, w_up)


def deliver_kernel(*refs):
    ins, outs, held, (one, two), sems = refs[:10], refs[10:21], refs[21:31], refs[31:33], refs[33:]
    come = [pltpu.make_async_copy(i, h, sems[0].at[n]) for n, (i, h) in enumerate(zip(ins, held))]
    leave = [pltpu.make_async_copy(h, o, sems[1].at[n]) for n, (h, o) in enumerate(zip(held[:9] + (one, two), outs))]
    for copy in come:
        copy.start()
    for before, after in zip(come[:9], leave):
        before.wait()
        after.start()
    come[9].wait()
    one[...] = held[9][0:1]
    two[...] = held[9][1:2]
    for copy in leave[9:]:
        copy.start()
    for copy in leave:
        copy.wait()


def deliver(parts):
    shapes = [jax.ShapeDtypeStruct(a.shape, F32) for a in parts[:9]] + [jax.ShapeDtypeStruct((1, 16), F32)] * 2
    return pl.pallas_call(
        deliver_kernel,
        name="deliver",
        out_shape=shapes,
        in_specs=[pl.BlockSpec(memory_space=pl.ANY)] * 10,
        out_specs=[pl.BlockSpec(memory_space=pl.ANY)] * 11,
        scratch_shapes=[pltpu.VMEM(a.shape, F32) for a in parts] + [pltpu.VMEM((1, 16), F32)] * 2
        + [pltpu.SemaphoreType.DMA((10,)), pltpu.SemaphoreType.DMA((11,))],
    )(*parts)


def per_device(
    tokens,
    norm_attn,
    w_query,
    w_key,
    w_value,
    w_out,
    norm_mlp,
    w_gate,
    w_up,
    w_down,
    segment_ids,
    cotangent,
):
    weights = (w_query, w_key, w_value, w_out, w_down, w_gate, w_up)
    kept = forward(tokens, norm_attn, norm_mlp, segment_ids, cotangent, *weights)
    (layer_out, grad_tokens, g_query, g_key, g_value, g_out, g_gate, g_up, g_down, gain1, gain2) = deliver(backward(
        kept, tokens, norm_attn, norm_mlp, *weights))
    return (layer_out, grad_tokens, gain1.reshape(16), g_query, g_key, g_value, g_out.T, gain2.reshape(16), g_gate, g_up,
            g_down.T)


def solution(mesh):
    placed = (
        P(("dp", "tp"), None),
        P(),
        P(None, "tp"),
        P(None, "tp"),
        P(None, "tp"),
        P("tp", None),
        P(),
        P(None, "tp"),
        P(None, "tp"),
        P("tp", None),
        P(("dp", "tp")),
        P(("dp", "tp"), None),
    )
    return jax.shard_map(
        per_device,
        mesh=mesh,
        in_specs=placed,
        out_specs=(
            P(("dp", "tp"), None),
            P(("dp", "tp"), None),
            P(("dp", "tp")),
            P("dp", "tp"),
            P("dp", "tp"),
            P("dp", "tp"),
            P("tp", "dp"),
            P(("dp", "tp")),
            P("dp", "tp"),
            P("dp", "tp"),
            P("tp", "dp"),
        ),
        check_vma=False,
    )
```
